32 devices in a mesh: segment: 4 (over z), expert: 8 (over y, x, core).
Axes of the slice: x: 2, y: 2, z: 4, core: 2. Of those that a mesh axis runs over, the one named last changes fastest.
Arguments:
- inputs: bfloat16 [4, 2, 1024, 2048], P('segment', None, 'expert'), may hold values from -6 to 6
- entering: bfloat16 [4, 1024, 2048], P('segment', 'expert'), may hold values from -6 to 6
- weight_in: bfloat16 [4, 8, 704, 2048], P('segment', 'expert'), may hold values from -0.125 to 0.125
- weight_out: bfloat16 [4, 8, 704, 2048], P('segment', 'expert'), may hold values from -0.21875 to 0.21875
- gate_probs: bfloat16 [4, 2, 1024, 2], P('segment', None, 'expert'), may hold values from 0.049804688 to 1
- expert_ids: int32 [4, 2, 1024, 2], P('segment', None, 'expert'), may hold values from 0 to 7, as said below
Outputs:
- grad_in: bfloat16 [4, 8, 704, 2048], P('segment', 'expert')
- grad_out: bfloat16 [4, 8, 704, 2048], P('segment', 'expert')
- prob_grads: bfloat16 [4, 2, 1024, 2], P('segment', None, 'expert')
The draws below stay inside these ranges and needn't reach their ends.
Inputs may be any that keep to these rules, and one draw needn't show every extreme that they name: `expert_ids`: each token names 2 different experts. In each aligned block of 128 tokens of one section and tick no expert is named by more than 48 tokens, and in every section and tick one expert, the same for all blocks of that section and tick, is named by exactly 48 tokens of every block.
All inputs are finite; a program needn't handle non-finite values.
Results may differ from the reference program's by a relative error of at most 0.0085.
Values may be sent and summed in bfloat16 or wider, within the bound.
No kernel may reach another device: no remote copies, remote signals or barrier semaphores. Data moves between devices by JAX's collectives and lax.ppermute only.
A program may use at most 128 MiB of HBM per device.

```python
import math
import jax
import jax.numpy as jnp
from jax import lax

D = 2048
FF = 704
TOPK = 2
TICKS = 2
TOK_DEV = 128
SEGMENTS = 4
EXPERTS = 8
TOKENS = 1024
CAP = 48


def draw_expert_ids(key, part):
    blocks = TOKENS // TOK_DEV
    candidates = EXPERTS * CAP
    hot_expert = jax.random.randint(jax.random.fold_in(key, 7), (SEGMENTS, TICKS), 0, EXPERTS)
    hot_expert = jnp.broadcast_to(hot_expert[:, :, None], (SEGMENTS, TICKS, blocks)).reshape(-1)
    block_count = SEGMENTS * TICKS * blocks
    block_keys = jax.random.split(jax.random.fold_in(key, 11), block_count)

    def one_block(block_key, hot_one):
        key_bias, key_score, key_rows = jax.random.split(block_key, 3)
        positions = jnp.arange(candidates, dtype=jnp.int32)
        owner = positions // CAP
        owner_bias = jax.random.randint(key_bias, (EXPERTS,), 0, 4)
        score = jax.random.randint(key_score, (candidates,), 0, 1 << 16)
        score = (score + owner_bias[owner] * (1 << 16)) * candidates + positions
        score = jnp.where(owner == hot_one, -1 - positions, score)
        ranking = jnp.argsort(score)
        chosen = jnp.sort(owner[ranking[:TOK_DEV * TOPK]])
        row_pairs = chosen.reshape(TOPK, TOK_DEV).T
        return row_pairs[jax.random.permutation(key_rows, TOK_DEV)]
    drawn = jax.vmap(one_block)(block_keys, hot_expert)
    return drawn.reshape(SEGMENTS, TICKS, TOKENS, TOPK).astype(jnp.int32)


def level_of(own_key, extent, cuts, low, high):
    def one(axis_at, parts):
        draws = jax.random.uniform(jax.random.fold_in(jax.random.fold_in(own_key, 6), axis_at), (parts,), jnp.float32, low / len(cuts), high / len(cuts))
        return jnp.repeat(jnp.exp(draws), extent[axis_at] // parts).reshape((-1,) + (1,) * (len(extent) - axis_at - 1))

    factor_of = one(*cuts[0])
    for cut in cuts[1:]:
        factor_of = factor_of * one(*cut)
    return factor_of


def scatter_about(key, extent, scale, limit, cuts=(), held_as=jnp.bfloat16):
    gain = level_of(key, extent, cuts, -0.22, 0.18) if cuts else 1.0
    result = jax.random.normal(key, extent, jnp.float32) * scale * gain
    return jnp.minimum(jnp.maximum(result, -limit), limit).astype(held_as)


def setup_inputs(seed: int = 0) -> dict:
    splits = jax.random.split(jax.random.key(seed), 7)
    return {
        "inputs": scatter_about(splits[0], (SEGMENTS, TICKS, TOKENS, D), 1.0, 6.0, ((0, 4), (2, 8))),
        "entering": scatter_about(splits[1], (SEGMENTS, TOKENS, D), 1.0, 6.0, ((0, 4), (1, 8))),
        "weight_in": scatter_about(splits[2], (SEGMENTS, EXPERTS, FF, D), D ** -0.5, 0.125, ((0, 4), (1, 8))),
        "weight_out": scatter_about(splits[3], (SEGMENTS, EXPERTS, FF, D), FF ** -0.5, 0.21875, ((0, 4), (1, 8))),
        "gate_probs": jnp.clip(jnp.exp(math.log(1.0) - 2.9996462 * jax.random.uniform(splits[4], (SEGMENTS, TICKS, TOKENS, TOPK), jnp.float32) ** level_of(splits[4], (SEGMENTS, TICKS, TOKENS, TOPK), ((0, 4), (2, 8)), -0.2, 0.2)), 0.049804688, 1.0).astype(jnp.bfloat16),
        "expert_ids": draw_expert_ids(jax.random.fold_in(splits[6], 71), 0),
    }


half_root = 0.7071067811865476
density_scale = 0.3989422804014327


def gelu_parts(preact):
    normal_cdf = 0.5 * (1.0 + jax.scipy.special.erf(preact * half_root))
    normal_pdf = density_scale * jnp.exp(-0.5 * preact * preact)
    return preact * normal_cdf, normal_cdf + preact * normal_pdf


def segment_tick(rows_in, incoming, w_in, w_out, probs, chosen):
    sources = TOKENS // TOK_DEV
    per_source = chosen.reshape(sources, TOK_DEV * TOPK).astype(jnp.int32)
    matches = (per_source[:, :, None] == jnp.arange(EXPERTS, dtype=jnp.int32)[None, None, :]).astype(jnp.int32)
    before = jnp.cumsum(matches, axis=1) - matches
    rank_in = jnp.sum(before * matches, axis=2).astype(jnp.int32)
    source_grid = jnp.broadcast_to(jnp.arange(sources, dtype=jnp.int32)[:, None], rank_in.shape)
    token_at = (source_grid * TOK_DEV + jnp.arange(TOK_DEV * TOPK, dtype=jnp.int32)[None, :] // TOPK).reshape(-1)
    source_at = source_grid.reshape(-1)
    expert_at = per_source.reshape(-1)
    slot_at = rank_in.reshape(-1)
    features = rows_in.shape[1]
    slots_x = jnp.zeros((EXPERTS, sources, CAP, features), rows_in.dtype).at[expert_at, source_at, slot_at].set(rows_in[token_at])
    slots_g = jnp.zeros((EXPERTS, sources, CAP, features), incoming.dtype).at[expert_at, source_at, slot_at].set(incoming[token_at])
    slots_p = jnp.zeros((EXPERTS, sources, CAP), probs.dtype).at[expert_at, source_at, slot_at].set(probs.reshape(-1))
    rows_x = slots_x.reshape(EXPERTS, sources * CAP, features).astype(jnp.float32)
    rows_g = slots_g.reshape(EXPERTS, sources * CAP, features).astype(jnp.float32)
    rows_p = slots_p.reshape(EXPERTS, sources * CAP, 1).astype(jnp.float32)
    weights_in = w_in.astype(jnp.float32)
    weights_out = w_out.astype(jnp.float32)
    preact = jnp.einsum("erd,efd->erf", rows_x, weights_in)
    activated, gate_slope = gelu_parts(preact)
    hidden = lax.optimization_barrier(activated.astype(jnp.bfloat16)).astype(jnp.float32)
    pulled = jnp.einsum("erd,efd->erf", rows_g, weights_out)
    scores = jnp.sum(hidden * pulled, axis=2).astype(jnp.bfloat16)
    grad_pre = lax.optimization_barrier((rows_p * pulled * gate_slope).astype(jnp.bfloat16)).astype(jnp.float32)
    grad_y = lax.optimization_barrier((rows_p * rows_g).astype(jnp.bfloat16)).astype(jnp.float32)
    part_out = jnp.einsum("erf,erd->efd", hidden, grad_y)
    part_in = jnp.einsum("erf,erd->efd", grad_pre, rows_x)
    returned = jnp.einsum("erf,efd->erd", grad_pre, weights_in).astype(jnp.bfloat16)
    returned = lax.optimization_barrier(returned).reshape(EXPERTS, sources, CAP, features)
    picked = returned[expert_at, source_at, slot_at].astype(jnp.float32).reshape(TOKENS, TOPK, features)
    leaving = (incoming.astype(jnp.float32) + jnp.sum(picked, axis=1)).astype(jnp.bfloat16)
    prob_part = scores.reshape(EXPERTS, sources, CAP)[expert_at, source_at, slot_at].reshape(TOKENS, TOPK)
    return leaving, part_in, part_out, prob_part


def reference(inputs, entering, weight_in, weight_out, gate_probs, expert_ids):
    def per_segment(from_next, pieces):
        rows_all, entering_one, w_in, w_out, probs_all, chosen_all = pieces
        total_in = jnp.zeros((EXPERTS, FF, D), jnp.float32)
        total_out = jnp.zeros((EXPERTS, FF, D), jnp.float32)
        produced = []
        prob_list = []
        incoming = entering_one
        for moment in range(TICKS):
            if moment > 0:
                incoming = from_next[moment - 1]
            leaving, part_in, part_out, prob_part = segment_tick(rows_all[moment], incoming, w_in, w_out, probs_all[moment], chosen_all[moment])
            total_in = total_in + part_in
            total_out = total_out + part_out
            produced.append(leaving)
            prob_list.append(prob_part)
        carry_out = jnp.stack(produced[:TICKS - 1])
        return carry_out, (total_in.astype(jnp.bfloat16), total_out.astype(jnp.bfloat16), jnp.stack(prob_list))

    start_carry = jnp.zeros((TICKS - 1, TOKENS, D), entering.dtype)
    unused_carry, outputs = lax.scan(per_segment, start_carry, (inputs, entering, weight_in, weight_out, gate_probs, expert_ids), reverse=True)
    return outputs[0], outputs[1], outputs[2]
```

```python
import functools

import jax
import jax.numpy as jnp
from jax import lax
from jax.experimental import pallas as pl
from jax.experimental.pallas import tpu as pltpu
from jax.sharding import PartitionSpec as P

half_root = 0.7071067811865476
density_scale = 0.3989422804014327
TAIL = 128
VMEM_LIMIT = 48 * 1024 * 1024
f32 = jnp.float32
bf16 = jnp.bfloat16


def dot(a, b, ca, cb):
    return lax.dot_general(a, b, (((ca,), (cb,)), ((), ())), preferred_element_type=f32)


def call(kernel, out_shape, *args, flops=0, scratch=()):
    size = sum(a.size * a.dtype.itemsize for a in args)
    size += sum(s.size * s.dtype.itemsize for s in out_shape)
    return pl.pallas_call(
        kernel,
        out_shape=out_shape,
        in_specs=[pl.BlockSpec(memory_space=pltpu.VMEM)] * len(args),
        out_specs=[pl.BlockSpec(memory_space=pltpu.VMEM)] * len(out_shape),
        scratch_shapes=scratch,
        compiler_params=pltpu.CompilerParams(vmem_limit_bytes=VMEM_LIMIT),
        cost_estimate=pl.CostEstimate(flops=flops, bytes_accessed=size, transcendentals=0),
    )(*args)


def shaped(shape, dtype):
    return jax.ShapeDtypeStruct(shape, dtype)


def expander(rows, experts, capacity):
    first = lax.broadcasted_iota(jnp.int32, (rows, experts), 1) * capacity
    row = lax.broadcasted_iota(jnp.int32, (rows, experts), 0)
    return ((row >= first) & (row < first + capacity)).astype(f32).astype(bf16)


def slot_masks(ids, experts, capacity):
    tokens = ids.shape[1]
    rows = experts * capacity
    expert = lax.broadcasted_iota(jnp.int32, (experts, tokens), 0)
    named = [(ids[j : j + 1, :] == expert).astype(f32) for j in range(ids.shape[0])]
    count = sum(named)
    earlier = lax.broadcasted_iota(jnp.int32, (tokens, tokens), 0)
    later = lax.broadcasted_iota(jnp.int32, (tokens, tokens), 1)
    before = (earlier < later).astype(f32).astype(bf16)
    rank = dot(count.astype(bf16), before, 1, 0)
    place = jnp.where(count > 0, rank, -1.0).astype(bf16)
    rep = expander(rows, experts, capacity)
    spread = dot(rep, place, 1, 0)
    row = lax.broadcasted_iota(jnp.int32, (rows, tokens), 0)
    owner = ((row.astype(f32) + 0.5) * (1.0 / capacity)).astype(jnp.int32)
    position = (row - owner * capacity).astype(f32)
    return (spread == position).astype(f32), named, rep


def source_kernel(experts, capacity, ids_ref, prob_ref, x_ref, g_ref, xg_ref, hot0_ref, hot1_ref):
    features = x_ref.shape[1]
    rows = experts * capacity
    lane = lax.broadcasted_iota(jnp.int32, (rows, TAIL), 1)
    tail = jnp.zeros((rows, TAIL), f32)
    for k, hot_ref in enumerate((hot0_ref, hot1_ref)):
        hot, named, rep = slot_masks(ids_ref[k], experts, capacity)
        hot_ref[...] = hot.astype(bf16)
        probs = prob_ref[k].astype(f32)
        by_expert = sum(n * probs[j : j + 1, :] for j, n in enumerate(named)).astype(bf16)
        column = jnp.sum(hot * dot(rep, by_expert, 1, 0), axis=1, keepdims=True)
        tail = jnp.where(lane == k, column, tail)
    xg_ref[:, 2 * features :] = tail.astype(bf16)
    hot = hot0_ref[...]
    xg_ref[:, :features] = dot(hot, x_ref[...], 1, 0).astype(bf16)
    xg_ref[:, features : 2 * features] = dot(hot, g_ref[...], 1, 0).astype(bf16)


def spread_kernel(hot_ref, x_ref, out_ref):
    out_ref[...] = dot(hot_ref[...], x_ref[...], 1, 0).astype(bf16)


def combine_kernel(hot_ref, back_ref, g_ref, out_ref):
    summed = dot(hot_ref[...], back_ref[...], 0, 0)
    out_ref[...] = (g_ref[...].astype(f32) + summed).astype(bf16)


def gelu_parts(preact):
    cdf = 0.5 * (1.0 + lax.erf(preact * half_root))
    pdf = density_scale * jnp.exp(-0.5 * preact * preact)
    return preact * cdf, cdf + preact * pdf


def first_kernel(step, xg_ref, win_ref, wout_ref, hid_ref, gp_ref, ret_ref, score_ref):
    units, features = win_ref.shape
    tail = jnp.transpose(xg_ref[:, 2 * features :].astype(f32))
    prob = tail[0:1, :]
    score = jnp.zeros(prob.shape, f32)
    for f in range(0, units, step):
        at = slice(f, f + step)
        preact = dot(win_ref[at, :], xg_ref[:, :features], 1, 1)
        activated, slope = gelu_parts(preact)
        hidden = activated.astype(bf16)
        pulled = dot(wout_ref[at, :], xg_ref[:, features : 2 * features], 1, 1)
        score = score + jnp.sum(hidden.astype(f32) * pulled, axis=0, keepdims=True)
        hid_ref[at, :] = hidden
        gp_ref[at, :] = (prob * pulled * slope).astype(bf16)
    ret_ref[...] = dot(gp_ref[...], win_ref[...], 0, 0).astype(bf16)
    score_ref[...] = score


def preact_kernel(step, x_ref, win_ref, hid_ref, slope_ref):
    units = win_ref.shape[0]
    for f in range(0, units, step):
        at = slice(f, f + step)
        activated, slope = gelu_parts(dot(win_ref[at, :], x_ref[...], 1, 1))
        hid_ref[at, :] = activated.astype(bf16)
        slope_ref[at, :] = slope


def second_kernel(step, g_ref, xg_ref, wout_ref, hid_ref, slope_ref, score0_ref, gp_ref, score_ref):
    units, features = wout_ref.shape
    tail = jnp.transpose(xg_ref[:, 2 * features :].astype(f32))
    prob = tail[1:2, :]
    score = jnp.zeros(prob.shape, f32)
    for f in range(0, units, step):
        at = slice(f, f + step)
        pulled = dot(wout_ref[at, :], g_ref[...], 1, 1)
        score = score + jnp.sum(hid_ref[at, :].astype(f32) * pulled, axis=0, keepdims=True)
        gp_ref[at, :] = (prob * pulled * slope_ref[at, :]).astype(bf16)
    row = lax.broadcasted_iota(jnp.int32, (TAIL, prob.shape[1]), 0)
    both = jnp.where(row == 0, score0_ref[...], jnp.where(row == 1, score, 0.0))
    score_ref[...] = jnp.transpose(both).astype(bf16)


def grads_kernel(xg_ref, x1_ref, g1_ref, hid0_ref, hid1_ref, gp0_ref, gp1_ref, gin_ref, gout_ref, gy0, gy1):
    features = x1_ref.shape[1]

    @pl.when(pl.program_id(0) == 0)
    def _():
        tail = xg_ref[:, 2 * features :].astype(f32)
        gy0[...] = (tail[:, 0:1] * xg_ref[:, features : 2 * features].astype(f32)).astype(bf16)
        gy1[...] = (tail[:, 1:2] * g1_ref[...].astype(f32)).astype(bf16)

    gin = dot(gp0_ref[...], xg_ref[:, :features], 1, 0) + dot(gp1_ref[...], x1_ref[...], 1, 0)
    gin_ref[...] = gin.astype(bf16)
    gout = dot(hid0_ref[...], gy0[...], 1, 0) + dot(hid1_ref[...], gy1[...], 1, 0)
    gout_ref[...] = gout.astype(bf16)


def grads(step, xg, x1, g1, hid0, hid1, gp0, gp1):
    units, rows = hid0.shape
    features = x1.shape[1]
    whole = lambda a: pl.BlockSpec(a.shape, lambda i: (0, 0))
    part = pl.BlockSpec((step, rows), lambda i: (i, 0))
    out = pl.BlockSpec((step, features), lambda i: (i, 0))
    return pl.pallas_call(
        grads_kernel,
        grid=(units // step,),
        out_shape=[shaped((units, features), bf16)] * 2,
        in_specs=[whole(xg), whole(x1), whole(g1)] + [part] * 4,
        out_specs=[out] * 2,
        scratch_shapes=[pltpu.VMEM((rows, features), bf16)] * 2,
        compiler_params=pltpu.CompilerParams(vmem_limit_bytes=VMEM_LIMIT),
        cost_estimate=pl.CostEstimate(
            flops=8 * units * rows * features, bytes_accessed=8 * units * features, transcendentals=0
        ),
    )(xg, x1, g1, hid0, hid1, gp0, gp1)


def collect_kernel(experts, capacity, ids_ref, hot0_ref, hot1_ref, score_ref, out_ref):
    rows = experts * capacity
    tokens = ids_ref.shape[2]
    rep = expander(rows, experts, capacity)
    expert = lax.broadcasted_iota(jnp.int32, (experts, tokens), 0)
    for k, hot_ref in enumerate((hot0_ref, hot1_ref)):
        placed = hot_ref[...].astype(f32) * score_ref[:, k : k + 1].astype(f32)
        by_expert = dot(rep, placed.astype(bf16), 0, 0)
        ids = ids_ref[k]
        for j in range(ids.shape[0]):
            picked = jnp.where(ids[j : j + 1, :] == expert, by_expert, 0.0)
            out_ref[k, j : j + 1, :] = jnp.sum(picked, axis=0, keepdims=True).astype(bf16)


def exchange(rows, experts):
    width = rows.shape[1]
    pieces = rows.reshape(experts, -1, width)
    arrived = lax.all_to_all(pieces, "expert", split_axis=0, concat_axis=0, tiled=True)
    return arrived.reshape(-1, width)


def step_of(units, wanted):
    return next(s for s in range(wanted, 0, -1) if units % s == 0 and (s % 16 == 0 or s == units))


def body(inputs, entering, weight_in, weight_out, gate_probs, expert_ids):
    experts = lax.axis_size("expert")
    segments = lax.axis_size("segment")
    tokens, features = entering.shape[1:]
    topk = expert_ids.shape[3]
    units = weight_in.shape[2]
    capacity = 3 * tokens * topk // (2 * experts)
    rows = experts * capacity
    step = step_of(units, 352)
    matmul = 2 * rows * units * features
    w_in, w_out = weight_in[0, 0], weight_out[0, 0]
    ids = jnp.transpose(expert_ids[0], (0, 2, 1))
    probs = jnp.transpose(gate_probs[0], (0, 2, 1))
    x0, x1, g0 = inputs[0, 0], inputs[0, 1], entering[0]

    spread = 2 * rows * tokens * features
    xg, hot0, hot1 = call(
        functools.partial(source_kernel, experts, capacity),
        [shaped((rows, 2 * features + TAIL), bf16)] + [shaped((rows, tokens), bf16)] * 2,
        ids, probs, x0, g0, flops=2 * spread,
    )
    xg = exchange(xg, experts)
    (x1,) = call(spread_kernel, [shaped((rows, features), bf16)], hot1, x1, flops=spread)

    hid0, gp0, back, score0 = call(
        functools.partial(first_kernel, step),
        [shaped((units, rows), bf16)] * 2 + [shaped((rows, features), bf16), shaped((1, rows), f32)],
        xg, w_in, w_out, flops=3 * matmul,
    )
    back = exchange(back, experts)
    (leaving,) = call(combine_kernel, [shaped((tokens, features), bf16)], hot0, back, g0, flops=spread)
    g1 = lax.ppermute(leaving, "segment", [(i, i - 1) for i in range(1, segments)])
    x1 = exchange(x1, experts)
    hid1, slope1 = call(
        functools.partial(preact_kernel, step),
        [shaped((units, rows), bf16), shaped((units, rows), f32)], x1, w_in, flops=matmul,
    )
    (g1,) = call(spread_kernel, [shaped((rows, features), bf16)], hot1, g1, flops=spread)
    g1 = exchange(g1, experts)
    gp1, scores = call(
        functools.partial(second_kernel, step),
        [shaped((units, rows), bf16), shaped((rows, TAIL), bf16)],
        g1, xg, w_out, hid1, slope1, score0, flops=matmul,
    )
    scores = exchange(scores, experts)
    grad_in, grad_out = grads(step_of(units, 176), xg, x1, g1, hid0, hid1, gp0, gp1)
    (prob_grads,) = call(
        functools.partial(collect_kernel, experts, capacity), [shaped(ids.shape, bf16)], ids, hot0, hot1, scores
    )
    prob_grads = jnp.transpose(prob_grads, (0, 2, 1))
    return grad_in[None, None], grad_out[None, None], prob_grads[None]


def solution(mesh):
    return jax.shard_map(
        body,
        mesh=mesh,
        in_specs=(
            P("segment", None, "expert", None),
            P("segment", "expert", None),
            P("segment", "expert", None, None),
            P("segment", "expert", None, None),
            P("segment", None, "expert", None),
            P("segment", None, "expert", None),
        ),
        out_specs=(
            P("segment", "expert", None, None),
            P("segment", "expert", None, None),
            P("segment", None, "expert", None),
        ),
        check_vma=False,
    )
```

```python
import functools

import jax
import jax.numpy as jnp
from jax import lax
from jax.experimental import pallas as pl
from jax.experimental.pallas import tpu as pltpu
from jax.sharding import PartitionSpec as P

half_root = 0.7071067811865476
density_scale = 0.3989422804014327
LANES = 128
HALVES = 2
VMEM_LIMIT = 16 * 1024 * 1024
f32 = jnp.float32
bf16 = jnp.bfloat16
VMEM = pl.BlockSpec(memory_space=pltpu.VMEM)


def dot(a, b, ca, cb):
    return lax.dot_general(a, b, (((ca,), (cb,)), ((), ())), preferred_element_type=f32)


def shaped(shape, dtype):
    return jax.ShapeDtypeStruct(shape, dtype)


def cost(args, outs, flops):
    size = sum(a.size * a.dtype.itemsize for a in list(args) + list(outs))
    return pl.CostEstimate(flops=flops, bytes_accessed=size, transcendentals=0)


def call(kernel, outs, *args, flops=0):
    return pl.pallas_call(
        kernel,
        out_shape=outs,
        in_specs=[VMEM] * len(args),
        out_specs=[VMEM] * len(outs),
        compiler_params=pltpu.CompilerParams(vmem_limit_bytes=VMEM_LIMIT),
        cost_estimate=cost(args, outs, flops),
    )(*args)


class Plane:
    def __init__(self, experts):
        chips = experts // 2
        across = next(n for n in range(int(chips**0.5), 0, -1) if chips % n == 0)
        self.size = (chips // across, across, 2)
        self.experts = experts

    def other(self, i, offset):
        _, across, cores = self.size
        coords = (i // (across * cores), (i // cores) % across, i % cores)
        a, b, c = ((p + o) % n for p, o, n in zip(coords, offset, self.size))
        return (a * across + b) * cores + c

    def back(self, *offsets):
        return tuple(-sum(o) % n for o, n in zip(zip(*offsets), self.size))

    def send(self, value, offset):
        if not any(offset):
            return value
        route = [(i, self.other(i, offset)) for i in range(self.experts)]
        return lax.ppermute(value, "expert", route)


def other_of(plane, offset):
    _, across, cores = plane.size
    i = lax.axis_index("expert")
    coords = (lax.div(i, across * cores), lax.rem(lax.div(i, cores), across), lax.rem(i, cores))
    a, b, c = (lax.rem(p + o, n) for p, o, n in zip(coords, offset, plane.size))
    return (a * across + b) * cores + c


def expander(rows, groups, capacity):
    first = lax.broadcasted_iota(jnp.int32, (rows, groups), 1) * capacity
    row = lax.broadcasted_iota(jnp.int32, (rows, groups), 0)
    return ((row >= first) & (row < first + capacity)).astype(f32).astype(bf16)


def slot_masks(named, capacity):
    count = sum(named)
    groups, tokens = count.shape
    rows = groups * capacity
    earlier = lax.broadcasted_iota(jnp.int32, (tokens, tokens), 0)
    later = lax.broadcasted_iota(jnp.int32, (tokens, tokens), 1)
    before = (earlier < later).astype(f32).astype(bf16)
    rank = dot(count.astype(bf16), before, 1, 0)
    place = jnp.where(count > 0, rank, -1.0).astype(bf16)
    rep = expander(rows, groups, capacity)
    spread = dot(rep, place, 1, 0)
    row = lax.broadcasted_iota(jnp.int32, (rows, tokens), 0)
    owner = ((row.astype(f32) + 0.5) * (1.0 / capacity)).astype(jnp.int32)
    position = (row - owner * capacity).astype(f32)
    return (spread == position).astype(f32), rep


def slots_kernel(experts, capacity, topk, meta_ref, hot0_ref, hot1_ref, prob_ref):
    tokens = meta_ref.shape[2]
    me = lax.axis_index("expert")
    expert = lax.broadcasted_iota(jnp.int32, (experts, tokens), 0).astype(f32)
    own = meta_ref[me]
    lane = lax.broadcasted_iota(jnp.int32, prob_ref.shape, 1)
    columns = jnp.zeros(prob_ref.shape, f32)
    ranks = range(topk)
    for k, hot_ref in enumerate((hot0_ref, hot1_ref)):
        at = [k * topk + j for j in ranks]
        hot, _ = slot_masks([(own[i : i + 1, :] == expert).astype(f32) for i in at], capacity)
        hot_ref[...] = hot.astype(bf16)
        mine = me.astype(f32)
        named = [(meta_ref[:, i, :] == mine).astype(f32) for i in at]
        hot, rep = slot_masks(named, capacity)
        probs = sum(n * meta_ref[:, 2 * topk + i, :] for n, i in zip(named, at))
        column = jnp.sum(hot * dot(rep, probs.astype(bf16), 1, 0), axis=1, keepdims=True)
        columns = jnp.where(lane == k, column, columns)
    prob_ref[...] = columns


def select_kernel(plane, capacity, ranks, sources, targets, meta_ref, *refs):
    raw_refs, out_refs = refs[: len(sources)], refs[len(sources) :]
    tokens = raw_refs[0].shape[0]
    row = lax.broadcasted_iota(jnp.int32, (len(targets), tokens), 0)
    expert = jnp.zeros(row.shape, f32)
    for i, target in enumerate(targets):
        expert = jnp.where(row == i, other_of(plane, target).astype(f32), expert)
    for s, source in enumerate(sources):
        ids = meta_ref[other_of(plane, source)]
        hot, _ = slot_masks([(ids[i : i + 1, :] == expert).astype(f32) for i in ranks], capacity)
        picked = dot(hot.astype(bf16), raw_refs[s][...], 1, 0).astype(bf16)
        for i, out_ref in enumerate(out_refs):
            out_ref[s * capacity : (s + 1) * capacity, :] = picked[i * capacity : (i + 1) * capacity]


def two_step(plane, capacity, topk, tick, axis, value, meta):
    tokens, width = value.shape
    unit = lambda n: tuple(n if d == axis else 0 for d in range(3))
    hops = range(plane.size[axis])
    sources = [plane.back(unit(n)) for n in hops]
    raws = [plane.send(value, unit(n)) for n in hops]
    cross = 1 - axis
    targets = [
        tuple(n if d == cross else core if d == 2 else 0 for d in range(3))
        for n in range(plane.size[cross])
        for core in range(plane.size[2])
    ]
    ranks = [tick * topk + j for j in range(topk)]
    outs = [shaped((len(sources) * capacity, width), bf16)] * len(targets)
    flops = 2 * tokens * width * capacity * len(sources) * len(targets)
    picked = call(
        functools.partial(select_kernel, plane, capacity, ranks, sources, targets), outs, meta, *raws, flops=flops
    )
    pieces = [plane.send(p, t) for p, t in zip(picked, targets)]
    layout = [[plane.back(t, unit(n)) for n in hops] for t in targets]
    return pieces, layout


def spread_kernel(hot_ref, x_ref, out_ref):
    out_ref[...] = dot(hot_ref[...], x_ref[...], 1, 0).astype(bf16)


def spread(hot, x):
    outs = [shaped((hot.shape[0], x.shape[1]), bf16)]
    return call(spread_kernel, outs, hot, x, flops=2 * hot.size * x.shape[1])[0]


def exchange(rows, experts):
    width = rows.shape[1]
    pieces = rows.reshape(experts, -1, width)
    arrived = lax.all_to_all(pieces, "expert", split_axis=0, concat_axis=0, tiled=True)
    return arrived.reshape(-1, width)


def combine_kernel(first, hot_ref, back_ref, g_ref, out_ref):
    width = out_ref.shape[1]
    summed = dot(hot_ref[...], back_ref[...], 0, 0)
    out_ref[...] = (g_ref[:, first : first + width].astype(f32) + summed).astype(bf16)


def arrange(plane, capacity, groups, refs, out_ref):
    refs = list(refs)
    for first, layout in groups:
        if layout is None:
            piece = refs.pop(0)
            out_ref[:, first : first + piece.shape[1]] = piece[...]
            continue
        for offsets in layout:
            piece = refs.pop(0)
            lanes = slice(first, first + piece.shape[1])
            for s, offset in enumerate(offsets):
                at = pl.multiple_of(other_of(plane, offset) * capacity, 16)
                out_ref[pl.ds(at, capacity), lanes] = piece[s * capacity : (s + 1) * capacity, :]


def gelu_parts(preact):
    cdf = 0.5 * (1.0 + lax.erf(preact * half_root))
    pdf = density_scale * jnp.exp(-0.5 * preact * preact)
    return preact * cdf, cdf + preact * pdf


def preact_kernel(plane, capacity, groups, win_ref, *refs):
    x_ref, hid_ref, slope_ref = refs[-3:]
    arrange(plane, capacity, groups, refs[:-3], x_ref)
    activated, slope = gelu_parts(dot(x_ref[...], win_ref[...], 1, 1))
    hid_ref[...] = activated.astype(bf16)
    slope_ref[...] = slope


def first_kernel(plane, capacity, groups, win_ref, wout_ref, hid_ref, slope_ref, prob_ref, *refs):
    g_ref, gp_ref, score_ref, *back_refs = refs[-3 - HALVES :]
    arrange(plane, capacity, groups, refs[: -3 - HALVES], g_ref)
    pulled = dot(g_ref[...], wout_ref[...], 1, 1)
    grad_pre = (prob_ref[:, 0:1] * pulled * slope_ref[...]).astype(bf16)
    gp_ref[...] = grad_pre
    width = back_refs[0].shape[1]
    for h, back_ref in enumerate(back_refs):
        back_ref[...] = dot(grad_pre, win_ref[:, h * width : (h + 1) * width], 1, 0).astype(bf16)
    score = jnp.sum(hid_ref[...].astype(f32) * pulled, axis=1, keepdims=True)
    score_ref[...] = jnp.broadcast_to(score, score_ref.shape)


def second_kernel(wout_ref, hid_ref, slope_ref, prob_ref, score0_ref, *refs):
    g_refs, (gp_ref, score_ref) = refs[:-2], refs[-2:]
    width = g_refs[0].shape[1]
    pulled = sum(
        dot(g_ref[...], wout_ref[:, h * width : (h + 1) * width], 1, 1) for h, g_ref in enumerate(g_refs)
    )
    score = jnp.sum(hid_ref[...].astype(f32) * pulled, axis=1, keepdims=True)
    lane = lax.broadcasted_iota(jnp.int32, score_ref.shape, 1)
    both = jnp.where(lane == 0, score0_ref[...], jnp.where(lane == 1, score, 0.0))
    score_ref[...] = both.astype(bf16)
    gp_ref[...] = (prob_ref[:, 1:2] * pulled * slope_ref[...]).astype(bf16)


def grads_kernel(prob_ref, x0_ref, x1_ref, g0_ref, *refs):
    g1_refs = refs[:HALVES]
    hid0_ref, hid1_ref, gp0_ref, gp1_ref, gin_ref, gout_ref, hid, gp = refs[HALVES:]
    i = pl.program_id(0)
    rows = hid0_ref.shape[0]
    width = gin_ref.shape[1]

    @pl.when(i == 0)
    def _():
        hid[:rows, :] = hid0_ref[...]
        hid[rows:, :] = hid1_ref[...]
        gp[:rows, :] = gp0_ref[...]
        gp[rows:, :] = gp1_ref[...]

    lanes = pl.ds(pl.multiple_of(i * width, width), width)
    x = jnp.concatenate([x0_ref[:, lanes], x1_ref[:, lanes]], axis=0)
    gin_ref[...] = dot(gp[...], x, 0, 0).astype(bf16)

    per = g1_refs[0].shape[1] // width
    for h, g1_ref in enumerate(g1_refs):

        @pl.when((i >= h * per) & (i < (h + 1) * per))
        def _():
            y0 = prob_ref[:, 0:1] * g0_ref[:, lanes].astype(f32)
            part = pl.ds(pl.multiple_of((i - h * per) * width, width), width)
            y1 = prob_ref[:, 1:2] * g1_ref[:, part].astype(f32)
            y = jnp.concatenate([y0.astype(bf16), y1.astype(bf16)], axis=0)
            gout_ref[...] = dot(hid[...], y, 0, 0).astype(bf16)


def grads(width, *args):
    features = args[1].shape[1]
    rows, units = args[-1].shape
    outs = [shaped((units, features), bf16)] * 2
    return pl.pallas_call(
        grads_kernel,
        grid=(features // width,),
        out_shape=outs,
        in_specs=[VMEM] * len(args),
        out_specs=[pl.BlockSpec((units, width), lambda i: (0, i))] * 2,
        scratch_shapes=[pltpu.VMEM((2 * rows, units), bf16)] * 2,
        compiler_params=pltpu.CompilerParams(vmem_limit_bytes=VMEM_LIMIT),
        cost_estimate=cost(args, outs, 8 * units * rows * features),
    )(*args)


def collect_kernel(experts, capacity, topk, meta_ref, hot0_ref, hot1_ref, score_ref, out_ref):
    tokens = meta_ref.shape[2]
    rep = expander(experts * capacity, experts, capacity)
    expert = lax.broadcasted_iota(jnp.int32, (experts, tokens), 0).astype(f32)
    own = meta_ref[lax.axis_index("expert")]
    for k, hot_ref in enumerate((hot0_ref, hot1_ref)):
        placed = hot_ref[...].astype(f32) * score_ref[:, k : k + 1].astype(f32)
        by_expert = dot(rep, placed.astype(bf16), 0, 0)
        for j in range(topk):
            i = k * topk + j
            picked = jnp.where(own[i : i + 1, :] == expert, by_expert, 0.0)
            out_ref[i : i + 1, :] = jnp.sum(picked, axis=0, keepdims=True).astype(bf16)


def body(inputs, entering, weight_in, weight_out, gate_probs, expert_ids):
    experts = lax.axis_size("expert")
    segments = lax.axis_size("segment")
    tokens, features = entering.shape[1:]
    ticks, topk = expert_ids.shape[1], expert_ids.shape[3]
    units = weight_in.shape[2]
    capacity = 3 * tokens * topk // (2 * experts)
    rows = experts * capacity
    plane = Plane(experts)
    matmul = 2 * rows * units * features
    half = features // HALVES
    w_in, w_out = weight_in[0, 0], weight_out[0, 0]
    x0, x1, g0 = inputs[0, 0], inputs[0, 1], entering[0]

    ids = jnp.transpose(expert_ids[0], (0, 2, 1)).reshape(ticks * topk, tokens)
    probs = jnp.transpose(gate_probs[0], (0, 2, 1)).reshape(ticks * topk, tokens)
    meta = jnp.concatenate([ids.astype(f32), probs.astype(f32)], axis=0)
    meta = jnp.broadcast_to(meta[None], (experts,) + meta.shape)
    meta = lax.all_to_all(meta, "expert", split_axis=0, concat_axis=0, tiled=True)
    hot0, hot1, prob = call(
        functools.partial(slots_kernel, experts, capacity, topk),
        [shaped((rows, tokens), bf16)] * 2 + [shaped((rows, LANES), f32)],
        meta,
    )

    if capacity % 16 == 0:
        step = functools.partial(two_step, plane, capacity, topk)
        x0, x0_layout = step(0, 1, x0, meta)
        g0_in, g0_layout = step(0, 0, g0, meta)
        left, left_layout = step(1, 1, x1[:, :half], meta)
        right, right_layout = step(1, 0, x1[:, half:], meta)
        x1, x1_groups = left + right, [(0, left_layout), (half, right_layout)]
    else:
        x0, x0_layout = [exchange(spread(hot0, x0), experts)], None
        g0_in, g0_layout = [exchange(spread(hot0, g0), experts)], None
        x1, x1_groups = [exchange(spread(hot1, x1), experts)], [(0, None)]

    acts = [shaped((rows, features), bf16), shaped((rows, units), bf16), shaped((rows, units), f32)]
    x0, hid0, slope0 = call(
        functools.partial(preact_kernel, plane, capacity, [(0, x0_layout)]), acts, w_in, *x0, flops=matmul
    )
    g0_in, gp0, score0, *backs = call(
        functools.partial(first_kernel, plane, capacity, [(0, g0_layout)]),
        [shaped((rows, features), bf16), shaped((rows, units), bf16), shaped((rows, LANES), f32)]
        + [shaped((rows, half), bf16)] * HALVES,
        w_in, w_out, hid0, slope0, prob, *g0_in, flops=2 * matmul,
    )
    x1, hid1, slope1 = call(
        functools.partial(preact_kernel, plane, capacity, x1_groups), acts, w_in, *x1, flops=matmul
    )
    g1 = []
    for h, back in enumerate(backs):
        back = exchange(back, experts)
        (leaving,) = call(
            functools.partial(combine_kernel, h * half), [shaped((tokens, half), bf16)], hot0, back, g0,
            flops=2 * rows * tokens * half,
        )
        arrived = lax.ppermute(leaving, "segment", [(i, i - 1) for i in range(1, segments)])
        g1.append(exchange(spread(hot1, arrived), experts))
    gp1, scores = call(
        second_kernel, [shaped((rows, units), bf16), shaped((rows, LANES), bf16)],
        w_out, hid1, slope1, prob, score0, *g1, flops=matmul,
    )
    scores = exchange(scores, experts)
    grad_in, grad_out = grads(half // 2, prob, x0, x1, g0_in, *g1, hid0, hid1, gp0, gp1)
    (prob_grads,) = call(
        functools.partial(collect_kernel, experts, capacity, topk),
        [shaped((ticks * topk, tokens), bf16)], meta, hot0, hot1, scores,
    )
    prob_grads = jnp.transpose(prob_grads.reshape(ticks, topk, tokens), (0, 2, 1))
    return grad_in[None, None], grad_out[None, None], prob_grads[None]


def solution(mesh):
    return jax.shard_map(
        body,
        mesh=mesh,
        in_specs=(
            P("segment", None, "expert", None),
            P("segment", "expert", None),
            P("segment", "expert", None, None),
            P("segment", "expert", None, None),
            P("segment", None, "expert", None),
            P("segment", None, "expert", None),
        ),
        out_specs=(
            P("segment", "expert", None, None),
            P("segment", "expert", None, None),
            P("segment", None, "expert", None),
        ),
        check_vma=False,
    )
```

```python
import functools

import jax
import jax.numpy as jnp
from jax import lax
from jax.experimental import pallas as pl
from jax.experimental.pallas import tpu as pltpu
from jax.sharding import PartitionSpec as P

half_root = 0.7071067811865476
density_scale = 0.3989422804014327
LANES = 128
AXES = (2, 2)
HALVES = len(AXES)
VMEM_LIMIT = 20 * 1024 * 1024
f32 = jnp.float32
bf16 = jnp.bfloat16


def dot(a, b, ca, cb):
    return lax.dot_general(a, b, (((ca,), (cb,)), ((), ())), preferred_element_type=f32)


def shaped(shape, dtype):
    return jax.ShapeDtypeStruct(shape, dtype)


def cost(args, outs, flops):
    size = sum(a.size * a.dtype.itemsize for a in list(args) + list(outs))
    return pl.CostEstimate(flops=flops, bytes_accessed=size, transcendentals=0)


def call(kernel, outs, *args, flops=0, scratch=()):
    return pl.pallas_call(
        kernel,
        out_shape=outs,
        scratch_shapes=scratch,
        compiler_params=pltpu.CompilerParams(vmem_limit_bytes=VMEM_LIMIT),
        cost_estimate=cost(args, outs, flops),
    )(*args)


class Plane:
    def __init__(self, experts):
        chips = experts // 2
        across = next(n for n in range(int(chips**0.5), 0, -1) if chips % n == 0)
        self.size = (chips // across, across, 2)
        self.experts = experts

    def other(self, i, offset):
        _, across, cores = self.size
        coords = (i // (across * cores), (i // cores) % across, i % cores)
        a, b, c = ((p + o) % n for p, o, n in zip(coords, offset, self.size))
        return (a * across + b) * cores + c

    def back(self, *offsets):
        return tuple(-sum(o) % n for o, n in zip(zip(*offsets), self.size))

    def along(self, axis):
        return [tuple(n if d == axis else 0 for d in range(3)) for n in range(self.size[axis])]

    def across(self, axis):
        spans = [range(1 if d == axis else n) for d, n in enumerate(self.size)]
        return [(a, b, c) for a in spans[0] for b in spans[1] for c in spans[2]]

    def send(self, value, offset):
        if not any(offset):
            return value
        route = [(i, self.other(i, offset)) for i in range(self.experts)]
        return lax.ppermute(value, "expert", route)


def other_of(plane, offset):
    _, across, cores = plane.size
    i = lax.axis_index("expert")
    coords = (lax.div(i, across * cores), lax.rem(lax.div(i, cores), across), lax.rem(i, cores))
    a, b, c = (lax.rem(p + o, n) for p, o, n in zip(coords, offset, plane.size))
    return (a * across + b) * cores + c


def expander(rows, groups, capacity):
    first = lax.broadcasted_iota(jnp.int32, (rows, groups), 1) * capacity
    row = lax.broadcasted_iota(jnp.int32, (rows, groups), 0)
    return ((row >= first) & (row < first + capacity)).astype(f32).astype(bf16)


def slot_masks(named, capacity):
    count = sum(named)
    groups, tokens = count.shape
    rows = groups * capacity
    earlier = lax.broadcasted_iota(jnp.int32, (tokens, tokens), 0)
    later = lax.broadcasted_iota(jnp.int32, (tokens, tokens), 1)
    before = (earlier < later).astype(f32).astype(bf16)
    rank = dot(count.astype(bf16), before, 1, 0)
    place = jnp.where(count > 0, rank, -1.0).astype(bf16)
    rep = expander(rows, groups, capacity)
    spread = dot(rep, place, 1, 0)
    row = lax.broadcasted_iota(jnp.int32, (rows, tokens), 0)
    owner = ((row.astype(f32) + 0.5) * (1.0 / capacity)).astype(jnp.int32)
    position = (row - owner * capacity).astype(f32)
    return (spread == position).astype(f32), rep


def slots_kernel(experts, capacity, topk, meta_ref, hot0_ref, hot1_ref, prob_ref):
    tokens = meta_ref.shape[2]
    me = lax.axis_index("expert")
    expert = lax.broadcasted_iota(jnp.int32, (experts, tokens), 0).astype(f32)
    own = meta_ref[me]
    lane = lax.broadcasted_iota(jnp.int32, prob_ref.shape, 1)
    columns = jnp.zeros(prob_ref.shape, f32)
    ranks = range(topk)
    for k, hot_ref in enumerate((hot0_ref, hot1_ref)):
        at = [k * topk + j for j in ranks]
        hot, _ = slot_masks([(own[i : i + 1, :] == expert).astype(f32) for i in at], capacity)
        hot_ref[...] = hot.astype(bf16)
        mine = me.astype(f32)
        named = [(meta_ref[:, i, :] == mine).astype(f32) for i in at]
        hot, rep = slot_masks(named, capacity)
        probs = sum(n * meta_ref[:, 2 * topk + i, :] for n, i in zip(named, at))
        column = jnp.sum(hot * dot(rep, probs.astype(bf16), 1, 0), axis=1, keepdims=True)
        columns = jnp.where(lane == k, column, columns)
    prob_ref[...] = columns


def block_masks(plane, capacity, ranks, meta_ref, block, experts):
    tokens = meta_ref.shape[2]
    row = lax.broadcasted_iota(jnp.int32, (len(experts), tokens), 0)
    expert = jnp.zeros(row.shape, f32)
    for i, offset in enumerate(experts):
        expert = jnp.where(row == i, other_of(plane, offset).astype(f32), expert)
    ids = meta_ref[other_of(plane, block)]
    return slot_masks([(ids[i : i + 1, :] == expert).astype(f32) for i in ranks], capacity)[0]


def masks_kernel(plane, capacity, plans, meta_ref, *out_refs):
    for (ranks, blocks, experts), out_ref in zip(plans, out_refs):
        for s, block in enumerate(blocks):
            out_ref[s] = block_masks(plane, capacity, ranks, meta_ref, block, experts).astype(bf16)


def select_kernel(plane, capacity, plan, meta_ref, *refs):
    ranks, sources, targets = plan
    raw_refs, out_refs = refs[: len(sources)], refs[len(sources) :]
    for s, source in enumerate(sources):
        hot = block_masks(plane, capacity, ranks, meta_ref, source, targets)
        picked = dot(hot.astype(bf16), raw_refs[s][...], 1, 0).astype(bf16)
        for i, out_ref in enumerate(out_refs):
            out_ref[s * capacity : (s + 1) * capacity, :] = picked[i * capacity : (i + 1) * capacity]


def pick_kernel(capacity, sources, hot_ref, *refs):
    raw_refs, out_refs = refs[:sources], refs[sources:]
    for s, raw_ref in enumerate(raw_refs):
        picked = dot(hot_ref[s], raw_ref[...], 1, 0).astype(bf16)
        for i, out_ref in enumerate(out_refs):
            out_ref[s * capacity : (s + 1) * capacity, :] = picked[i * capacity : (i + 1) * capacity]


def gather_plan(plane, ranks, axis):
    return ranks, [plane.back(u) for u in plane.along(axis)], plane.across(axis)


def return_plan(plane, ranks, axis):
    return ranks, plane.along(axis), [plane.back(t) for t in plane.across(axis)]


def picked_rows(plane, capacity, ranks, axis, value, meta, hot=None):
    tokens, width = value.shape
    plan = gather_plan(plane, ranks, axis)
    raws = [plane.send(value, u) for u in plane.along(axis)]
    outs = [shaped((len(plan[1]) * capacity, width), bf16)] * len(plan[2])
    flops = 2 * tokens * width * capacity * len(plan[1]) * len(plan[2])
    if hot is None:
        return call(functools.partial(select_kernel, plane, capacity, plan), outs, meta, *raws, flops=flops)
    return call(functools.partial(pick_kernel, capacity, len(raws)), outs, hot, *raws, flops=flops)


def sent_rows(plane, axis, picked):
    targets = plane.across(axis)
    pieces = [plane.send(p, t) for p, t in zip(picked, targets)]
    return pieces, [[plane.back(t, u) for u in plane.along(axis)] for t in targets]


def combine_parts_kernel(capacity, blocks, hot_ref, *refs):
    pieces, out_refs = refs[:-blocks], refs[-blocks:]
    for s, out_ref in enumerate(out_refs):
        rows = jnp.concatenate([p[s * capacity : (s + 1) * capacity, :] for p in pieces], axis=0)
        out_ref[...] = dot(hot_ref[s], rows, 0, 0).astype(out_ref.dtype)


def add_kernel(first, g_ref, own_ref, *refs):
    out_ref = refs[-1]
    width = out_ref.shape[1]
    total = g_ref[:, first : first + width].astype(f32) + own_ref[...]
    for ref in refs[:-1]:
        total = total + ref[...].astype(f32)
    out_ref[...] = total.astype(bf16)


def returned_rows(plane, capacity, axis, pieces, hot, g, first):
    width, tokens = pieces[0].shape[1], g.shape[0]
    pieces = [plane.send(p, t) for p, t in zip(pieces, plane.across(axis))]
    along = plane.along(axis)
    outs = [shaped((tokens, width), bf16 if any(u) else f32) for u in along]
    own, *parts = call(
        functools.partial(combine_parts_kernel, capacity, len(along)), outs, hot, *pieces,
        flops=2 * hot.size * width,
    )
    parts = [plane.send(p, u) for p, u in zip(parts, along[1:])]
    return call(functools.partial(add_kernel, first), [shaped((tokens, width), bf16)], g, own, *parts)[0]


def spread_kernel(hot_ref, x_ref, out_ref):
    out_ref[...] = dot(hot_ref[...], x_ref[...], 1, 0).astype(bf16)


def spread(hot, x):
    outs = [shaped((hot.shape[0], x.shape[1]), bf16)]
    return call(spread_kernel, outs, hot, x, flops=2 * hot.size * x.shape[1])[0]


def exchange(rows, experts):
    width = rows.shape[1]
    pieces = rows.reshape(experts, -1, width)
    arrived = lax.all_to_all(pieces, "expert", split_axis=0, concat_axis=0, tiled=True)
    return arrived.reshape(-1, width)


def combine_kernel(first, hot_ref, back_ref, g_ref, out_ref):
    width = out_ref.shape[1]
    summed = dot(hot_ref[...], back_ref[...], 0, 0)
    out_ref[...] = (g_ref[:, first : first + width].astype(f32) + summed).astype(bf16)


def arrange(plane, capacity, groups, refs, out_ref):
    refs = list(refs)
    for first, layout in groups:
        if layout is None:
            piece = refs.pop(0)
            out_ref[:, first : first + piece.shape[1]] = piece[...]
            continue
        for offsets in layout:
            piece = refs.pop(0)
            lanes = slice(first, first + piece.shape[1])
            for s, offset in enumerate(offsets):
                at = pl.multiple_of(other_of(plane, offset) * capacity, 16)
                out_ref[pl.ds(at, capacity), lanes] = piece[s * capacity : (s + 1) * capacity, :]


def gelu_parts(preact):
    cdf = 0.5 * (1.0 + lax.erf(preact * half_root))
    pdf = density_scale * jnp.exp(-0.5 * preact * preact)
    return preact * cdf, cdf + preact * pdf


def preact_kernel(plane, capacity, groups, win_ref, *refs):
    x_ref, hid_ref, slope_ref = refs[-3:]
    arrange(plane, capacity, groups, refs[:-3], x_ref)
    activated, slope = gelu_parts(dot(x_ref[...], win_ref[...], 1, 1))
    hid_ref[...] = activated.astype(bf16)
    slope_ref[...] = slope


def first_kernel(plane, capacity, groups, plans, win_ref, wout_ref, hid_ref, slope_ref, prob_ref, *refs):
    refs, back = refs[:-1], refs[-1]
    pieces = sum(1 if plan is None else len(plan) for plan in plans)
    refs, back_refs = refs[:-pieces], list(refs[-pieces:])
    g_ref, gp_ref, score_ref = refs[-3:]
    arrange(plane, capacity, groups, refs[:-3], g_ref)
    pulled = dot(g_ref[...], wout_ref[...], 1, 1)
    grad_pre = (prob_ref[:, 0:1] * pulled * slope_ref[...]).astype(bf16)
    gp_ref[...] = grad_pre
    width = back.shape[1]
    for h, plan in enumerate(plans):
        back[...] = dot(grad_pre, win_ref[:, h * width : (h + 1) * width], 1, 0).astype(bf16)
        if plan is None:
            back_refs.pop(0)[...] = back[...]
            continue
        for blocks in plan:
            out_ref = back_refs.pop(0)
            for s, block in enumerate(blocks):
                at = pl.multiple_of(other_of(plane, block) * capacity, 16)
                out_ref[s * capacity : (s + 1) * capacity, :] = back[pl.ds(at, capacity), :]
    score = jnp.sum(hid_ref[...].astype(f32) * pulled, axis=1, keepdims=True)
    score_ref[...] = jnp.broadcast_to(score, score_ref.shape)


def second_kernel(plane, capacity, groups, wout_ref, hid_ref, slope_ref, prob_ref, score0_ref, *refs):
    g_ref, gp_ref, score_ref = refs[-3:]
    arrange(plane, capacity, groups, refs[:-3], g_ref)
    pulled = dot(g_ref[...], wout_ref[...], 1, 1)
    score = jnp.sum(hid_ref[...].astype(f32) * pulled, axis=1, keepdims=True)
    lane = lax.broadcasted_iota(jnp.int32, score_ref.shape, 1)
    both = jnp.where(lane == 0, score0_ref[...], jnp.where(lane == 1, score, 0.0))
    score_ref[...] = both.astype(bf16)
    gp_ref[...] = (prob_ref[:, 1:2] * pulled * slope_ref[...]).astype(bf16)


def grads_kernel(prob_ref, x0_ref, x1_ref, g0_ref, g1_ref, hid0_ref, hid1_ref, gp0_ref, gp1_ref, gin_ref, gout_ref, hid, gp):
    rows = hid0_ref.shape[0]

    @pl.when(pl.program_id(0) == 0)
    def _():
        hid[:rows, :] = hid0_ref[...]
        hid[rows:, :] = hid1_ref[...]
        gp[:rows, :] = gp0_ref[...]
        gp[rows:, :] = gp1_ref[...]

    x = jnp.concatenate([x0_ref[...], x1_ref[...]], axis=0)
    gin_ref[...] = dot(gp[...], x, 0, 0).astype(bf16)
    y0 = (prob_ref[:, 0:1] * g0_ref[...].astype(f32)).astype(bf16)
    y1 = (prob_ref[:, 1:2] * g1_ref[...].astype(f32)).astype(bf16)
    gout_ref[...] = dot(hid[...], jnp.concatenate([y0, y1], axis=0), 0, 0).astype(bf16)


def grads(width, prob, x0, x1, g0, g1, hid0, hid1, gp0, gp1):
    args = (prob, x0, x1, g0, g1, hid0, hid1, gp0, gp1)
    rows, units = hid0.shape
    features = x0.shape[1]
    outs = [shaped((units, features), bf16)] * 2
    tile = pl.BlockSpec((rows, width), lambda i: (0, i))
    whole = lambda a: pl.BlockSpec(a.shape, lambda i: (0, 0))
    return pl.pallas_call(
        grads_kernel,
        grid=(features // width,),
        out_shape=outs,
        in_specs=[whole(prob)] + [tile] * 4 + [whole(hid0)] * 4,
        out_specs=[pl.BlockSpec((units, width), lambda i: (0, i))] * 2,
        scratch_shapes=[pltpu.VMEM((2 * rows, units), bf16)] * 2,
        compiler_params=pltpu.CompilerParams(vmem_limit_bytes=VMEM_LIMIT),
        cost_estimate=cost(args, outs, 8 * units * rows * features),
    )(*args)


def collect_kernel(experts, capacity, topk, meta_ref, hot0_ref, hot1_ref, score_ref, out_ref):
    tokens = meta_ref.shape[2]
    rep = expander(experts * capacity, experts, capacity)
    expert = lax.broadcasted_iota(jnp.int32, (experts, tokens), 0).astype(f32)
    own = meta_ref[lax.axis_index("expert")]
    for k, hot_ref in enumerate((hot0_ref, hot1_ref)):
        placed = hot_ref[...].astype(f32) * score_ref[:, k : k + 1].astype(f32)
        by_expert = dot(rep, placed.astype(bf16), 0, 0)
        for j in range(topk):
            i = k * topk + j
            picked = jnp.where(own[i : i + 1, :] == expert, by_expert, 0.0)
            out_ref[i : i + 1, :] = jnp.sum(picked, axis=0, keepdims=True).astype(bf16)


def body(inputs, entering, weight_in, weight_out, gate_probs, expert_ids):
    experts = lax.axis_size("expert")
    segments = lax.axis_size("segment")
    tokens, features = entering.shape[1:]
    ticks, topk = expert_ids.shape[1], expert_ids.shape[3]
    units = weight_in.shape[2]
    capacity = 3 * tokens * topk // (2 * experts)
    rows = experts * capacity
    plane = Plane(experts)
    matmul = 2 * rows * units * features
    half = features // HALVES
    w_in, w_out = weight_in[0, 0], weight_out[0, 0]
    x0, x1, g0 = inputs[0, 0], inputs[0, 1], entering[0]

    ids = jnp.transpose(expert_ids[0], (0, 2, 1)).reshape(ticks * topk, tokens)
    probs = jnp.transpose(gate_probs[0], (0, 2, 1)).reshape(ticks * topk, tokens)
    meta = jnp.concatenate([ids.astype(f32), probs.astype(f32)], axis=0)
    meta = jnp.broadcast_to(meta[None], (experts,) + meta.shape)
    meta = lax.all_to_all(meta, "expert", split_axis=0, concat_axis=0, tiled=True)
    hot0, hot1, prob = call(
        functools.partial(slots_kernel, experts, capacity, topk),
        [shaped((rows, tokens), bf16)] * 2 + [shaped((rows, LANES), f32)],
        meta,
    )

    acts = [shaped((rows, features), bf16), shaped((rows, units), bf16), shaped((rows, units), f32)]
    stepped = capacity % 16 == 0
    ranks = [list(range(k * topk, (k + 1) * topk)) for k in range(ticks)]
    pick = functools.partial(picked_rows, plane, capacity)
    if stepped:
        x0, x0_layout = sent_rows(plane, 1, pick(ranks[0], 1, x0, meta))
        g0_in, g0_layout = sent_rows(plane, 0, pick(ranks[0], 0, g0, meta))
        left = pick(ranks[1], 1, x1[:, :half], meta)
        right = pick(ranks[1], 0, x1[:, half:], meta)
        g0_in, _ = lax.optimization_barrier((g0_in, (left, right)))
        plans = [return_plan(plane, ranks[0], axis) for axis in AXES]
        plans += [gather_plan(plane, ranks[1], axis) for axis in AXES]
        shapes = [shaped((len(b), len(e) * capacity, tokens), bf16) for _, b, e in plans]
        masks = call(functools.partial(masks_kernel, plane, capacity, plans), shapes, meta)
        back_plans = [[[plane.back(plane.back(t, u)) for u in plane.along(axis)] for t in plane.across(axis)] for axis in AXES]
        shapes = [shaped((len(blocks) * capacity, half), bf16) for plan in back_plans for blocks in plan]
    else:
        x0, x0_layout = [exchange(spread(hot0, x0), experts)], None
        g0_in, g0_layout = [exchange(spread(hot0, g0), experts)], None
        back_plans = [None] * HALVES
        shapes = [shaped((rows, half), bf16)] * HALVES

    x0, hid0, slope0 = call(
        functools.partial(preact_kernel, plane, capacity, [(0, x0_layout)]), acts, w_in, *x0, flops=matmul
    )
    g0_in, gp0, score0, *backs = call(
        functools.partial(first_kernel, plane, capacity, [(0, g0_layout)], back_plans),
        [shaped((rows, features), bf16), shaped((rows, units), bf16), shaped((rows, LANES), f32)] + shapes,
        w_in, w_out, hid0, slope0, prob, *g0_in, flops=2 * matmul,
        scratch=[pltpu.VMEM((rows, half), bf16)],
    )
    if stepped:
        left, left_layout = sent_rows(plane, 1, left)
        right, right_layout = sent_rows(plane, 0, right)
        x1, x1_groups = left + right, [(0, left_layout), (half, right_layout)]
    else:
        x1, x1_groups = [exchange(spread(hot1, x1), experts)], [(0, None)]
    x1, hid1, slope1 = call(
        functools.partial(preact_kernel, plane, capacity, x1_groups), acts, w_in, *x1, flops=matmul
    )

    g1, g1_groups = [], []
    for h, axis in enumerate(AXES):
        if stepped:
            count = len(plane.across(axis))
            pieces, backs = backs[:count], backs[count:]
            leaving = returned_rows(plane, capacity, axis, pieces, masks[h], g0, h * half)
        else:
            (leaving,) = call(
                functools.partial(combine_kernel, h * half), [shaped((tokens, half), bf16)],
                hot0, exchange(backs[h], experts), g0, flops=2 * rows * tokens * half,
            )
        arrived = lax.ppermute(leaving, "segment", [(i, i - 1) for i in range(1, segments)])
        if stepped:
            pieces, layout = sent_rows(plane, axis, pick(ranks[1], axis, arrived, meta, masks[HALVES + h]))
        else:
            pieces, layout = [exchange(spread(hot1, arrived), experts)], None
        g1 += pieces
        g1_groups.append((h * half, layout))
    g1, gp1, scores = call(
        functools.partial(second_kernel, plane, capacity, g1_groups),
        [shaped((rows, features), bf16), shaped((rows, units), bf16), shaped((rows, LANES), bf16)],
        w_out, hid1, slope1, prob, score0, *g1, flops=matmul,
    )
    scores = exchange(scores, experts)
    grad_in, grad_out = grads(half // 2, prob, x0, x1, g0_in, g1, hid0, hid1, gp0, gp1)
    (prob_grads,) = call(
        functools.partial(collect_kernel, experts, capacity, topk),
        [shaped((ticks * topk, tokens), bf16)], meta, hot0, hot1, scores,
    )
    prob_grads = jnp.transpose(prob_grads.reshape(ticks, topk, tokens), (0, 2, 1))
    return grad_in[None, None], grad_out[None, None], prob_grads[None]


def solution(mesh):
    return jax.shard_map(
        body,
        mesh=mesh,
        in_specs=(
            P("segment", None, "expert", None),
            P("segment", "expert", None),
            P("segment", "expert", None, None),
            P("segment", "expert", None, None),
            P("segment", None, "expert", None),
            P("segment", None, "expert", None),
        ),
        out_specs=(
            P("segment", "expert", None, None),
            P("segment", "expert", None, None),
            P("segment", None, "expert", None),
        ),
        check_vma=False,
    )
```

```python
import functools

import jax
import jax.numpy as jnp
from jax import lax
from jax.experimental import pallas as pl
from jax.experimental.pallas import tpu as pltpu
from jax.sharding import PartitionSpec as P

half_root = 0.7071067811865476
density_scale = 0.3989422804014327
LANES = 128
AXES = (2, 2)
HALVES = len(AXES)
VMEM_LIMIT = 20 * 1024 * 1024
f32 = jnp.float32
bf16 = jnp.bfloat16


def dot(a, b, ca, cb):
    return lax.dot_general(a, b, (((ca,), (cb,)), ((), ())), preferred_element_type=f32)


def shaped(shape, dtype):
    return jax.ShapeDtypeStruct(shape, dtype)


def cost(args, outs, flops):
    size = sum(a.size * a.dtype.itemsize for a in list(args) + list(outs))
    return pl.CostEstimate(flops=flops, bytes_accessed=size, transcendentals=0)


def call(kernel, outs, *args, flops=0, scratch=()):
    return pl.pallas_call(
        kernel,
        out_shape=outs,
        scratch_shapes=scratch,
        compiler_params=pltpu.CompilerParams(vmem_limit_bytes=VMEM_LIMIT),
        cost_estimate=cost(args, outs, flops),
    )(*args)


class Plane:
    def __init__(self, experts):
        chips = experts // 2
        across = next(n for n in range(int(chips**0.5), 0, -1) if chips % n == 0)
        self.size = (chips // across, across, 2)
        self.experts = experts

    def other(self, i, offset):
        _, across, cores = self.size
        coords = (i // (across * cores), (i // cores) % across, i % cores)
        a, b, c = ((p + o) % n for p, o, n in zip(coords, offset, self.size))
        return (a * across + b) * cores + c

    def back(self, *offsets):
        return tuple(-sum(o) % n for o, n in zip(zip(*offsets), self.size))

    def along(self, axis):
        return [tuple(n if d == axis else 0 for d in range(3)) for n in range(self.size[axis])]

    def across(self, axis):
        spans = [range(1 if d == axis else n) for d, n in enumerate(self.size)]
        return [(a, b, c) for a in spans[0] for b in spans[1] for c in spans[2]]

    def send(self, value, offset):
        if not any(offset):
            return value
        route = [(i, self.other(i, offset)) for i in range(self.experts)]
        return lax.ppermute(value, "expert", route)


def other_of(plane, offset):
    _, across, cores = plane.size
    i = lax.axis_index("expert")
    coords = (lax.div(i, across * cores), lax.rem(lax.div(i, cores), across), lax.rem(i, cores))
    a, b, c = (lax.rem(p + o, n) for p, o, n in zip(coords, offset, plane.size))
    return (a * across + b) * cores + c


def expander(rows, groups, capacity):
    first = lax.broadcasted_iota(jnp.int32, (rows, groups), 1) * capacity
    row = lax.broadcasted_iota(jnp.int32, (rows, groups), 0)
    return ((row >= first) & (row < first + capacity)).astype(f32).astype(bf16)


def slot_masks(named, capacity):
    count = sum(named)
    groups, tokens = count.shape
    rows = groups * capacity
    earlier = lax.broadcasted_iota(jnp.int32, (tokens, tokens), 0)
    later = lax.broadcasted_iota(jnp.int32, (tokens, tokens), 1)
    before = (earlier < later).astype(f32).astype(bf16)
    rank = dot(count.astype(bf16), before, 1, 0)
    place = jnp.where(count > 0, rank, -1.0).astype(bf16)
    rep = expander(rows, groups, capacity)
    spread = dot(rep, place, 1, 0)
    row = lax.broadcasted_iota(jnp.int32, (rows, tokens), 0)
    owner = ((row.astype(f32) + 0.5) * (1.0 / capacity)).astype(jnp.int32)
    position = (row - owner * capacity).astype(f32)
    return (spread == position).astype(f32), rep


def slots_kernel(experts, capacity, topk, meta_ref, hot0_ref, hot1_ref, prob_ref):
    tokens = meta_ref.shape[2]
    me = lax.axis_index("expert")
    expert = lax.broadcasted_iota(jnp.int32, (experts, tokens), 0).astype(f32)
    own = meta_ref[me]
    lane = lax.broadcasted_iota(jnp.int32, prob_ref.shape, 1)
    columns = jnp.zeros(prob_ref.shape, f32)
    ranks = range(topk)
    for k, hot_ref in enumerate((hot0_ref, hot1_ref)):
        at = [k * topk + j for j in ranks]
        hot, _ = slot_masks([(own[i : i + 1, :] == expert).astype(f32) for i in at], capacity)
        hot_ref[...] = hot.astype(bf16)
        mine = me.astype(f32)
        named = [(meta_ref[:, i, :] == mine).astype(f32) for i in at]
        hot, rep = slot_masks(named, capacity)
        probs = sum(n * meta_ref[:, 2 * topk + i, :] for n, i in zip(named, at))
        column = jnp.sum(hot * dot(rep, probs.astype(bf16), 1, 0), axis=1, keepdims=True)
        columns = jnp.where(lane == k, column, columns)
    prob_ref[...] = columns


def block_masks(plane, capacity, ranks, meta_ref, block, experts):
    tokens = meta_ref.shape[2]
    row = lax.broadcasted_iota(jnp.int32, (len(experts), tokens), 0)
    expert = jnp.zeros(row.shape, f32)
    for i, offset in enumerate(experts):
        expert = jnp.where(row == i, other_of(plane, offset).astype(f32), expert)
    ids = meta_ref[other_of(plane, block)]
    return slot_masks([(ids[i : i + 1, :] == expert).astype(f32) for i in ranks], capacity)[0]


def masks_kernel(plane, capacity, plans, meta_ref, *out_refs):
    for (ranks, blocks, experts), out_ref in zip(plans, out_refs):
        for s, block in enumerate(blocks):
            out_ref[s] = block_masks(plane, capacity, ranks, meta_ref, block, experts).astype(bf16)


def select_kernel(plane, capacity, plan, meta_ref, *refs):
    ranks, sources, targets = plan
    raw_refs, out_refs = refs[: len(sources)], refs[len(sources) :]
    for s, source in enumerate(sources):
        hot = block_masks(plane, capacity, ranks, meta_ref, source, targets)
        picked = dot(hot.astype(bf16), raw_refs[s][...], 1, 0).astype(bf16)
        for i, out_ref in enumerate(out_refs):
            out_ref[s * capacity : (s + 1) * capacity, :] = picked[i * capacity : (i + 1) * capacity]


def pick_kernel(capacity, sources, hot_ref, *refs):
    raw_refs, out_refs = refs[:sources], refs[sources:]
    for s, raw_ref in enumerate(raw_refs):
        picked = dot(hot_ref[s], raw_ref[...], 1, 0).astype(bf16)
        for i, out_ref in enumerate(out_refs):
            out_ref[s * capacity : (s + 1) * capacity, :] = picked[i * capacity : (i + 1) * capacity]


def gather_plan(plane, ranks, axis):
    return ranks, [plane.back(u) for u in plane.along(axis)], plane.across(axis)


def return_plan(plane, ranks, axis):
    return ranks, plane.along(axis), [plane.back(t) for t in plane.across(axis)]


def picked_rows(plane, capacity, ranks, axis, value, meta, hot=None):
    tokens, width = value.shape
    plan = gather_plan(plane, ranks, axis)
    raws = [plane.send(value, u) for u in plane.along(axis)]
    outs = [shaped((len(plan[1]) * capacity, width), bf16)] * len(plan[2])
    flops = 2 * tokens * width * capacity * len(plan[1]) * len(plan[2])
    if hot is None:
        return call(functools.partial(select_kernel, plane, capacity, plan), outs, meta, *raws, flops=flops)
    return call(functools.partial(pick_kernel, capacity, len(raws)), outs, hot, *raws, flops=flops)


def sent_rows(plane, axis, picked):
    targets = plane.across(axis)
    pieces = [plane.send(p, t) for p, t in zip(picked, targets)]
    return pieces, [[plane.back(t, u) for u in plane.along(axis)] for t in targets]


def combine_parts_kernel(capacity, blocks, hot_ref, *refs):
    pieces, out_refs = refs[:-blocks], refs[-blocks:]
    for s, out_ref in enumerate(out_refs):
        rows = jnp.concatenate([p[s * capacity : (s + 1) * capacity, :] for p in pieces], axis=0)
        out_ref[...] = dot(hot_ref[s], rows, 0, 0).astype(out_ref.dtype)


def add_kernel(first, g_ref, own_ref, *refs):
    out_ref = refs[-1]
    width = out_ref.shape[1]
    total = g_ref[:, first : first + width].astype(f32) + own_ref[...]
    for ref in refs[:-1]:
        total = total + ref[...].astype(f32)
    out_ref[...] = total.astype(bf16)


def returned_rows(plane, capacity, axis, pieces, hot, g, first, after):
    width, tokens = pieces[0].shape[1], g.shape[0]
    pieces = [plane.send(p, t) for p, t in zip(pieces, plane.across(axis))]
    pieces = behind(pieces, after)
    along = plane.along(axis)
    outs = [shaped((tokens, width), bf16 if any(u) else f32) for u in along]
    own, *parts = call(
        functools.partial(combine_parts_kernel, capacity, len(along)), outs, hot, *pieces,
        flops=2 * hot.size * width,
    )
    sent = [plane.send(p, u) for p, u in zip(parts, along[1:])]
    return call(functools.partial(add_kernel, first), [shaped((tokens, width), bf16)], g, own, *sent)[0], parts


def behind(values, after):
    return lax.optimization_barrier((values, after))[0] if after else values


def spread_kernel(hot_ref, x_ref, out_ref):
    out_ref[...] = dot(hot_ref[...], x_ref[...], 1, 0).astype(bf16)


def spread(hot, x):
    outs = [shaped((hot.shape[0], x.shape[1]), bf16)]
    return call(spread_kernel, outs, hot, x, flops=2 * hot.size * x.shape[1])[0]


def exchange(rows, experts):
    width = rows.shape[1]
    pieces = rows.reshape(experts, -1, width)
    arrived = lax.all_to_all(pieces, "expert", split_axis=0, concat_axis=0, tiled=True)
    return arrived.reshape(-1, width)


def combine_kernel(first, hot_ref, back_ref, g_ref, out_ref):
    width = out_ref.shape[1]
    summed = dot(hot_ref[...], back_ref[...], 0, 0)
    out_ref[...] = (g_ref[:, first : first + width].astype(f32) + summed).astype(bf16)


def arrange(plane, capacity, groups, refs, out_ref):
    refs = list(refs)
    for first, layout in groups:
        if layout is None:
            piece = refs.pop(0)
            out_ref[:, first : first + piece.shape[1]] = piece[...]
            continue
        for offsets in layout:
            piece = refs.pop(0)
            lanes = slice(first, first + piece.shape[1])
            for s, offset in enumerate(offsets):
                at = pl.multiple_of(other_of(plane, offset) * capacity, 16)
                out_ref[pl.ds(at, capacity), lanes] = piece[s * capacity : (s + 1) * capacity, :]


def gelu_parts(preact):
    cdf = 0.5 * (1.0 + lax.erf(preact * half_root))
    pdf = density_scale * jnp.exp(-0.5 * preact * preact)
    return preact * cdf, cdf + preact * pdf


def preact_kernel(plane, capacity, groups, win_ref, *refs):
    x_ref, hid_ref, slope_ref = refs[-3:]
    arrange(plane, capacity, groups, refs[:-3], x_ref)
    activated, slope = gelu_parts(dot(x_ref[...], win_ref[...], 1, 1))
    hid_ref[...] = activated.astype(bf16)
    slope_ref[...] = slope


def first_kernel(plane, capacity, groups, plans, win_ref, wout_ref, hid_ref, slope_ref, prob_ref, *refs):
    refs, back = refs[:-1], refs[-1]
    pieces = sum(1 if plan is None else len(plan) for plan in plans)
    refs, back_refs = refs[:-pieces], list(refs[-pieces:])
    g_ref, gp_ref, score_ref = refs[-3:]
    arrange(plane, capacity, groups, refs[:-3], g_ref)
    pulled = dot(g_ref[...], wout_ref[...], 1, 1)
    grad_pre = (prob_ref[:, 0:1] * pulled * slope_ref[...]).astype(bf16)
    gp_ref[...] = grad_pre
    width = back.shape[1]
    for h, plan in enumerate(plans):
        back[...] = dot(grad_pre, win_ref[:, h * width : (h + 1) * width], 1, 0).astype(bf16)
        if plan is None:
            back_refs.pop(0)[...] = back[...]
            continue
        for blocks in plan:
            out_ref = back_refs.pop(0)
            for s, block in enumerate(blocks):
                at = pl.multiple_of(other_of(plane, block) * capacity, 16)
                out_ref[s * capacity : (s + 1) * capacity, :] = back[pl.ds(at, capacity), :]
    score = jnp.sum(hid_ref[...].astype(f32) * pulled, axis=1, keepdims=True)
    score_ref[...] = jnp.broadcast_to(score, score_ref.shape)


def weighted(prob_ref, k, g):
    return (prob_ref[:, k : k + 1] * g.astype(f32)).astype(bf16)


def early_kernel(plane, capacity, groups, wout_ref, hid0_ref, hid1_ref, prob_ref, g0_ref, *refs):
    g_ref, pulled_ref, gout_ref = refs[-3:]
    arrange(plane, capacity, groups, refs[:-3], g_ref)
    pulled_ref[...] = dot(g_ref[...], wout_ref[...], 1, 1)
    y = jnp.concatenate([weighted(prob_ref, 0, g0_ref[...]), weighted(prob_ref, 1, g_ref[...])], axis=0)
    hid = jnp.concatenate([hid0_ref[...], hid1_ref[...]], axis=0)
    gout_ref[...] = dot(hid, y, 0, 0).astype(bf16)


def early(plane, capacity, groups, w_out, hid0, hid1, prob, g0, *pieces):
    rows, units = hid0.shape
    features = w_out.shape[1]
    width = features // HALVES
    args = (w_out, hid0, hid1, prob, g0, *pieces)
    outs = [shaped((rows, width), bf16), shaped((rows, units), f32), shaped((units, features), bf16)]
    whole = lambda a: pl.BlockSpec(a.shape, lambda i: (0, 0))
    first = lambda a: pl.BlockSpec((a.shape[0], width), lambda i: (0, 0))
    return pl.pallas_call(
        functools.partial(early_kernel, plane, capacity, groups),
        grid=(1,),
        out_shape=outs,
        in_specs=[first(w_out), whole(hid0), whole(hid1), whole(prob), first(g0)] + [whole(p) for p in pieces],
        out_specs=[whole(outs[0]), whole(outs[1]), first(outs[2])],
        compiler_params=pltpu.CompilerParams(vmem_limit_bytes=VMEM_LIMIT),
        cost_estimate=cost(args, outs, 3 * units * rows * features),
    )(*args)


def second_kernel(plane, capacity, groups, first, wout_ref, hid_ref, slope_ref, prob_ref, score0_ref, pulled_ref, *refs):
    g_ref, gp_ref, score_ref = refs[-3:]
    arrange(plane, capacity, groups, refs[:-3], g_ref)
    pulled = pulled_ref[...] + dot(g_ref[...], wout_ref[:, first:], 1, 1)
    score = jnp.sum(hid_ref[...].astype(f32) * pulled, axis=1, keepdims=True)
    lane = lax.broadcasted_iota(jnp.int32, score_ref.shape, 1)
    both = jnp.where(lane == 0, score0_ref[...], jnp.where(lane == 1, score, 0.0))
    score_ref[...] = both.astype(bf16)
    gp_ref[...] = (prob_ref[:, 1:2] * pulled * slope_ref[...]).astype(bf16)


def late_kernel(done_ref, prob_ref, x0_ref, x1_ref, g0_ref, g1_ref, hid0_ref, hid1_ref, gp0_ref, gp1_ref, *refs):
    gin_ref, gout_ref, hid, gp = refs
    rows = hid0_ref.shape[0]

    @pl.when(pl.program_id(0) == 0)
    def _():
        hid[:rows, :] = hid0_ref[...]
        hid[rows:, :] = hid1_ref[...]
        gp[:rows, :] = gp0_ref[...]
        gp[rows:, :] = gp1_ref[...]

    gin_ref[...] = dot(gp[...], jnp.concatenate([x0_ref[...], x1_ref[...]], axis=0), 0, 0).astype(bf16)
    y = jnp.concatenate([weighted(prob_ref, 0, g0_ref[...]), weighted(prob_ref, 1, g1_ref[...])], axis=0)
    gout_ref[...] = dot(hid[...], y, 0, 0).astype(bf16)


def late(steps, done, prob, x0, x1, g0, g1, hid0, hid1, gp0, gp1):
    args = (done, prob, x0, x1, g0, g1, hid0, hid1, gp0, gp1)
    rows, units = hid0.shape
    features, part = x0.shape[1], g1.shape[1]
    outs = [shaped((units, features), bf16)] * 2
    skip = (features - part) // (part // steps)
    tile = lambda n, width, at: pl.BlockSpec((n, width // steps), lambda i: (0, at + i))
    whole = lambda a: pl.BlockSpec(a.shape, lambda i: (0, 0))
    return pl.pallas_call(
        late_kernel,
        grid=(steps,),
        out_shape=outs,
        in_specs=[pl.BlockSpec(memory_space=pl.ANY), whole(prob)]
        + [tile(rows, features, 0)] * 2
        + [tile(rows, part, skip), tile(rows, part, 0)]
        + [whole(hid0)] * 4,
        out_specs=[tile(units, features, 0), tile(units, part, skip)],
        scratch_shapes=[pltpu.VMEM((2 * rows, units), bf16)] * 2,
        input_output_aliases={0: 1},
        compiler_params=pltpu.CompilerParams(vmem_limit_bytes=VMEM_LIMIT),
        cost_estimate=cost(args, outs, 6 * units * rows * features),
    )(*args)


def collect_kernel(experts, capacity, topk, meta_ref, hot0_ref, hot1_ref, score_ref, out_ref):
    tokens = meta_ref.shape[2]
    rep = expander(experts * capacity, experts, capacity)
    expert = lax.broadcasted_iota(jnp.int32, (experts, tokens), 0).astype(f32)
    own = meta_ref[lax.axis_index("expert")]
    for k, hot_ref in enumerate((hot0_ref, hot1_ref)):
        placed = hot_ref[...].astype(f32) * score_ref[:, k : k + 1].astype(f32)
        by_expert = dot(rep, placed.astype(bf16), 0, 0)
        for j in range(topk):
            i = k * topk + j
            picked = jnp.where(own[i : i + 1, :] == expert, by_expert, 0.0)
            out_ref[i : i + 1, :] = jnp.sum(picked, axis=0, keepdims=True).astype(bf16)


def body(inputs, entering, weight_in, weight_out, gate_probs, expert_ids):
    experts = lax.axis_size("expert")
    segments = lax.axis_size("segment")
    tokens, features = entering.shape[1:]
    ticks, topk = expert_ids.shape[1], expert_ids.shape[3]
    units = weight_in.shape[2]
    capacity = 3 * tokens * topk // (2 * experts)
    rows = experts * capacity
    plane = Plane(experts)
    matmul = 2 * rows * units * features
    half = features // HALVES
    w_in, w_out = weight_in[0, 0], weight_out[0, 0]
    g0 = entering[0]

    x0 = inputs[0, 0]
    expert_ids, gate_probs = behind((expert_ids, gate_probs), [x0])
    ids = jnp.transpose(expert_ids[0], (0, 2, 1)).reshape(ticks * topk, tokens)
    probs = jnp.transpose(gate_probs[0], (0, 2, 1)).reshape(ticks * topk, tokens)
    meta = jnp.concatenate([ids.astype(f32), probs.astype(f32)], axis=0)
    meta = jnp.broadcast_to(meta[None], (experts,) + meta.shape)
    meta = lax.all_to_all(meta, "expert", split_axis=0, concat_axis=0, tiled=True)
    hot0, hot1, prob = call(
        functools.partial(slots_kernel, experts, capacity, topk),
        [shaped((rows, tokens), bf16)] * 2 + [shaped((rows, LANES), f32)],
        meta,
    )

    acts = [shaped((rows, features), bf16), shaped((rows, units), bf16), shaped((rows, units), f32)]
    stepped = capacity % 16 == 0
    ranks = [list(range(k * topk, (k + 1) * topk)) for k in range(ticks)]
    pick = functools.partial(picked_rows, plane, capacity)
    if stepped:
        x0, x0_layout = sent_rows(plane, 1, pick(ranks[0], 1, x0, meta))
        g0_in, g0_layout = sent_rows(plane, 0, pick(ranks[0], 0, g0, meta))
        x1 = behind(inputs, [x0[1], g0_in[1]])[0, 1]
        x1 = pick(ranks[1], 2, x1, meta)
        plans = [return_plan(plane, ranks[0], axis) for axis in AXES]
        plans += [gather_plan(plane, ranks[1], axis) for axis in AXES]
        shapes = [shaped((len(b), len(e) * capacity, tokens), bf16) for _, b, e in plans]
        masks = call(functools.partial(masks_kernel, plane, capacity, plans), shapes, meta)
        back_plans = [[[plane.back(plane.back(t, u)) for u in plane.along(axis)] for t in plane.across(axis)] for axis in AXES]
        shapes = [shaped((len(blocks) * capacity, half), bf16) for plan in back_plans for blocks in plan]
    else:
        x0, x0_layout = [exchange(spread(hot0, x0), experts)], None
        g0_in, g0_layout = [exchange(spread(hot0, g0), experts)], None
        back_plans = [None] * HALVES
        shapes = [shaped((rows, half), bf16)] * HALVES

    x0, hid0, slope0 = call(
        functools.partial(preact_kernel, plane, capacity, [(0, x0_layout)]), acts, w_in, *x0, flops=matmul
    )
    g0_in, gp0, score0, *backs = call(
        functools.partial(first_kernel, plane, capacity, [(0, g0_layout)], back_plans),
        [shaped((rows, features), bf16), shaped((rows, units), bf16), shaped((rows, LANES), f32)] + shapes,
        w_in, w_out, hid0, slope0, prob, *g0_in, flops=2 * matmul,
        scratch=[pltpu.VMEM((rows, half), bf16)],
    )
    leaving, after = [], []
    for h, axis in enumerate(AXES):
        if stepped:
            count = len(plane.across(axis))
            pieces, backs = backs[:count], backs[count:]
            out, parts = returned_rows(plane, capacity, axis, pieces, masks[h], g0, h * half, after)
        else:
            (out,) = call(
                functools.partial(combine_kernel, h * half), [shaped((tokens, half), bf16)],
                hot0, exchange(backs[h], experts), g0, flops=2 * rows * tokens * half,
            )
        leaving.append(out)
        after = [out]

    if stepped:
        x1, x1_layout = sent_rows(plane, 2, behind(x1, leaving))
        x1_groups = [(0, x1_layout)]
    else:
        x1, x1_groups = [exchange(spread(hot1, inputs[0, 1]), experts)], [(0, None)]
    parts, after = [], []
    for h, axis in enumerate(AXES):
        arrived = lax.ppermute(leaving[h], "segment", [(i, i - 1) for i in range(1, segments)])
        arrived = behind(arrived, after)
        if stepped:
            picked = pick(ranks[1], axis, arrived, meta, masks[HALVES + h])
            pieces, layout = sent_rows(plane, axis, picked)
            after = picked
        else:
            pieces, layout = [exchange(spread(hot1, arrived), experts)], None
        parts.append((pieces, [(0, layout)]))
    x1 = behind(x1, after)
    x1, hid1, slope1 = call(
        functools.partial(preact_kernel, plane, capacity, x1_groups), acts, w_in, *x1, flops=matmul
    )
    part, pulled, gout = early(plane, capacity, parts[0][1], w_out, hid0, hid1, prob, g0_in, *parts[0][0])
    pieces = behind(parts[1][0], [pulled])
    g1, gp1, scores = call(
        functools.partial(second_kernel, plane, capacity, parts[1][1], half),
        [shaped((rows, half), bf16), shaped((rows, units), bf16), shaped((rows, LANES), bf16)],
        w_out, hid1, slope1, prob, score0, pulled, *pieces, flops=matmul // 2,
    )
    scores = exchange(scores, experts)
    grad_in, grad_out = late(4, gout, prob, x0, x1, g0_in, g1, hid0, hid1, gp0, gp1)
    (prob_grads,) = call(
        functools.partial(collect_kernel, experts, capacity, topk),
        [shaped((ticks * topk, tokens), bf16)], meta, hot0, hot1, scores,
    )
    prob_grads = jnp.transpose(prob_grads.reshape(ticks, topk, tokens), (0, 2, 1))
    return grad_in[None, None], grad_out[None, None], prob_grads[None]


def solution(mesh):
    return jax.shard_map(
        body,
        mesh=mesh,
        in_specs=(
            P("segment", None, "expert", None),
            P("segment", "expert", None),
            P("segment", "expert", None, None),
            P("segment", "expert", None, None),
            P("segment", None, "expert", None),
            P("segment", None, "expert", None),
        ),
        out_specs=(
            P("segment", "expert", None, None),
            P("segment", "expert", None, None),
            P("segment", None, "expert", None),
        ),
        check_vma=False,
    )
```

```python
import functools

import jax
import jax.numpy as jnp
from jax import lax
from jax.experimental import pallas as pl
from jax.experimental.pallas import tpu as pltpu
from jax.sharding import PartitionSpec as P

half_root = 0.7071067811865476
density_scale = 0.3989422804014327
LANES = 128
AXES = (2, 2)
HALVES = len(AXES)
TILES = 2
LONG = 10**11
VMEM_LIMIT = 20 * 1024 * 1024
f32 = jnp.float32
bf16 = jnp.bfloat16


def dot(a, b, ca, cb):
    return lax.dot_general(a, b, (((ca,), (cb,)), ((), ())), preferred_element_type=f32)


def shaped(shape, dtype):
    return jax.ShapeDtypeStruct(shape, dtype)


def cost(args, outs, flops):
    size = sum(a.size * a.dtype.itemsize for a in list(args) + list(outs))
    return pl.CostEstimate(flops=flops if flops == LONG else 0, bytes_accessed=0, transcendentals=0)


def call(kernel, outs, *args, flops=0, scratch=()):
    return pl.pallas_call(
        kernel,
        out_shape=outs,
        scratch_shapes=scratch,
        compiler_params=pltpu.CompilerParams(vmem_limit_bytes=VMEM_LIMIT),
        cost_estimate=cost(args, outs, flops),
    )(*args)


class Plane:
    def __init__(self, experts):
        chips = experts // 2
        across = next(n for n in range(int(chips**0.5), 0, -1) if chips % n == 0)
        self.size = (chips // across, across, 2)
        self.experts = experts

    def other(self, i, offset):
        _, across, cores = self.size
        coords = (i // (across * cores), (i // cores) % across, i % cores)
        a, b, c = ((p + o) % n for p, o, n in zip(coords, offset, self.size))
        return (a * across + b) * cores + c

    def back(self, *offsets):
        return tuple(-sum(o) % n for o, n in zip(zip(*offsets), self.size))

    def along(self, axis):
        return [tuple(n if d == axis else 0 for d in range(3)) for n in range(self.size[axis])]

    def across(self, axis):
        spans = [range(1 if d == axis else n) for d, n in enumerate(self.size)]
        return [(a, b, c) for a in spans[0] for b in spans[1] for c in spans[2]]

    def send(self, value, offset):
        if not any(offset):
            return value
        route = [(i, self.other(i, offset)) for i in range(self.experts)]
        return lax.ppermute(value, "expert", route)


def other_of(plane, offset):
    _, across, cores = plane.size
    i = lax.axis_index("expert")
    coords = (lax.div(i, across * cores), lax.rem(lax.div(i, cores), across), lax.rem(i, cores))
    a, b, c = (lax.rem(p + o, n) for p, o, n in zip(coords, offset, plane.size))
    return (a * across + b) * cores + c


def expander(rows, groups, capacity):
    first = lax.broadcasted_iota(jnp.int32, (rows, groups), 1) * capacity
    row = lax.broadcasted_iota(jnp.int32, (rows, groups), 0)
    return ((row >= first) & (row < first + capacity)).astype(f32).astype(bf16)


def slot_masks(named, capacity):
    count = sum(named)
    groups, tokens = count.shape
    rows = groups * capacity
    earlier = lax.broadcasted_iota(jnp.int32, (tokens, tokens), 0)
    later = lax.broadcasted_iota(jnp.int32, (tokens, tokens), 1)
    before = (earlier < later).astype(f32).astype(bf16)
    rank = dot(count.astype(bf16), before, 1, 0)
    place = jnp.where(count > 0, rank, -1.0).astype(bf16)
    rep = expander(rows, groups, capacity)
    spread = dot(rep, place, 1, 0)
    row = lax.broadcasted_iota(jnp.int32, (rows, tokens), 0)
    owner = ((row.astype(f32) + 0.5) * (1.0 / capacity)).astype(jnp.int32)
    position = (row - owner * capacity).astype(f32)
    return (spread == position).astype(f32), rep


def slots_kernel(experts, capacity, topk, meta_ref, hot0_ref, hot1_ref, prob_ref):
    tokens = meta_ref.shape[2]
    me = lax.axis_index("expert")
    expert = lax.broadcasted_iota(jnp.int32, (experts, tokens), 0).astype(f32)
    own = meta_ref[me]
    lane = lax.broadcasted_iota(jnp.int32, prob_ref.shape, 1)
    columns = jnp.zeros(prob_ref.shape, f32)
    ranks = range(topk)
    for k, hot_ref in enumerate((hot0_ref, hot1_ref)):
        at = [k * topk + j for j in ranks]
        hot, _ = slot_masks([(own[i : i + 1, :] == expert).astype(f32) for i in at], capacity)
        hot_ref[...] = hot.astype(bf16)
        mine = me.astype(f32)
        named = [(meta_ref[:, i, :] == mine).astype(f32) for i in at]
        hot, rep = slot_masks(named, capacity)
        probs = sum(n * meta_ref[:, 2 * topk + i, :] for n, i in zip(named, at))
        column = jnp.sum(hot * dot(rep, probs.astype(bf16), 1, 0), axis=1, keepdims=True)
        columns = jnp.where(lane == k, column, columns)
    prob_ref[...] = columns


def block_masks(plane, capacity, ranks, ids, experts):
    tokens = ids.shape[1]
    row = lax.broadcasted_iota(jnp.int32, (len(experts), tokens), 0)
    expert = jnp.zeros(row.shape, f32)
    for i, offset in enumerate(experts):
        expert = jnp.where(row == i, other_of(plane, offset).astype(f32), expert)
    return slot_masks([(ids[i : i + 1, :] == expert).astype(f32) for i in ranks], capacity)[0]


def masks_kernel(plane, capacity, plans, meta_ref, *out_refs):
    for (ranks, blocks, experts), out_ref in zip(plans, out_refs):
        for s, block in enumerate(blocks):
            out_ref[s] = block_masks(
                plane, capacity, ranks, meta_ref[other_of(plane, block)], experts
            ).astype(bf16)


def select_kernel(plane, capacity, plan, meta_ref, *refs):
    ranks, sources, targets = plan
    raw_refs, out_refs = refs[: len(sources)], refs[len(sources) :]
    for s, source in enumerate(sources):
        hot = block_masks(plane, capacity, ranks, meta_ref[other_of(plane, source)], targets)
        picked = dot(hot.astype(bf16), raw_refs[s][...], 1, 0).astype(bf16)
        for i, out_ref in enumerate(out_refs):
            out_ref[s * capacity : (s + 1) * capacity, :] = picked[i * capacity : (i + 1) * capacity]


def own_select_kernel(plane, capacity, plan, *refs):
    ranks, sources, targets = plan
    count = len(sources)
    for s in range(count):
        hot = block_masks(plane, capacity, ranks, refs[s][...], targets)
        picked = dot(hot.astype(bf16), refs[count + s][...], 1, 0).astype(bf16)
        for i, out_ref in enumerate(refs[2 * count :]):
            out_ref[s * capacity : (s + 1) * capacity, :] = picked[i * capacity : (i + 1) * capacity]


def pick_own_kernel(hot_ref, raw_ref, out_ref):
    out_ref[...] = dot(hot_ref[0], raw_ref[...], 1, 0).astype(bf16)


def pick_kernel(capacity, hot_ref, own_ref, *refs):
    sources = hot_ref.shape[0]
    raw_refs, out_refs = refs[: sources - 1], refs[sources - 1 :]
    picked = [own_ref[...]]
    picked += [dot(hot_ref[s + 1], raw_ref[...], 1, 0).astype(bf16) for s, raw_ref in enumerate(raw_refs)]
    for s, rows in enumerate(picked):
        for i, out_ref in enumerate(out_refs):
            out_ref[s * capacity : (s + 1) * capacity, :] = rows[i * capacity : (i + 1) * capacity]


def gather_plan(plane, ranks, axis):
    return ranks, [plane.back(u) for u in plane.along(axis)], plane.across(axis)


def return_plan(plane, ranks, axis):
    return ranks, plane.along(axis), [plane.back(t) for t in plane.across(axis)]


def picked_rows(plane, capacity, ranks, axis, value, meta, hot=None):
    tokens, width = value.shape
    plan = gather_plan(plane, ranks, axis)
    raws = [plane.send(value, u) for u in plane.along(axis)]
    outs = [shaped((len(plan[1]) * capacity, width), bf16)] * len(plan[2])
    flops = 2 * tokens * width * capacity * len(plan[1]) * len(plan[2])
    if type(meta) is list:
        return call(functools.partial(own_select_kernel, plane, capacity, plan), outs, *meta, *raws, flops=flops)
    if hot is None:
        return call(functools.partial(select_kernel, plane, capacity, plan), outs, meta, *raws, flops=flops)
    (own,) = call(pick_own_kernel, [shaped((hot.shape[1], width), bf16)], hot, raws[0], flops=LONG)
    return call(functools.partial(pick_kernel, capacity), outs, hot, own, *raws[1:], flops=flops)


def sent_rows(plane, axis, picked):
    return [plane.send(p, t) for p, t in zip(picked, plane.across(axis))], sent_layout(plane, axis)


def sent_layout(plane, axis):
    return [[plane.back(t, u) for u in plane.along(axis)] for t in plane.across(axis)]


def combine_parts_kernel(capacity, blocks, hot_ref, *refs):
    pieces, out_refs = refs[:-blocks], refs[-blocks:]
    for s, out_ref in enumerate(out_refs):
        rows = jnp.concatenate([p[s * capacity : (s + 1) * capacity, :] for p in pieces], axis=0)
        out_ref[...] = dot(hot_ref[s], rows, 0, 0).astype(out_ref.dtype)


def seed_kernel(first, g_ref, own_ref, out_ref):
    width = out_ref.shape[1]
    out_ref[...] = g_ref[:, first : first + width].astype(f32) + own_ref[...]


def add_kernel(own_ref, *refs):
    out_ref = refs[-1]
    total = own_ref[...]
    for ref in refs[:-1]:
        total = total + ref[...].astype(f32)
    out_ref[...] = total.astype(bf16)


def returned_rows(plane, capacity, axis, pieces, hot, g, first, after):
    width, tokens = pieces[0].shape[1], g.shape[0]
    pieces = [plane.send(p, t) for p, t in zip(pieces, plane.across(axis))]
    pieces = behind(pieces, after)
    along = plane.along(axis)
    outs = [shaped((tokens, width), bf16 if any(u) else f32) for u in along]
    own, *parts = call(
        functools.partial(combine_parts_kernel, capacity, len(along)), outs, hot, *pieces,
        flops=2 * hot.size * width,
    )
    sent = [plane.send(p, u) for p, u in zip(parts, along[1:])]
    (own,) = call(functools.partial(seed_kernel, first), [shaped((tokens, width), f32)], g, own, flops=LONG)
    return call(add_kernel, [shaped((tokens, width), bf16)], own, *sent)[0], parts


def behind(values, after):
    return lax.optimization_barrier((values, after))[0] if after else values


def spread_kernel(hot_ref, x_ref, out_ref):
    out_ref[...] = dot(hot_ref[...], x_ref[...], 1, 0).astype(bf16)


def spread(hot, x):
    outs = [shaped((hot.shape[0], x.shape[1]), bf16)]
    return call(spread_kernel, outs, hot, x, flops=2 * hot.size * x.shape[1])[0]


def exchange(rows, experts):
    width = rows.shape[1]
    pieces = rows.reshape(experts, -1, width)
    arrived = lax.all_to_all(pieces, "expert", split_axis=0, concat_axis=0, tiled=True)
    return arrived.reshape(-1, width)


def combine_kernel(first, hot_ref, back_ref, g_ref, out_ref):
    width = out_ref.shape[1]
    summed = dot(hot_ref[...], back_ref[...], 0, 0)
    out_ref[...] = (g_ref[:, first : first + width].astype(f32) + summed).astype(bf16)


def arrange(plane, capacity, groups, refs, out_ref):
    refs = list(refs)
    for first, layout in groups:
        if layout is None:
            piece = refs.pop(0)
            out_ref[:, first : first + piece.shape[1]] = piece[...]
            continue
        for offsets in layout:
            piece = refs.pop(0)
            lanes = slice(first, first + piece.shape[1])
            for s, offset in enumerate(offsets):
                at = pl.multiple_of(other_of(plane, offset) * capacity, 16)
                out_ref[pl.ds(at, capacity), lanes] = piece[s * capacity : (s + 1) * capacity, :]


def gelu_parts(preact):
    cdf = 0.5 * (1.0 + lax.erf(preact * half_root))
    pdf = density_scale * jnp.exp(-0.5 * preact * preact)
    return preact * cdf, cdf + preact * pdf


def preact_kernel(plane, capacity, groups, win_ref, *refs):
    x_ref, hid_ref, slope_ref = refs[-3:]
    arrange(plane, capacity, groups, refs[:-3], x_ref)
    activated, slope = gelu_parts(dot(x_ref[...], win_ref[...], 1, 1))
    hid_ref[...] = activated.astype(bf16)
    slope_ref[...] = slope


def first_kernel(plane, capacity, groups, plans, win_ref, wout_ref, hid_ref, slope_ref, prob_ref, *refs):
    refs, back = refs[:-1], refs[-1]
    pieces = sum(1 if plan is None else len(plan) for plan in plans)
    refs, back_refs = refs[:-pieces], list(refs[-pieces:])
    g_ref, gp_ref, score_ref = refs[-3:]
    arrange(plane, capacity, groups, refs[:-3], g_ref)
    pulled = dot(g_ref[...], wout_ref[...], 1, 1)
    grad_pre = (prob_ref[:, 0:1] * pulled * slope_ref[...]).astype(bf16)
    gp_ref[...] = grad_pre
    width = back.shape[1]
    for h, plan in enumerate(plans):
        back[...] = dot(grad_pre, win_ref[:, h * width : (h + 1) * width], 1, 0).astype(bf16)
        if plan is None:
            back_refs.pop(0)[...] = back[...]
            continue
        for blocks in plan:
            out_ref = back_refs.pop(0)
            for s, block in enumerate(blocks):
                at = pl.multiple_of(other_of(plane, block) * capacity, 16)
                out_ref[s * capacity : (s + 1) * capacity, :] = back[pl.ds(at, capacity), :]
    score = jnp.sum(hid_ref[...].astype(f32) * pulled, axis=1, keepdims=True)
    score_ref[...] = jnp.broadcast_to(score, score_ref.shape)


def weighted(prob_ref, k, g):
    return (prob_ref[:, k : k + 1] * g.astype(f32)).astype(bf16)


def early_kernel(plane, capacity, groups, wout_ref, hid0_ref, hid1_ref, prob_ref, g0_ref, *refs):
    pulled_ref, gout_ref, g_ref = refs[-3:]
    arrange(plane, capacity, groups, refs[:-3], g_ref)
    pulled_ref[...] = dot(g_ref[...], wout_ref[...], 1, 1)
    y = jnp.concatenate([weighted(prob_ref, 0, g0_ref[...]), weighted(prob_ref, 1, g_ref[...])], axis=0)
    hid = jnp.concatenate([hid0_ref[...], hid1_ref[...]], axis=0)
    gout_ref[...] = dot(hid, y, 0, 0).astype(bf16)


def early(plane, capacity, groups, w_out, hid0, hid1, prob, g0, *pieces):
    rows, units = hid0.shape
    features = w_out.shape[1]
    width = features // HALVES
    args = (w_out, hid0, hid1, prob, g0, *pieces)
    outs = [shaped((rows, units), f32), shaped((units, features), bf16)]
    whole = lambda a: pl.BlockSpec(a.shape, lambda i: (0, 0))
    first = lambda a: pl.BlockSpec((a.shape[0], width), lambda i: (0, 0))
    return pl.pallas_call(
        functools.partial(early_kernel, plane, capacity, groups),
        grid=(1,),
        out_shape=outs,
        in_specs=[first(w_out), whole(hid0), whole(hid1), whole(prob), first(g0)] + [whole(p) for p in pieces],
        out_specs=[whole(outs[0]), first(outs[1])],
        scratch_shapes=[pltpu.VMEM((rows, width), bf16)],
        compiler_params=pltpu.CompilerParams(vmem_limit_bytes=VMEM_LIMIT),
        cost_estimate=cost(args, outs, 3 * units * rows * features),
    )(*args)


def second_kernel(plane, capacity, groups, first, wout_ref, hid_ref, slope_ref, prob_ref, score0_ref, pulled_ref, *refs):
    g_ref, gp_ref, score_ref = refs[-3:]
    arrange(plane, capacity, groups, refs[:-3], g_ref)
    pulled = pulled_ref[...] + dot(g_ref[...], wout_ref[:, first:], 1, 1)
    score = jnp.sum(hid_ref[...].astype(f32) * pulled, axis=1, keepdims=True)
    lane = lax.broadcasted_iota(jnp.int32, score_ref.shape, 1)
    both = jnp.where(lane == 0, score0_ref[...], jnp.where(lane == 1, score, 0.0))
    score_ref[...] = both.astype(bf16)
    gp_ref[...] = (prob_ref[:, 1:2] * pulled * slope_ref[...]).astype(bf16)


def late_kernel(width, _, prob_ref, x0_ref, x1_ref, g0_ref, g1_ref, hid0_ref, hid1_ref, gp0_ref, gp1_ref, *refs):
    gin_ref, gout_ref, prob, x, g, hid, gp, held, sem, out_sem = refs
    rows, units = hid0_ref.shape
    features, part = x0_ref.shape[1], g1_ref.shape[1]
    skip = features - part
    fetched = []

    def fetch(ref, out_ref):
        fetched.append(pltpu.make_async_copy(ref, out_ref, sem.at[len(fetched)]))
        fetched[-1].start()
        return fetched[-1]

    top, low = pl.ds(0, rows), pl.ds(rows, rows)
    lanes = lambda at: pl.ds(at, width)
    first = [fetch(gp0_ref, gp.at[top, :]), fetch(gp1_ref, gp.at[low, :])]
    tiles = []
    for at in range(0, features, width):
        tiles.append(
            [fetch(x0_ref.at[:, lanes(at)], x.at[top, lanes(at)]), fetch(x1_ref.at[:, lanes(at)], x.at[low, lanes(at)])]
        )
    then = [fetch(hid0_ref, hid.at[top, :]), fetch(hid1_ref, hid.at[low, :]), fetch(prob_ref, prob)]
    then += [fetch(g0_ref.at[:, pl.ds(skip, part)], g.at[top, :]), fetch(g1_ref, g.at[low, :])]
    sent = []

    def store(n, value, out_ref, at):
        slot = n % held.shape[0]
        if n >= held.shape[0]:
            sent[n - held.shape[0]].wait()
        held[slot] = value.astype(bf16)
        sent.append(pltpu.make_async_copy(held.at[slot], out_ref.at[:, lanes(at)], out_sem.at[slot]))
        sent[-1].start()

    for copy in first:
        copy.wait()
    for n, tile in enumerate(tiles):
        for copy in tile:
            copy.wait()
        at = n * width
        store(n, dot(gp[...], x[:, at : at + width], 0, 0), gin_ref, at)
    for copy in then:
        copy.wait()
    for n in range(part // width):
        at = n * width
        y0 = weighted(prob, 0, g[:rows, at : at + width])
        y1 = weighted(prob, 1, g[rows:, at : at + width])
        store(len(tiles) + n, dot(hid[...], jnp.concatenate([y0, y1], axis=0), 0, 0), gout_ref, skip + at)
    for copy in sent[-held.shape[0] :]:
        copy.wait()


def late(width, done, prob, x0, x1, g0, g1, hid0, hid1, gp0, gp1):
    args = (done, prob, x0, x1, g0, g1, hid0, hid1, gp0, gp1)
    rows, units = hid0.shape
    features, part = x0.shape[1], g1.shape[1]
    outs = [shaped((units, features), bf16)] * 2
    fetches = 7 + 2 * (features // width)
    return pl.pallas_call(
        functools.partial(late_kernel, width),
        out_shape=outs,
        in_specs=[pl.BlockSpec(memory_space=pltpu.HBM)] * len(args),
        out_specs=[pl.BlockSpec(memory_space=pltpu.HBM)] * 2,
        scratch_shapes=[pltpu.VMEM(prob.shape, f32), pltpu.VMEM((2 * rows, features), bf16)]
        + [pltpu.VMEM((2 * rows, part), bf16)]
        + [pltpu.VMEM((2 * rows, units), bf16)] * 2
        + [pltpu.VMEM((3, units, width), bf16)]
        + [pltpu.SemaphoreType.DMA((fetches,)), pltpu.SemaphoreType.DMA((3,))],
        input_output_aliases={0: 1},
        compiler_params=pltpu.CompilerParams(vmem_limit_bytes=60 * 1024 * 1024),
        cost_estimate=cost(args, outs, 6 * units * rows * features),
    )(*args)


def collect_kernel(experts, capacity, topk, meta_ref, hot0_ref, hot1_ref, score_ref, out_ref):
    tokens = meta_ref.shape[2]
    rep = expander(experts * capacity, experts, capacity)
    expert = lax.broadcasted_iota(jnp.int32, (experts, tokens), 0).astype(f32)
    own = meta_ref[lax.axis_index("expert")]
    for k, hot_ref in enumerate((hot0_ref, hot1_ref)):
        placed = hot_ref[...].astype(f32) * score_ref[:, k : k + 1].astype(f32)
        by_expert = dot(rep, placed.astype(bf16), 0, 0)
        for j in range(topk):
            i = k * topk + j
            picked = jnp.where(own[i : i + 1, :] == expert, by_expert, 0.0)
            out_ref[i : i + 1, :] = jnp.sum(picked, axis=0, keepdims=True).astype(bf16)


def body(inputs, entering, weight_in, weight_out, gate_probs, expert_ids):
    experts = lax.axis_size("expert")
    segments = lax.axis_size("segment")
    tokens, features = entering.shape[1:]
    ticks, topk = expert_ids.shape[1], expert_ids.shape[3]
    units = weight_in.shape[2]
    capacity = 3 * tokens * topk // (2 * experts)
    rows = experts * capacity
    plane = Plane(experts)
    matmul = 2 * rows * units * features
    half = features // HALVES
    w_in, w_out = weight_in[0, 0], weight_out[0, 0]
    g0 = entering[0]

    x0 = inputs[0, 0]
    expert_ids, gate_probs = behind((expert_ids, gate_probs), [x0])
    ids = jnp.transpose(expert_ids[0], (0, 2, 1)).reshape(ticks * topk, tokens)
    probs = jnp.transpose(gate_probs[0], (0, 2, 1)).reshape(ticks * topk, tokens)
    meta = jnp.concatenate([ids.astype(f32), probs.astype(f32)], axis=0)
    own_meta = meta
    meta = jnp.broadcast_to(meta[None], (experts,) + meta.shape)
    meta = lax.all_to_all(meta, "expert", split_axis=0, concat_axis=0, tiled=True)
    hot0, hot1, prob = call(
        functools.partial(slots_kernel, experts, capacity, topk),
        [shaped((rows, tokens), bf16)] * 2 + [shaped((rows, LANES), f32)],
        meta,
    )

    acts = [shaped((rows, features), bf16), shaped((rows, units), bf16), shaped((rows, units), f32)]
    stepped = capacity % 16 == 0
    ranks = [list(range(k * topk, (k + 1) * topk)) for k in range(ticks)]
    pick = functools.partial(picked_rows, plane, capacity)
    if stepped:
        metas = [own_meta, plane.send(own_meta, (0, 0, 1))]
        x1 = behind(inputs, [x0])[0, 1]
        x1 = pick(ranks[1], 2, x1, metas)
        x1_near, _ = sent_rows(plane, 2, x1[:-1])
        x1_groups, x1_rest = [(0, sent_layout(plane, 2))], x1[-1:]
        select_meta = behind(meta, x1)
        x0, x0_layout = sent_rows(plane, 1, pick(ranks[0], 1, x0, select_meta))
        g0_in, g0_layout = sent_rows(plane, 0, pick(ranks[0], 0, g0, select_meta))
        plans = [return_plan(plane, ranks[0], axis) for axis in AXES]
        plans += [gather_plan(plane, ranks[1], axis) for axis in AXES]
        shapes = [shaped((len(b), len(e) * capacity, tokens), bf16) for _, b, e in plans]
        masks = call(functools.partial(masks_kernel, plane, capacity, plans), shapes, meta)
        back_plans = [[[plane.back(plane.back(t, u)) for u in plane.along(axis)] for t in plane.across(axis)] for axis in AXES]
        shapes = [shaped((len(blocks) * capacity, half), bf16) for plan in back_plans for blocks in plan]
    else:
        x0, x0_layout = [exchange(spread(hot0, x0), experts)], None
        g0_in, g0_layout = [exchange(spread(hot0, g0), experts)], None
        back_plans = [None] * HALVES
        shapes = [shaped((rows, half), bf16)] * HALVES

    if stepped:
        x0 = behind(x0, x1_near)
    x0, hid0, slope0 = call(
        functools.partial(preact_kernel, plane, capacity, [(0, x0_layout)]), acts, w_in, *x0, flops=matmul
    )
    g0_in, gp0, score0, *backs = call(
        functools.partial(first_kernel, plane, capacity, [(0, g0_layout)], back_plans),
        [shaped((rows, features), bf16), shaped((rows, units), bf16), shaped((rows, LANES), f32)] + shapes,
        w_in, w_out, hid0, slope0, prob, *g0_in, flops=2 * matmul,
        scratch=[pltpu.VMEM((rows, half), bf16)],
    )
    leaving, after = [], []
    for h, axis in enumerate(AXES):
        if stepped:
            count = len(plane.across(axis))
            pieces, backs = backs[:count], backs[count:]
            out, parts = returned_rows(plane, capacity, axis, pieces, masks[h], g0, h * half, after)
        else:
            (out,) = call(
                functools.partial(combine_kernel, h * half), [shaped((tokens, half), bf16)],
                hot0, exchange(backs[h], experts), g0, flops=2 * rows * tokens * half,
            )
        leaving.append(out)
        after = [out]

    if stepped:
        x1_rest = [plane.send(p, t) for p, t in zip(behind(x1_rest, leaving), plane.across(2)[-1:])]
        x1 = x1_near + x1_rest
    else:
        x1, x1_groups = [exchange(spread(hot1, inputs[0, 1]), experts)], [(0, None)]
    parts, after = [], []
    for h, axis in enumerate(AXES):
        arrived = lax.ppermute(leaving[h], "segment", [(i, i - 1) for i in range(1, segments)])
        arrived = behind(arrived, after)
        if stepped:
            picked = pick(ranks[1], axis, arrived, meta, masks[HALVES + h])
            pieces, layout = sent_rows(plane, axis, picked)
            after = picked
        else:
            pieces, layout = [exchange(spread(hot1, arrived), experts)], None
        parts.append((pieces, [(0, layout)]))
    x1 = behind(x1, after)
    x1, hid1, slope1 = call(
        functools.partial(preact_kernel, plane, capacity, x1_groups), acts, w_in, *x1, flops=matmul
    )
    pulled, gout = early(plane, capacity, parts[0][1], w_out, hid0, hid1, prob, g0_in, *parts[0][0])
    pieces = behind(parts[1][0], [pulled])
    g1, gp1, scores = call(
        functools.partial(second_kernel, plane, capacity, parts[1][1], half),
        [shaped((rows, half), bf16), shaped((rows, units), bf16), shaped((rows, LANES), bf16)],
        w_out, hid1, slope1, prob, score0, pulled, *pieces, flops=matmul // 2,
    )
    scores = exchange(scores, experts)
    grad_in, grad_out = late(features // TILES, gout, prob, x0, x1, g0_in, g1, hid0, hid1, gp0, gp1)
    (prob_grads,) = call(
        functools.partial(collect_kernel, experts, capacity, topk),
        [shaped((ticks * topk, tokens), bf16)], meta, hot0, hot1, scores,
    )
    prob_grads = jnp.transpose(prob_grads.reshape(ticks, topk, tokens), (0, 2, 1))
    return grad_in[None, None], grad_out[None, None], prob_grads[None]


def solution(mesh):
    return jax.shard_map(
        body,
        mesh=mesh,
        in_specs=(
            P("segment", None, "expert", None),
            P("segment", "expert", None),
            P("segment", "expert", None, None),
            P("segment", "expert", None, None),
            P("segment", None, "expert", None),
            P("segment", None, "expert", None),
        ),
        out_specs=(
            P("segment", "expert", None, None),
            P("segment", "expert", None, None),
            P("segment", None, "expert", None),
        ),
        check_vma=False,
    )
```

```python
import functools

import jax
import jax.numpy as jnp
from jax import lax
from jax.experimental import pallas as pl
from jax.experimental.pallas import tpu as pltpu
from jax.sharding import PartitionSpec as P

half_root = 0.7071067811865476
density_scale = 0.3989422804014327
LANES = 128
AXES = (2, 2)
HALVES = len(AXES)
TILES = 2
LONG = 10**11
LATE_LIMIT = 32 * 1024 * 1024
X0, G0, X1, G1, HID0, HID1, GP0, GP1, COLS = range(9)
PAD_BYTES = 66 * 1024 * 1024
VMEM_LIMIT = 20 * 1024 * 1024
f32 = jnp.float32
bf16 = jnp.bfloat16


def dot(a, b, ca, cb):
    return lax.dot_general(a, b, (((ca,), (cb,)), ((), ())), preferred_element_type=f32)


def shaped(shape, dtype):
    return jax.ShapeDtypeStruct(shape, dtype)


def cost(args, outs, flops):
    size = sum(a.size * a.dtype.itemsize for a in list(args) + list(outs))
    return pl.CostEstimate(flops=flops if flops == LONG else 0, bytes_accessed=size * 64, transcendentals=0)


def in_hbm(ref):
    return pl.BlockSpec(memory_space=pltpu.HBM)


def call(kernel, outs, *args, flops=0, scratch=(), pad=None, pad_out=False):
    specs = [pl.BlockSpec() if n != pad else in_hbm(a) for n, a in enumerate(args)]
    return pl.pallas_call(
        kernel,
        out_shape=outs,
        in_specs=specs,
        out_specs=[in_hbm(o) if pad_out and n == 0 else pl.BlockSpec() for n, o in enumerate(outs)],
        input_output_aliases={pad: 0} if pad is not None and pad_out else {},
        scratch_shapes=scratch,
        compiler_params=pltpu.CompilerParams(vmem_limit_bytes=VMEM_LIMIT),
        cost_estimate=cost(args, outs, flops),
    )(*args)


class Plane:
    def __init__(self, experts):
        chips = experts // 2
        across = next(n for n in range(int(chips**0.5), 0, -1) if chips % n == 0)
        self.size = (chips // across, across, 2)
        self.experts = experts

    def other(self, i, offset):
        _, across, cores = self.size
        coords = (i // (across * cores), (i // cores) % across, i % cores)
        a, b, c = ((p + o) % n for p, o, n in zip(coords, offset, self.size))
        return (a * across + b) * cores + c

    def back(self, *offsets):
        return tuple(-sum(o) % n for o, n in zip(zip(*offsets), self.size))

    def along(self, axis):
        return [tuple(n if d == axis else 0 for d in range(3)) for n in range(self.size[axis])]

    def across(self, axis):
        spans = [range(1 if d == axis else n) for d, n in enumerate(self.size)]
        return [(a, b, c) for a in spans[0] for b in spans[1] for c in spans[2]]

    def send(self, value, offset):
        if not any(offset):
            return value
        route = [(i, self.other(i, offset)) for i in range(self.experts)]
        return lax.ppermute(value, "expert", route)


def other_of(plane, offset):
    _, across, cores = plane.size
    i = lax.axis_index("expert")
    coords = (lax.div(i, across * cores), lax.rem(lax.div(i, cores), across), lax.rem(i, cores))
    a, b, c = (lax.rem(p + o, n) for p, o, n in zip(coords, offset, plane.size))
    return (a * across + b) * cores + c


def expander(rows, groups, capacity):
    first = lax.broadcasted_iota(jnp.int32, (rows, groups), 1) * capacity
    row = lax.broadcasted_iota(jnp.int32, (rows, groups), 0)
    return ((row >= first) & (row < first + capacity)).astype(f32).astype(bf16)


def slot_masks(named, capacity):
    count = sum(named)
    groups, tokens = count.shape
    rows = groups * capacity
    earlier = lax.broadcasted_iota(jnp.int32, (tokens, tokens), 0)
    later = lax.broadcasted_iota(jnp.int32, (tokens, tokens), 1)
    before = (earlier < later).astype(f32).astype(bf16)
    rank = dot(count.astype(bf16), before, 1, 0)
    place = jnp.where(count > 0, rank, -1.0).astype(bf16)
    rep = expander(rows, groups, capacity)
    spread = dot(rep, place, 1, 0)
    row = lax.broadcasted_iota(jnp.int32, (rows, tokens), 0)
    owner = ((row.astype(f32) + 0.5) * (1.0 / capacity)).astype(jnp.int32)
    position = (row - owner * capacity).astype(f32)
    return (spread == position).astype(f32), rep


def slots_kernel(experts, capacity, topk, meta_ref, hot0_ref, hot1_ref, prob_ref):
    tokens = meta_ref.shape[2]
    me = lax.axis_index("expert")
    expert = lax.broadcasted_iota(jnp.int32, (experts, tokens), 0).astype(f32)
    own = meta_ref[me]
    lane = lax.broadcasted_iota(jnp.int32, prob_ref.shape, 1)
    columns = jnp.zeros(prob_ref.shape, f32)
    ranks = range(topk)
    for k, hot_ref in enumerate((hot0_ref, hot1_ref)):
        at = [k * topk + j for j in ranks]
        hot, _ = slot_masks([(own[i : i + 1, :] == expert).astype(f32) for i in at], capacity)
        hot_ref[...] = hot.astype(bf16)
        mine = me.astype(f32)
        named = [(meta_ref[:, i, :] == mine).astype(f32) for i in at]
        hot, rep = slot_masks(named, capacity)
        probs = sum(n * meta_ref[:, 2 * topk + i, :] for n, i in zip(named, at))
        column = jnp.sum(hot * dot(rep, probs.astype(bf16), 1, 0), axis=1, keepdims=True)
        columns = jnp.where(lane == k, column, columns)
    prob_ref[...] = columns.astype(bf16)


def block_masks(plane, capacity, ranks, ids, experts):
    tokens = ids.shape[1]
    row = lax.broadcasted_iota(jnp.int32, (len(experts), tokens), 0)
    expert = jnp.zeros(row.shape, f32)
    for i, offset in enumerate(experts):
        expert = jnp.where(row == i, other_of(plane, offset).astype(f32), expert)
    return slot_masks([(ids[i : i + 1, :] == expert).astype(f32) for i in ranks], capacity)[0]


def masks_kernel(plane, capacity, plans, meta_ref, *out_refs):
    for (ranks, blocks, experts), out_ref in zip(plans, out_refs):
        for s, block in enumerate(blocks):
            out_ref[s] = block_masks(
                plane, capacity, ranks, meta_ref[other_of(plane, block)], experts
            ).astype(bf16)


def select_kernel(plane, capacity, plan, meta_ref, *refs):
    ranks, sources, targets = plan
    raw_refs, out_refs = refs[: len(sources)], refs[len(sources) :]
    for s, source in enumerate(sources):
        hot = block_masks(plane, capacity, ranks, meta_ref[other_of(plane, source)], targets)
        picked = dot(hot.astype(bf16), raw_refs[s][...], 1, 0).astype(bf16)
        for i, out_ref in enumerate(out_refs):
            out_ref[s * capacity : (s + 1) * capacity, :] = picked[i * capacity : (i + 1) * capacity]


def own_select_kernel(plane, capacity, plan, *refs):
    ranks, sources, targets = plan
    count = len(sources)
    for s in range(count):
        hot = block_masks(plane, capacity, ranks, refs[s][...], targets)
        picked = dot(hot.astype(bf16), refs[count + s][...], 1, 0).astype(bf16)
        for i, out_ref in enumerate(refs[2 * count + 1 :]):
            out_ref[s * capacity : (s + 1) * capacity, :] = picked[i * capacity : (i + 1) * capacity]


def pick_own_kernel(hot_ref, raw_ref, out_ref):
    out_ref[...] = dot(hot_ref[0], raw_ref[...], 1, 0).astype(bf16)


def pick_kernel(capacity, hot_ref, own_ref, *refs):
    sources = hot_ref.shape[0]
    raw_refs, out_refs = refs[: sources - 1], refs[sources - 1 :]
    picked = [own_ref[...]]
    picked += [dot(hot_ref[s + 1], raw_ref[...], 1, 0).astype(bf16) for s, raw_ref in enumerate(raw_refs)]
    for s, rows in enumerate(picked):
        for i, out_ref in enumerate(out_refs):
            out_ref[s * capacity : (s + 1) * capacity, :] = rows[i * capacity : (i + 1) * capacity]


def gather_plan(plane, ranks, axis):
    return ranks, [plane.back(u) for u in plane.along(axis)], plane.across(axis)


def return_plan(plane, ranks, axis):
    return ranks, plane.along(axis), [plane.back(t) for t in plane.across(axis)]


def picked_rows(plane, capacity, ranks, axis, value, meta, hot=None, pad=None):
    tokens, width = value.shape
    plan = gather_plan(plane, ranks, axis)
    raws = [plane.send(value, u) for u in plane.along(axis)]
    outs = [shaped((len(plan[1]) * capacity, width), bf16)] * len(plan[2])
    flops = 2 * tokens * width * capacity * len(plan[1]) * len(plan[2])
    if pad is not None:
        kernel = functools.partial(own_select_kernel, plane, capacity, plan)
        return call(kernel, [pad] + outs, *meta, *raws, pad_out=True)
    if hot is None:
        return call(functools.partial(select_kernel, plane, capacity, plan), outs, meta, *raws, flops=flops)
    (own,) = call(pick_own_kernel, [shaped((hot.shape[1], width), bf16)], hot, raws[0], flops=LONG)
    return call(functools.partial(pick_kernel, capacity), outs, hot, own, *raws[1:], flops=flops)


def sent_rows(plane, axis, picked):
    return [plane.send(p, t) for p, t in zip(picked, plane.across(axis))], sent_layout(plane, axis)


def sent_layout(plane, axis):
    return [[plane.back(t, u) for u in plane.along(axis)] for t in plane.across(axis)]


def combine_parts_kernel(capacity, blocks, hot_ref, *refs):
    pieces, out_refs = refs[:-blocks], refs[-blocks:]
    for s, out_ref in enumerate(out_refs):
        rows = jnp.concatenate([p[s * capacity : (s + 1) * capacity, :] for p in pieces], axis=0)
        out_ref[...] = dot(hot_ref[s], rows, 0, 0).astype(out_ref.dtype)


def seed_kernel(first, g_ref, own_ref, out_ref):
    width = out_ref.shape[1]
    out_ref[...] = g_ref[:, first : first + width].astype(f32) + own_ref[...]


def add_kernel(own_ref, *refs):
    out_ref = refs[-1]
    total = own_ref[...]
    for ref in refs[:-1]:
        total = total + ref[...].astype(f32)
    out_ref[...] = total.astype(bf16)


def returned_rows(plane, capacity, axis, pieces, hot, g, first, after):
    width, tokens = pieces[0].shape[1], g.shape[0]
    pieces = [plane.send(p, t) for p, t in zip(pieces, plane.across(axis))]
    pieces = behind(pieces, after)
    along = plane.along(axis)
    outs = [shaped((tokens, width), bf16 if any(u) else f32) for u in along]
    own, *parts = call(
        functools.partial(combine_parts_kernel, capacity, len(along)), outs, hot, *pieces,
        flops=2 * hot.size * width,
    )
    sent = [plane.send(p, u) for p, u in zip(parts, along[1:])]
    (own,) = call(functools.partial(seed_kernel, first), [shaped((tokens, width), f32)], g, own, flops=LONG)
    return call(add_kernel, [shaped((tokens, width), bf16)], own, *sent)[0], parts


def behind(values, after):
    return lax.optimization_barrier((values, after))[0] if after else values


def spread_kernel(hot_ref, x_ref, out_ref):
    out_ref[...] = dot(hot_ref[...], x_ref[...], 1, 0).astype(bf16)


def spread(hot, x):
    outs = [shaped((hot.shape[0], x.shape[1]), bf16)]
    return call(spread_kernel, outs, hot, x, flops=2 * hot.size * x.shape[1])[0]


def exchange(rows, experts):
    width = rows.shape[1]
    pieces = rows.reshape(experts, -1, width)
    arrived = lax.all_to_all(pieces, "expert", split_axis=0, concat_axis=0, tiled=True)
    return arrived.reshape(-1, width)


def combine_kernel(first, hot_ref, back_ref, g_ref, out_ref):
    width = out_ref.shape[1]
    summed = dot(hot_ref[...], back_ref[...], 0, 0)
    out_ref[...] = (g_ref[:, first : first + width].astype(f32) + summed).astype(bf16)


def arrange(plane, capacity, groups, refs, out_ref):
    refs = list(refs)
    for first, layout in groups:
        if layout is None:
            piece = refs.pop(0)
            out_ref[:, first : first + piece.shape[1]] = piece[...]
            continue
        for offsets in layout:
            piece = refs.pop(0)
            lanes = slice(first, first + piece.shape[1])
            for s, offset in enumerate(offsets):
                at = pl.multiple_of(other_of(plane, offset) * capacity, 16)
                out_ref[pl.ds(at, capacity), lanes] = piece[s * capacity : (s + 1) * capacity, :]


def gelu_parts(preact):
    cdf = 0.5 * (1.0 + lax.erf(preact * half_root))
    pdf = density_scale * jnp.exp(-0.5 * preact * preact)
    return preact * cdf, cdf + preact * pdf


class Copies:
    def __init__(self, sem):
        self.sem, self.started = sem, []

    def start(self, source, target):
        self.started.append(pltpu.make_async_copy(source, target, self.sem.at[len(self.started)]))
        self.started[-1].start()
        return self.started[-1]

    def wait(self):
        for copy in self.started:
            copy.wait()


def lanes_of(units):
    return -(-units // LANES) * LANES


def plate(pad_ref, n, lanes):
    return pad_ref.at[n, :, pl.ds(0, lanes)]


def preact_kernel(plane, capacity, groups, places, win_ref, _, *refs):
    pad_ref, hid_ref, slope_ref, x, hid, sem = refs[-6:]
    units, copies = win_ref.shape[0], Copies(sem)
    arrange(plane, capacity, groups, refs[:-6], x)
    copies.start(x, pad_ref.at[places[0]])
    activated, slope = gelu_parts(dot(x[...], win_ref[...], 1, 1))
    hidden = activated.astype(bf16)
    hid[:, :units] = hidden
    copies.start(hid, plate(pad_ref, places[1], hid.shape[1]))
    hid_ref[...] = hidden
    slope_ref[...] = slope
    copies.wait()


def preact(plane, capacity, groups, places, w_in, pad, *pieces):
    units = w_in.shape[0]
    rows, features = pad.shape[1:]
    return call(
        functools.partial(preact_kernel, plane, capacity, groups, places),
        [shaped(pad.shape, bf16), shaped((rows, units), bf16), shaped((rows, units), f32)],
        w_in, pad, *pieces, pad=1, pad_out=True,
        scratch=[pltpu.VMEM((rows, n), bf16) for n in (features, lanes_of(units))] + [pltpu.SemaphoreType.DMA((2,))],
    )


def first_preact_kernel(plane, capacity, groups, win_ref, *refs):
    x_ref, hid_ref, slope_ref = refs[-3:]
    arrange(plane, capacity, groups, refs[:-3], x_ref)
    activated, slope = gelu_parts(dot(x_ref[...], win_ref[...], 1, 1))
    hid_ref[:, : slope.shape[1]] = activated.astype(bf16)
    slope_ref[...] = slope


def first_kernel(plane, capacity, groups, plans, win_ref, wout_ref, hid_ref, slope_ref, prob_ref, *refs):
    refs, back = refs[:-1], refs[-1]
    pieces = sum(1 if plan is None else len(plan) for plan in plans)
    refs, back_refs = refs[:-pieces], list(refs[-pieces:])
    g_ref, gp_ref, cols_ref = refs[-3:]
    units = win_ref.shape[0]
    arrange(plane, capacity, groups, refs[:-3], g_ref)
    pulled = dot(g_ref[...], wout_ref[...], 1, 1)
    grad_pre = (prob_ref[:, 0:1].astype(f32) * pulled * slope_ref[...]).astype(bf16)
    gp_ref[:, :units] = grad_pre
    score = jnp.sum(hid_ref[:, :units].astype(f32) * pulled, axis=1, keepdims=True)
    cols_ref[:, :LANES] = prob_ref[...]
    cols_ref[:, LANES:] = jnp.broadcast_to(score, (score.shape[0], LANES)).astype(bf16)
    width = back.shape[1]
    for h, plan in enumerate(plans):
        back[...] = dot(grad_pre, win_ref[:, h * width : (h + 1) * width], 1, 0).astype(bf16)
        if plan is None:
            back_refs.pop(0)[...] = back[...]
            continue
        for blocks in plan:
            out_ref = back_refs.pop(0)
            for s, block in enumerate(blocks):
                at = pl.multiple_of(other_of(plane, block) * capacity, 16)
                out_ref[s * capacity : (s + 1) * capacity, :] = back[pl.ds(at, capacity), :]


def stash_kernel(places, *refs):
    pad_ref, sem = refs[-2:]
    copies = Copies(sem)
    for n, ref in zip(places, refs):
        copies.start(ref, plate(pad_ref, n, ref.shape[1]))
    copies.wait()


def stash(pad, places, *arrays):
    return pl.pallas_call(
        functools.partial(stash_kernel, places),
        out_shape=shaped(pad.shape, bf16),
        in_specs=[pl.BlockSpec()] * len(arrays) + [in_hbm(pad)],
        out_specs=in_hbm(pad),
        compiler_params=pltpu.CompilerParams(vmem_limit_bytes=VMEM_LIMIT),
        scratch_shapes=[pltpu.SemaphoreType.DMA((len(arrays),))],
        input_output_aliases={len(arrays): 0},
        cost_estimate=pl.CostEstimate(flops=0, bytes_accessed=0, transcendentals=0),
    )(*arrays, pad)


def weighted(prob_ref, k, g):
    return (prob_ref[:, k : k + 1].astype(f32) * g.astype(f32)).astype(bf16)


def early_kernel(plane, capacity, groups, wout_ref, hid1_ref, pad_ref, *refs):
    pulled_ref, gout_ref, g, g0, hid0, cols, sem = refs[-7:]
    units, copies = wout_ref.shape[0], Copies(sem)
    copies.start(plate(pad_ref, G0, g0.shape[1]), g0)
    copies.start(plate(pad_ref, HID0, hid0.shape[1]), hid0)
    copies.start(plate(pad_ref, COLS, cols.shape[1]), cols)
    arrange(plane, capacity, groups, refs[:-7], g)
    pulled_ref[...] = dot(g[...], wout_ref[...], 1, 1)
    copies.wait()
    y = jnp.concatenate([weighted(cols, 0, g0[...]), weighted(cols, 1, g[...])], axis=0)
    hid = jnp.concatenate([hid0[:, :units], hid1_ref[...]], axis=0)
    gout_ref[...] = dot(hid, y, 0, 0).astype(bf16)


def early(plane, capacity, groups, w_out, hid1, pad, *pieces):
    rows, units = hid1.shape
    features = w_out.shape[1]
    width = features // HALVES
    args = (w_out, hid1, *pieces)
    outs = [shaped((rows, units), f32), shaped((units, features), bf16)]
    whole = lambda a: pl.BlockSpec(a.shape, lambda i: (0, 0))
    first = lambda a: pl.BlockSpec((a.shape[0], width), lambda i: (0, 0))
    return pl.pallas_call(
        functools.partial(early_kernel, plane, capacity, groups),
        grid=(1,),
        out_shape=outs,
        in_specs=[first(w_out), whole(hid1), in_hbm(pad)] + [whole(p) for p in pieces],
        out_specs=[whole(outs[0]), first(outs[1])],
        scratch_shapes=[pltpu.VMEM((rows, n), bf16) for n in (width, width, lanes_of(units), 2 * LANES)]
        + [pltpu.SemaphoreType.DMA((3,))],
        compiler_params=pltpu.CompilerParams(vmem_limit_bytes=VMEM_LIMIT),
        cost_estimate=cost(args, outs, 3 * units * rows * features),
    )(w_out, hid1, pad, *pieces)


def second_kernel(plane, capacity, groups, first, wout_ref, hid_ref, slope_ref, pulled_ref, pad_ref, *refs):
    g_ref, gp_ref, score_ref, cols, sem = refs[-5:]
    units, copies = wout_ref.shape[0], Copies(sem)
    copies.start(plate(pad_ref, COLS, cols.shape[1]), cols)
    arrange(plane, capacity, groups, refs[:-5], g_ref)
    pulled = pulled_ref[...] + dot(g_ref[...], wout_ref[:, first:], 1, 1)
    copies.wait()
    gp_ref[:, :units] = (cols[:, 1:2].astype(f32) * pulled * slope_ref[...]).astype(bf16)
    score = jnp.sum(hid_ref[...].astype(f32) * pulled, axis=1, keepdims=True)
    lane = lax.broadcasted_iota(jnp.int32, score_ref.shape, 1)
    both = jnp.where(lane == 0, cols[:, LANES:].astype(f32), jnp.where(lane == 1, score, 0.0))
    score_ref[...] = both.astype(bf16)


def late_kernel(width, part, units, _, pad_ref, g1_ref, gp1_ref, *refs):
    gin_ref, gout_ref, cols, x, g, hid, gp, held, sem, out_sem = refs
    rows, features = pad_ref.shape[1:]
    skip = features - part
    copies = Copies(sem)
    top, low = pl.ds(0, rows), pl.ds(rows, rows)
    lanes = lambda at: pl.ds(at, width)
    first = [copies.start(plate(pad_ref, GP0, gp.shape[1]), gp.at[top, :])]
    tiles = []
    for at in range(0, features, width):
        tiles.append(
            [copies.start(pad_ref.at[n, :, lanes(at)], x.at[to, lanes(at)]) for n, to in ((X0, top), (X1, low))]
        )
    then = [copies.start(plate(pad_ref, n, hid.shape[1]), hid.at[at, :]) for n, at in ((HID0, top), (HID1, low))]
    then.append(copies.start(plate(pad_ref, COLS, cols.shape[1]), cols))
    then.append(copies.start(pad_ref.at[G0, :, pl.ds(skip, part)], g))
    sent = []

    def store(n, value, out_ref, at):
        slot = n % held.shape[0]
        if n >= held.shape[0]:
            sent[n - held.shape[0]].wait()
        held[slot] = value.astype(bf16)
        sent.append(pltpu.make_async_copy(held.at[slot], out_ref.at[:, lanes(at)], out_sem.at[slot]))
        sent[-1].start()

    gp[rows:, :] = gp1_ref[...]
    for copy in first:
        copy.wait()
    for n, tile in enumerate(tiles):
        for copy in tile:
            copy.wait()
        at = n * width
        store(n, dot(gp[:, :units], x[:, at : at + width], 0, 0), gin_ref, at)
    for copy in then:
        copy.wait()
    for n in range(part // width):
        at = n * width
        y0 = weighted(cols, 0, g[:, at : at + width])
        y1 = weighted(cols, 1, g1_ref[:, at : at + width])
        store(len(tiles) + n, dot(hid[:, :units], jnp.concatenate([y0, y1], axis=0), 0, 0), gout_ref, skip + at)
    for copy in sent[-held.shape[0] :]:
        copy.wait()


def late(width, done, pad, g1, gp1):
    units, features = done.shape
    rows, part = g1.shape
    outs = [shaped((units, features), bf16)] * 2
    return pl.pallas_call(
        functools.partial(late_kernel, width, part, units),
        out_shape=outs,
        in_specs=[in_hbm(done), in_hbm(pad), pl.BlockSpec(), pl.BlockSpec()],
        out_specs=[in_hbm(o) for o in outs],
        scratch_shapes=[pltpu.VMEM((rows, 2 * LANES), bf16), pltpu.VMEM((2 * rows, features), bf16)]
        + [pltpu.VMEM((rows, part), bf16)]
        + [pltpu.VMEM((2 * rows, lanes_of(units)), bf16)] * 2
        + [pltpu.VMEM((3, units, width), bf16)]
        + [pltpu.SemaphoreType.DMA((7 + 2 * (features // width),)), pltpu.SemaphoreType.DMA((3,))],
        input_output_aliases={0: 1},
        compiler_params=pltpu.CompilerParams(vmem_limit_bytes=LATE_LIMIT),
        cost_estimate=cost((), outs, 6 * units * rows * features),
    )(done, pad, g1, gp1)


def collect_kernel(experts, capacity, topk, meta_ref, hot0_ref, hot1_ref, score_ref, out_ref):
    tokens = meta_ref.shape[2]
    rep = expander(experts * capacity, experts, capacity)
    expert = lax.broadcasted_iota(jnp.int32, (experts, tokens), 0).astype(f32)
    own = meta_ref[lax.axis_index("expert")]
    for k, hot_ref in enumerate((hot0_ref, hot1_ref)):
        placed = hot_ref[...].astype(f32) * score_ref[:, k : k + 1].astype(f32)
        by_expert = dot(rep, placed.astype(bf16), 0, 0)
        for j in range(topk):
            i = k * topk + j
            picked = jnp.where(own[i : i + 1, :] == expert, by_expert, 0.0)
            out_ref[i : i + 1, :] = jnp.sum(picked, axis=0, keepdims=True).astype(bf16)


def body(inputs, entering, weight_in, weight_out, gate_probs, expert_ids):
    experts = lax.axis_size("expert")
    segments = lax.axis_size("segment")
    tokens, features = entering.shape[1:]
    ticks, topk = expert_ids.shape[1], expert_ids.shape[3]
    units = weight_in.shape[2]
    capacity = 3 * tokens * topk // (2 * experts)
    rows = experts * capacity
    plane = Plane(experts)
    matmul = 2 * rows * units * features
    half = features // HALVES
    w_in, w_out = weight_in[0, 0], weight_out[0, 0]
    g0 = entering[0]

    x0 = inputs[0, 0]
    expert_ids, gate_probs = behind((expert_ids, gate_probs), [x0])
    ids = jnp.transpose(expert_ids[0], (0, 2, 1)).reshape(ticks * topk, tokens)
    probs = jnp.transpose(gate_probs[0], (0, 2, 1)).reshape(ticks * topk, tokens)
    meta = jnp.concatenate([ids.astype(f32), probs.astype(f32)], axis=0)
    own_meta = meta
    meta = jnp.broadcast_to(meta[None], (experts,) + meta.shape)
    meta = lax.all_to_all(meta, "expert", split_axis=0, concat_axis=0, tiled=True)
    hot0, hot1, prob = call(
        functools.partial(slots_kernel, experts, capacity, topk),
        [shaped((rows, tokens), bf16)] * 2 + [shaped((rows, LANES), bf16)],
        meta,
    )
    plate_bytes = rows * features * 2
    pad = shaped((max(9, -(-PAD_BYTES // plate_bytes)), rows, features), bf16)

    stepped = capacity % 16 == 0
    ranks = [list(range(k * topk, (k + 1) * topk)) for k in range(ticks)]
    pick = functools.partial(picked_rows, plane, capacity)
    if stepped:
        metas = [own_meta, plane.send(own_meta, (0, 0, 1))]
        x1 = inputs[0, 1]
        pad, *x1 = pick(ranks[1], 2, x1, metas, pad=pad)
        x1_near, _ = sent_rows(plane, 2, x1[:-1])
        x1_groups, x1_rest = [(0, sent_layout(plane, 2))], x1[-1:]
        select_meta = behind(meta, x1)
        x0, x0_layout = sent_rows(plane, 1, pick(ranks[0], 1, x0, select_meta))
        *g0_first, g0_last = pick(ranks[0], 0, g0, select_meta)
        g0_in, g0_layout = sent_rows(plane, 0, [*g0_first, behind(g0_last, [*x1_near, prob])])
        plans = [return_plan(plane, ranks[0], axis) for axis in AXES]
        plans += [gather_plan(plane, ranks[1], axis) for axis in AXES]
        shapes = [shaped((len(b), len(e) * capacity, tokens), bf16) for _, b, e in plans]
        masks = call(functools.partial(masks_kernel, plane, capacity, plans), shapes, meta)
        back_plans = [[[plane.back(plane.back(t, u)) for u in plane.along(axis)] for t in plane.across(axis)] for axis in AXES]
        shapes = [shaped((len(blocks) * capacity, half), bf16) for plan in back_plans for blocks in plan]
    else:
        (pad,) = call(lambda meta_ref, _: None, [pad], meta, pad_out=True)
        x0, x0_layout = [exchange(spread(hot0, x0), experts)], None
        g0_in, g0_layout = [exchange(spread(hot0, g0), experts)], None
        back_plans = [None] * HALVES
        shapes = [shaped((rows, half), bf16)] * HALVES

    if stepped:
        arrived = [*x0, *g0_in]
        x0 = behind(x0, x1_near)
    wide = lanes_of(units)
    vmem = lambda n: pltpu.VMEM((rows, n), bf16)
    x0, hid0, slope0 = call(
        functools.partial(first_preact_kernel, plane, capacity, [(0, x0_layout)]),
        [shaped((rows, features), bf16), shaped((rows, wide), bf16), shaped((rows, units), f32)], w_in, *x0,
    )
    g0_in, gp0, cols, *backs = call(
        functools.partial(first_kernel, plane, capacity, [(0, g0_layout)], back_plans),
        [shaped((rows, n), bf16) for n in (features, wide, 2 * LANES)] + shapes,
        w_in, w_out, hid0, slope0, prob, *g0_in, scratch=[vmem(half)],
    )
    pad = stash(pad, (X0, G0, HID0, GP0, COLS), x0, g0_in, hid0, gp0, cols)
    leaving, after = [], []
    if stepped:
        x1_rest = [plane.send(p, t) for p, t in zip(behind(x1_rest, [hid0, *arrived]), plane.across(2)[-1:])]
        after = [pad, *x1_rest]
    for h, axis in enumerate(AXES):
        if stepped:
            count = len(plane.across(axis))
            pieces, backs = backs[:count], backs[count:]
            out, parts = returned_rows(plane, capacity, axis, pieces, masks[h], g0, h * half, after)
        else:
            (out,) = call(
                functools.partial(combine_kernel, h * half), [shaped((tokens, half), bf16)],
                hot0, exchange(backs[h], experts), g0, flops=2 * rows * tokens * half,
            )
        leaving.append(out)
        after = [out]

    if stepped:
        x1 = x1_near + x1_rest
    else:
        x1, x1_groups = [exchange(spread(hot1, inputs[0, 1]), experts)], [(0, None)]
    parts, after = [], []
    for h, axis in enumerate(AXES):
        arrived = lax.ppermute(leaving[h], "segment", [(i, i - 1) for i in range(1, segments)])
        arrived = behind(arrived, after)
        if stepped:
            picked = pick(ranks[1], axis, arrived, meta, masks[HALVES + h])
            pieces, layout = sent_rows(plane, axis, picked)
            after = picked
        else:
            pieces, layout = [exchange(spread(hot1, arrived), experts)], None
        parts.append((pieces, [(0, layout)]))
    x1 = behind(x1, after)
    pad, hid1, slope1 = preact(plane, capacity, x1_groups, (X1, HID1), w_in, pad, *x1)
    pulled, gout = early(plane, capacity, parts[0][1], w_out, hid1, pad, *parts[0][0])
    pieces = behind(parts[1][0], [pulled])
    g1, gp1, scores = call(
        functools.partial(second_kernel, plane, capacity, parts[1][1], half),
        [shaped((rows, half), bf16), shaped((rows, wide), bf16), shaped((rows, LANES), bf16)],
        w_out, hid1, slope1, pulled, pad, *pieces, flops=matmul // 2, pad=4,
        scratch=[vmem(2 * LANES), pltpu.SemaphoreType.DMA((1,))],
    )
    scores = exchange(scores, experts)
    grad_in, grad_out = late(features // TILES, gout, pad, g1, gp1)
    (prob_grads,) = call(
        functools.partial(collect_kernel, experts, capacity, topk),
        [shaped((ticks * topk, tokens), bf16)], meta, hot0, hot1, scores,
    )
    prob_grads = jnp.transpose(prob_grads.reshape(ticks, topk, tokens), (0, 2, 1))
    return grad_in[None, None], grad_out[None, None], prob_grads[None]


def solution(mesh):
    return jax.shard_map(
        body,
        mesh=mesh,
        in_specs=(
            P("segment", None, "expert", None),
            P("segment", "expert", None),
            P("segment", "expert", None, None),
            P("segment", "expert", None, None),
            P("segment", None, "expert", None),
            P("segment", None, "expert", None),
        ),
        out_specs=(
            P("segment", "expert", None, None),
            P("segment", "expert", None, None),
            P("segment", None, "expert", None),
        ),
        check_vma=False,
    )
```

```python
import functools

import jax
import jax.numpy as jnp
from jax import lax
from jax.experimental import pallas as pl
from jax.experimental.pallas import tpu as pltpu
from jax.sharding import PartitionSpec as P

half_root = 0.7071067811865476
density_scale = 0.3989422804014327
LANES = 128
AXES = (2, 2)
HALVES = len(AXES)
TILES = 2
LONG = 10**11
LATE_LIMIT = 32 * 1024 * 1024
X0, G0, X1, G1, HID0, HID1, GP0, GP1, COLS = range(9)
PAD_BYTES = 66 * 1024 * 1024
VMEM_LIMIT = 20 * 1024 * 1024
f32 = jnp.float32
bf16 = jnp.bfloat16


def dot(a, b, ca, cb):
    return lax.dot_general(a, b, (((ca,), (cb,)), ((), ())), preferred_element_type=f32)


def shaped(shape, dtype):
    return jax.ShapeDtypeStruct(shape, dtype)


def cost(args, outs, flops):
    size = sum(a.size * a.dtype.itemsize for a in list(args) + list(outs))
    return pl.CostEstimate(flops=flops if flops == LONG else 0, bytes_accessed=size * 64, transcendentals=0)


def in_hbm(ref):
    return pl.BlockSpec(memory_space=pltpu.HBM)


def call(kernel, outs, *args, flops=0, scratch=(), pad=None, pad_out=False):
    specs = [pl.BlockSpec() if n != pad else in_hbm(a) for n, a in enumerate(args)]
    return pl.pallas_call(
        kernel,
        out_shape=outs,
        in_specs=specs,
        out_specs=[in_hbm(o) if pad_out and n == 0 else pl.BlockSpec() for n, o in enumerate(outs)],
        input_output_aliases={pad: 0} if pad is not None and pad_out else {},
        scratch_shapes=scratch,
        compiler_params=pltpu.CompilerParams(vmem_limit_bytes=VMEM_LIMIT),
        cost_estimate=cost(args, outs, flops),
    )(*args)


class Plane:
    def __init__(self, experts):
        chips = experts // 2
        across = next(n for n in range(int(chips**0.5), 0, -1) if chips % n == 0)
        self.size = (chips // across, across, 2)
        self.experts = experts

    def other(self, i, offset):
        _, across, cores = self.size
        coords = (i // (across * cores), (i // cores) % across, i % cores)
        a, b, c = ((p + o) % n for p, o, n in zip(coords, offset, self.size))
        return (a * across + b) * cores + c

    def back(self, *offsets):
        return tuple(-sum(o) % n for o, n in zip(zip(*offsets), self.size))

    def along(self, axis):
        return [tuple(n if d == axis else 0 for d in range(3)) for n in range(self.size[axis])]

    def across(self, axis):
        spans = [range(1 if d == axis else n) for d, n in enumerate(self.size)]
        return [(a, b, c) for a in spans[0] for b in spans[1] for c in spans[2]]

    def send(self, value, offset):
        if not any(offset):
            return value
        route = [(i, self.other(i, offset)) for i in range(self.experts)]
        return lax.ppermute(value, "expert", route)


def other_of(plane, offset):
    _, across, cores = plane.size
    i = lax.axis_index("expert")
    coords = (lax.div(i, across * cores), lax.rem(lax.div(i, cores), across), lax.rem(i, cores))
    a, b, c = (lax.rem(p + o, n) for p, o, n in zip(coords, offset, plane.size))
    return (a * across + b) * cores + c


def expander(rows, groups, capacity):
    first = lax.broadcasted_iota(jnp.int32, (rows, groups), 1) * capacity
    row = lax.broadcasted_iota(jnp.int32, (rows, groups), 0)
    return ((row >= first) & (row < first + capacity)).astype(f32).astype(bf16)


def slot_masks(named, capacity):
    count = sum(named)
    groups, tokens = count.shape
    rows = groups * capacity
    earlier = lax.broadcasted_iota(jnp.int32, (tokens, tokens), 0)
    later = lax.broadcasted_iota(jnp.int32, (tokens, tokens), 1)
    before = (earlier < later).astype(f32).astype(bf16)
    rank = dot(count.astype(bf16), before, 1, 0)
    place = jnp.where(count > 0, rank, -1.0).astype(bf16)
    rep = expander(rows, groups, capacity)
    spread = dot(rep, place, 1, 0)
    row = lax.broadcasted_iota(jnp.int32, (rows, tokens), 0)
    owner = ((row.astype(f32) + 0.5) * (1.0 / capacity)).astype(jnp.int32)
    position = (row - owner * capacity).astype(f32)
    return (spread == position).astype(f32), rep


def slots_kernel(experts, capacity, topk, meta_ref, hot0_ref, hot1_ref, prob_ref):
    tokens = meta_ref.shape[2]
    me = lax.axis_index("expert")
    expert = lax.broadcasted_iota(jnp.int32, (experts, tokens), 0).astype(f32)
    own = meta_ref[me]
    lane = lax.broadcasted_iota(jnp.int32, prob_ref.shape, 1)
    columns = jnp.zeros(prob_ref.shape, f32)
    ranks = range(topk)
    for k, hot_ref in enumerate((hot0_ref, hot1_ref)):
        at = [k * topk + j for j in ranks]
        hot, _ = slot_masks([(own[i : i + 1, :] == expert).astype(f32) for i in at], capacity)
        hot_ref[...] = hot.astype(bf16)
        mine = me.astype(f32)
        named = [(meta_ref[:, i, :] == mine).astype(f32) for i in at]
        hot, rep = slot_masks(named, capacity)
        probs = sum(n * meta_ref[:, 2 * topk + i, :] for n, i in zip(named, at))
        column = jnp.sum(hot * dot(rep, probs.astype(bf16), 1, 0), axis=1, keepdims=True)
        columns = jnp.where(lane == k, column, columns)
    prob_ref[...] = columns.astype(bf16)


def block_masks(plane, capacity, ranks, ids, experts):
    tokens = ids.shape[1]
    row = lax.broadcasted_iota(jnp.int32, (len(experts), tokens), 0)
    expert = jnp.zeros(row.shape, f32)
    for i, offset in enumerate(experts):
        expert = jnp.where(row == i, other_of(plane, offset).astype(f32), expert)
    return slot_masks([(ids[i : i + 1, :] == expert).astype(f32) for i in ranks], capacity)[0]


def masks_kernel(plane, capacity, plans, meta_ref, *out_refs):
    for (ranks, blocks, experts), out_ref in zip(plans, out_refs):
        for s, block in enumerate(blocks):
            out_ref[s] = block_masks(
                plane, capacity, ranks, meta_ref[other_of(plane, block)], experts
            ).astype(bf16)


def select_kernel(plane, capacity, plan, meta_ref, *refs):
    ranks, sources, targets = plan
    raw_refs, out_refs = refs[: len(sources)], refs[len(sources) :]
    for s, source in enumerate(sources):
        hot = block_masks(plane, capacity, ranks, meta_ref[other_of(plane, source)], targets)
        picked = dot(hot.astype(bf16), raw_refs[s][...], 1, 0).astype(bf16)
        for i, out_ref in enumerate(out_refs):
            out_ref[s * capacity : (s + 1) * capacity, :] = picked[i * capacity : (i + 1) * capacity]


def own_select_kernel(plane, capacity, plan, *refs):
    ranks, sources, targets = plan
    count = len(sources)
    for s in range(count):
        hot = block_masks(plane, capacity, ranks, refs[s][...], targets)
        picked = dot(hot.astype(bf16), refs[count + s][...], 1, 0).astype(bf16)
        at = slice(s * capacity, (s + 1) * capacity)
        for i, out_ref in enumerate(refs[2 * count + 1 : -HALVES]):
            out_ref[at, :] = picked[i * capacity : (i + 1) * capacity]
        width = refs[-1].shape[1]
        for h, out_ref in enumerate(refs[-HALVES:]):
            out_ref[at, :] = picked[-capacity:, h * width : (h + 1) * width]


def pick_own_kernel(hot_ref, raw_ref, out_ref):
    out_ref[...] = dot(hot_ref[0], raw_ref[...], 1, 0).astype(bf16)


def pick_kernel(capacity, hot_ref, own_ref, *refs):
    sources = hot_ref.shape[0]
    raw_refs, out_refs = refs[: sources - 1], refs[sources - 1 :]
    picked = [own_ref[...]]
    picked += [dot(hot_ref[s + 1], raw_ref[...], 1, 0).astype(bf16) for s, raw_ref in enumerate(raw_refs)]
    for s, rows in enumerate(picked):
        for i, out_ref in enumerate(out_refs):
            out_ref[s * capacity : (s + 1) * capacity, :] = rows[i * capacity : (i + 1) * capacity]


def gather_plan(plane, ranks, axis):
    return ranks, [plane.back(u) for u in plane.along(axis)], plane.across(axis)


def return_plan(plane, ranks, axis):
    return ranks, plane.along(axis), [plane.back(t) for t in plane.across(axis)]


def picked_rows(plane, capacity, ranks, axis, value, meta, hot=None, pad=None):
    tokens, width = value.shape
    plan = gather_plan(plane, ranks, axis)
    raws = [plane.send(value, u) for u in plane.along(axis)]
    outs = [shaped((len(plan[1]) * capacity, width), bf16)] * len(plan[2])
    flops = 2 * tokens * width * capacity * len(plan[1]) * len(plan[2])
    if pad is not None:
        kernel = functools.partial(own_select_kernel, plane, capacity, plan)
        parts = [shaped((outs[0].shape[0], width // HALVES), bf16)] * HALVES
        return call(kernel, [pad] + outs[:-1] + parts, *meta, *raws, pad_out=True)
    if hot is None:
        return call(functools.partial(select_kernel, plane, capacity, plan), outs, meta, *raws, flops=flops)
    (own,) = call(pick_own_kernel, [shaped((hot.shape[1], width), bf16)], hot, raws[0], flops=LONG)
    return call(functools.partial(pick_kernel, capacity), outs, hot, own, *raws[1:], flops=flops)


def sent_rows(plane, axis, picked):
    return [plane.send(p, t) for p, t in zip(picked, plane.across(axis))], sent_layout(plane, axis)


def sent_layout(plane, axis):
    return [[plane.back(t, u) for u in plane.along(axis)] for t in plane.across(axis)]


def combine_parts_kernel(capacity, blocks, hot_ref, *refs):
    pieces, out_refs = refs[:-blocks], refs[-blocks:]
    for s, out_ref in enumerate(out_refs):
        rows = jnp.concatenate([p[s * capacity : (s + 1) * capacity, :] for p in pieces], axis=0)
        out_ref[...] = dot(hot_ref[s], rows, 0, 0).astype(out_ref.dtype)


def seed_kernel(first, g_ref, own_ref, out_ref):
    width = out_ref.shape[1]
    out_ref[...] = g_ref[:, first : first + width].astype(f32) + own_ref[...]


def add_kernel(own_ref, *refs):
    out_ref = refs[-1]
    total = own_ref[...]
    for ref in refs[:-1]:
        total = total + ref[...].astype(f32)
    out_ref[...] = total.astype(bf16)


def returned_rows(plane, capacity, axis, pieces, hot, g, first, after):
    width, tokens = pieces[0].shape[1], g.shape[0]
    pieces = [plane.send(p, t) for p, t in zip(pieces, plane.across(axis))]
    pieces = behind(pieces, after)
    along = plane.along(axis)
    outs = [shaped((tokens, width), bf16 if any(u) else f32) for u in along]
    own, *parts = call(
        functools.partial(combine_parts_kernel, capacity, len(along)), outs, hot, *pieces,
        flops=2 * hot.size * width,
    )
    sent = [plane.send(p, u) for p, u in zip(parts, along[1:])]
    (own,) = call(functools.partial(seed_kernel, first), [shaped((tokens, width), f32)], g, own, flops=LONG)
    return call(add_kernel, [shaped((tokens, width), bf16)], own, *sent)[0], parts


def behind(values, after):
    return lax.optimization_barrier((values, after))[0] if after else values


def spread_kernel(hot_ref, x_ref, out_ref):
    out_ref[...] = dot(hot_ref[...], x_ref[...], 1, 0).astype(bf16)


def spread(hot, x):
    outs = [shaped((hot.shape[0], x.shape[1]), bf16)]
    return call(spread_kernel, outs, hot, x, flops=2 * hot.size * x.shape[1])[0]


def exchange(rows, experts):
    width = rows.shape[1]
    pieces = rows.reshape(experts, -1, width)
    arrived = lax.all_to_all(pieces, "expert", split_axis=0, concat_axis=0, tiled=True)
    return arrived.reshape(-1, width)


def combine_kernel(first, hot_ref, back_ref, g_ref, out_ref):
    width = out_ref.shape[1]
    summed = dot(hot_ref[...], back_ref[...], 0, 0)
    out_ref[...] = (g_ref[:, first : first + width].astype(f32) + summed).astype(bf16)


def arrange(plane, capacity, groups, refs, out_ref):
    refs = list(refs)
    for first, layout in groups:
        if layout is None:
            piece = refs.pop(0)
            out_ref[:, first : first + piece.shape[1]] = piece[...]
            continue
        for offsets in layout:
            piece = refs.pop(0)
            lanes = slice(first, first + piece.shape[1])
            for s, offset in enumerate(offsets):
                at = pl.multiple_of(other_of(plane, offset) * capacity, 16)
                out_ref[pl.ds(at, capacity), lanes] = piece[s * capacity : (s + 1) * capacity, :]


def gelu_parts(preact):
    cdf = 0.5 * (1.0 + lax.erf(preact * half_root))
    pdf = density_scale * jnp.exp(-0.5 * preact * preact)
    return preact * cdf, cdf + preact * pdf


class Copies:
    def __init__(self, sem):
        self.sem, self.started = sem, []

    def start(self, source, target):
        self.started.append(pltpu.make_async_copy(source, target, self.sem.at[len(self.started)]))
        self.started[-1].start()
        return self.started[-1]

    def wait(self):
        for copy in self.started:
            copy.wait()


def lanes_of(units):
    return -(-units // LANES) * LANES


def plate(pad_ref, n, lanes):
    return pad_ref.at[n, :, pl.ds(0, lanes)]


def preact_kernel(plane, capacity, groups, places, win_ref, _, *refs):
    pad_ref, hid_ref, slope_ref, x, hid, sem = refs[-6:]
    units, copies = win_ref.shape[0], Copies(sem)
    arrange(plane, capacity, groups, refs[:-6], x)
    copies.start(x, pad_ref.at[places[0]])
    activated, slope = gelu_parts(dot(x[...], win_ref[...], 1, 1))
    hidden = activated.astype(bf16)
    hid[:, :units] = hidden
    copies.start(hid, plate(pad_ref, places[1], hid.shape[1]))
    hid_ref[...] = hidden
    slope_ref[...] = slope
    copies.wait()


def preact(plane, capacity, groups, places, w_in, pad, *pieces):
    units = w_in.shape[0]
    rows, features = pad.shape[1:]
    return call(
        functools.partial(preact_kernel, plane, capacity, groups, places),
        [shaped(pad.shape, bf16), shaped((rows, units), bf16), shaped((rows, units), f32)],
        w_in, pad, *pieces, pad=1, pad_out=True,
        scratch=[pltpu.VMEM((rows, n), bf16) for n in (features, lanes_of(units))] + [pltpu.SemaphoreType.DMA((2,))],
    )


def first_preact_kernel(plane, capacity, groups, win_ref, *refs):
    x_ref, hid_ref, slope_ref = refs[-3:]
    arrange(plane, capacity, groups, refs[:-3], x_ref)
    activated, slope = gelu_parts(dot(x_ref[...], win_ref[...], 1, 1))
    hid_ref[:, : slope.shape[1]] = activated.astype(bf16)
    slope_ref[...] = slope


def first_kernel(plane, capacity, groups, plans, win_ref, wout_ref, hid_ref, slope_ref, prob_ref, *refs):
    refs, back = refs[:-1], refs[-1]
    pieces = sum(1 if plan is None else len(plan) for plan in plans)
    refs, back_refs = refs[:-pieces], list(refs[-pieces:])
    g_ref, gp_ref, cols_ref = refs[-3:]
    units = win_ref.shape[0]
    arrange(plane, capacity, groups, refs[:-3], g_ref)
    pulled = dot(g_ref[...], wout_ref[...], 1, 1)
    grad_pre = (prob_ref[:, 0:1].astype(f32) * pulled * slope_ref[...]).astype(bf16)
    gp_ref[:, :units] = grad_pre
    score = jnp.sum(hid_ref[:, :units].astype(f32) * pulled, axis=1, keepdims=True)
    cols_ref[:, :LANES] = prob_ref[...]
    cols_ref[:, LANES:] = jnp.broadcast_to(score, (score.shape[0], LANES)).astype(bf16)
    width = back.shape[1]
    for h, plan in enumerate(plans):
        back[...] = dot(grad_pre, win_ref[:, h * width : (h + 1) * width], 1, 0).astype(bf16)
        if plan is None:
            back_refs.pop(0)[...] = back[...]
            continue
        for blocks in plan:
            out_ref = back_refs.pop(0)
            for s, block in enumerate(blocks):
                at = pl.multiple_of(other_of(plane, block) * capacity, 16)
                out_ref[s * capacity : (s + 1) * capacity, :] = back[pl.ds(at, capacity), :]


def stash_kernel(places, *refs):
    pad_ref, sem = refs[-2:]
    copies = Copies(sem)
    for n, ref in zip(places, refs):
        copies.start(ref, plate(pad_ref, n, ref.shape[1]))
    copies.wait()


def stash(pad, places, *arrays):
    return pl.pallas_call(
        functools.partial(stash_kernel, places),
        out_shape=shaped(pad.shape, bf16),
        in_specs=[pl.BlockSpec()] * len(arrays) + [in_hbm(pad)],
        out_specs=in_hbm(pad),
        compiler_params=pltpu.CompilerParams(vmem_limit_bytes=VMEM_LIMIT),
        scratch_shapes=[pltpu.SemaphoreType.DMA((len(arrays),))],
        input_output_aliases={len(arrays): 0},
        cost_estimate=pl.CostEstimate(flops=0, bytes_accessed=0, transcendentals=0),
    )(*arrays, pad)


def weighted(prob_ref, k, g):
    return (prob_ref[:, k : k + 1].astype(f32) * g.astype(f32)).astype(bf16)


def early_kernel(plane, capacity, groups, wout_ref, hid1_ref, pad_ref, *refs):
    pulled_ref, gout_ref, g, g0, hid0, cols, sem = refs[-7:]
    units, copies = wout_ref.shape[0], Copies(sem)
    copies.start(plate(pad_ref, G0, g0.shape[1]), g0)
    copies.start(plate(pad_ref, HID0, hid0.shape[1]), hid0)
    copies.start(plate(pad_ref, COLS, cols.shape[1]), cols)
    arrange(plane, capacity, groups, refs[:-7], g)
    pulled_ref[...] = dot(g[...], wout_ref[...], 1, 1)
    copies.wait()
    y = jnp.concatenate([weighted(cols, 0, g0[...]), weighted(cols, 1, g[...])], axis=0)
    hid = jnp.concatenate([hid0[:, :units], hid1_ref[...]], axis=0)
    gout_ref[...] = dot(hid, y, 0, 0).astype(bf16)


def early(plane, capacity, groups, w_out, hid1, pad, *pieces):
    rows, units = hid1.shape
    features = w_out.shape[1]
    width = features // HALVES
    args = (w_out, hid1, *pieces)
    outs = [shaped((rows, units), f32), shaped((units, features), bf16)]
    whole = lambda a: pl.BlockSpec(a.shape, lambda i: (0, 0))
    first = lambda a: pl.BlockSpec((a.shape[0], width), lambda i: (0, 0))
    return pl.pallas_call(
        functools.partial(early_kernel, plane, capacity, groups),
        grid=(1,),
        out_shape=outs,
        in_specs=[first(w_out), whole(hid1), in_hbm(pad)] + [whole(p) for p in pieces],
        out_specs=[whole(outs[0]), first(outs[1])],
        scratch_shapes=[pltpu.VMEM((rows, n), bf16) for n in (width, width, lanes_of(units), 2 * LANES)]
        + [pltpu.SemaphoreType.DMA((3,))],
        compiler_params=pltpu.CompilerParams(vmem_limit_bytes=VMEM_LIMIT),
        cost_estimate=cost(args, outs, 3 * units * rows * features),
    )(w_out, hid1, pad, *pieces)


def second_kernel(plane, capacity, groups, first, wout_ref, hid_ref, slope_ref, pulled_ref, pad_ref, *refs):
    g_ref, gp_ref, score_ref, cols, sem = refs[-5:]
    units, copies = wout_ref.shape[0], Copies(sem)
    copies.start(plate(pad_ref, COLS, cols.shape[1]), cols)
    arrange(plane, capacity, groups, refs[:-5], g_ref)
    pulled = pulled_ref[...] + dot(g_ref[...], wout_ref[:, first:], 1, 1)
    copies.wait()
    gp_ref[:, :units] = (cols[:, 1:2].astype(f32) * pulled * slope_ref[...]).astype(bf16)
    score = jnp.sum(hid_ref[...].astype(f32) * pulled, axis=1, keepdims=True)
    lane = lax.broadcasted_iota(jnp.int32, score_ref.shape, 1)
    both = jnp.where(lane == 0, cols[:, LANES:].astype(f32), jnp.where(lane == 1, score, 0.0))
    score_ref[...] = both.astype(bf16)


def late_kernel(width, part, units, _, pad_ref, g1_ref, gp1_ref, *refs):
    gin_ref, gout_ref, cols, x, g, hid, gp, held, sem, out_sem = refs
    rows, features = pad_ref.shape[1:]
    skip = features - part
    copies = Copies(sem)
    top, low = pl.ds(0, rows), pl.ds(rows, rows)
    lanes = lambda at: pl.ds(at, width)
    first = [copies.start(plate(pad_ref, GP0, gp.shape[1]), gp.at[top, :])]
    tiles = []
    for at in range(0, features, width):
        tiles.append(
            [copies.start(pad_ref.at[n, :, lanes(at)], x.at[to, lanes(at)]) for n, to in ((X0, top), (X1, low))]
        )
    then = [copies.start(plate(pad_ref, n, hid.shape[1]), hid.at[at, :]) for n, at in ((HID0, top), (HID1, low))]
    then.append(copies.start(plate(pad_ref, COLS, cols.shape[1]), cols))
    then.append(copies.start(pad_ref.at[G0, :, pl.ds(skip, part)], g))
    sent = []

    def store(n, value, out_ref, at):
        slot = n % held.shape[0]
        if n >= held.shape[0]:
            sent[n - held.shape[0]].wait()
        held[slot] = value.astype(bf16)
        sent.append(pltpu.make_async_copy(held.at[slot], out_ref.at[:, lanes(at)], out_sem.at[slot]))
        sent[-1].start()

    gp[rows:, :] = gp1_ref[...]
    for copy in first:
        copy.wait()
    for n, tile in enumerate(tiles):
        for copy in tile:
            copy.wait()
        at = n * width
        store(n, dot(gp[:, :units], x[:, at : at + width], 0, 0), gin_ref, at)
    for copy in then:
        copy.wait()
    for n in range(part // width):
        at = n * width
        y0 = weighted(cols, 0, g[:, at : at + width])
        y1 = weighted(cols, 1, g1_ref[:, at : at + width])
        store(len(tiles) + n, dot(hid[:, :units], jnp.concatenate([y0, y1], axis=0), 0, 0), gout_ref, skip + at)
    for copy in sent[-held.shape[0] :]:
        copy.wait()


def late(width, done, pad, g1, gp1):
    units, features = done.shape
    rows, part = g1.shape
    outs = [shaped((units, features), bf16)] * 2
    return pl.pallas_call(
        functools.partial(late_kernel, width, part, units),
        out_shape=outs,
        in_specs=[in_hbm(done), in_hbm(pad), pl.BlockSpec(), pl.BlockSpec()],
        out_specs=[in_hbm(o) for o in outs],
        scratch_shapes=[pltpu.VMEM((rows, 2 * LANES), bf16), pltpu.VMEM((2 * rows, features), bf16)]
        + [pltpu.VMEM((rows, part), bf16)]
        + [pltpu.VMEM((2 * rows, lanes_of(units)), bf16)] * 2
        + [pltpu.VMEM((3, units, width), bf16)]
        + [pltpu.SemaphoreType.DMA((7 + 2 * (features // width),)), pltpu.SemaphoreType.DMA((3,))],
        input_output_aliases={0: 1},
        compiler_params=pltpu.CompilerParams(vmem_limit_bytes=LATE_LIMIT),
        cost_estimate=cost((), outs, 6 * units * rows * features),
    )(done, pad, g1, gp1)


def collect_kernel(experts, capacity, topk, meta_ref, hot0_ref, hot1_ref, score_ref, out_ref):
    tokens = meta_ref.shape[2]
    rep = expander(experts * capacity, experts, capacity)
    expert = lax.broadcasted_iota(jnp.int32, (experts, tokens), 0).astype(f32)
    own = meta_ref[lax.axis_index("expert")]
    for k, hot_ref in enumerate((hot0_ref, hot1_ref)):
        placed = hot_ref[...].astype(f32) * score_ref[:, k : k + 1].astype(f32)
        by_expert = dot(rep, placed.astype(bf16), 0, 0)
        for j in range(topk):
            i = k * topk + j
            picked = jnp.where(own[i : i + 1, :] == expert, by_expert, 0.0)
            out_ref[i : i + 1, :] = jnp.sum(picked, axis=0, keepdims=True).astype(bf16)


def body(inputs, entering, weight_in, weight_out, gate_probs, expert_ids):
    experts = lax.axis_size("expert")
    segments = lax.axis_size("segment")
    tokens, features = entering.shape[1:]
    ticks, topk = expert_ids.shape[1], expert_ids.shape[3]
    units = weight_in.shape[2]
    capacity = 3 * tokens * topk // (2 * experts)
    rows = experts * capacity
    plane = Plane(experts)
    matmul = 2 * rows * units * features
    half = features // HALVES
    w_in, w_out = weight_in[0, 0], weight_out[0, 0]
    g0 = entering[0]

    x0 = inputs[0, 0]
    expert_ids, gate_probs = behind((expert_ids, gate_probs), [x0])
    ids = jnp.transpose(expert_ids[0], (0, 2, 1)).reshape(ticks * topk, tokens)
    probs = jnp.transpose(gate_probs[0], (0, 2, 1)).reshape(ticks * topk, tokens)
    meta = jnp.concatenate([ids.astype(f32), probs.astype(f32)], axis=0)
    own_meta = meta
    meta = jnp.broadcast_to(meta[None], (experts,) + meta.shape)
    meta = lax.all_to_all(meta, "expert", split_axis=0, concat_axis=0, tiled=True)
    hot0, hot1, prob = call(
        functools.partial(slots_kernel, experts, capacity, topk),
        [shaped((rows, tokens), bf16)] * 2 + [shaped((rows, LANES), bf16)],
        meta,
    )
    plate_bytes = rows * features * 2
    pad = shaped((max(9, -(-PAD_BYTES // plate_bytes)), rows, features), bf16)

    stepped = capacity % 16 == 0
    ranks = [list(range(k * topk, (k + 1) * topk)) for k in range(ticks)]
    pick = functools.partial(picked_rows, plane, capacity)
    if stepped:
        metas = [own_meta, plane.send(own_meta, (0, 0, 1))]
        x1 = inputs[0, 1]
        pad, *x1 = pick(ranks[1], 2, x1, metas, pad=pad)
        x1_near, _ = sent_rows(plane, 2, x1[:-HALVES])
        *near_layout, rest_layout = sent_layout(plane, 2)
        x1_groups = [(0, near_layout)] + [(h * half, [rest_layout]) for h in range(HALVES)]
        x1_rest = x1[-HALVES:]
        select_meta = behind(meta, x1)
        x0, x0_layout = sent_rows(plane, 1, pick(ranks[0], 1, x0, select_meta))
        *g0_first, g0_last = pick(ranks[0], 0, g0, select_meta)
        g0_in, g0_layout = sent_rows(plane, 0, [*g0_first, behind(g0_last, [*x1_near, prob])])
        plans = [return_plan(plane, ranks[0], axis) for axis in AXES]
        plans += [gather_plan(plane, ranks[1], axis) for axis in AXES]
        shapes = [shaped((len(b), len(e) * capacity, tokens), bf16) for _, b, e in plans]
        masks = call(functools.partial(masks_kernel, plane, capacity, plans), shapes, meta)
        back_plans = [[[plane.back(plane.back(t, u)) for u in plane.along(axis)] for t in plane.across(axis)] for axis in AXES]
        shapes = [shaped((len(blocks) * capacity, half), bf16) for plan in back_plans for blocks in plan]
    else:
        (pad,) = call(lambda meta_ref, _: None, [pad], meta, pad_out=True)
        x0, x0_layout = [exchange(spread(hot0, x0), experts)], None
        g0_in, g0_layout = [exchange(spread(hot0, g0), experts)], None
        back_plans = [None] * HALVES
        shapes = [shaped((rows, half), bf16)] * HALVES

    if stepped:
        arrived = [*x0, *g0_in]
        x0 = behind(x0, x1_near)
    wide = lanes_of(units)
    vmem = lambda n: pltpu.VMEM((rows, n), bf16)
    x0, hid0, slope0 = call(
        functools.partial(first_preact_kernel, plane, capacity, [(0, x0_layout)]),
        [shaped((rows, features), bf16), shaped((rows, wide), bf16), shaped((rows, units), f32)], w_in, *x0,
    )
    g0_in, gp0, cols, *backs = call(
        functools.partial(first_kernel, plane, capacity, [(0, g0_layout)], back_plans),
        [shaped((rows, n), bf16) for n in (features, wide, 2 * LANES)] + shapes,
        w_in, w_out, hid0, slope0, prob, *g0_in, scratch=[vmem(half)],
    )
    pad = stash(pad, (X0, G0, HID0, GP0, COLS), x0, g0_in, hid0, gp0, cols)
    leaving, after = [], []
    if stepped:
        far = plane.across(2)[-1]
        x1_rest[0] = plane.send(behind(x1_rest[0], [hid0, *arrived]), far)
        after = [pad, x1_rest[0]]
    for h, axis in enumerate(AXES):
        if stepped:
            count = len(plane.across(axis))
            pieces, backs = backs[:count], backs[count:]
            out, parts = returned_rows(plane, capacity, axis, pieces, masks[h], g0, h * half, after)
        else:
            (out,) = call(
                functools.partial(combine_kernel, h * half), [shaped((tokens, half), bf16)],
                hot0, exchange(backs[h], experts), g0, flops=2 * rows * tokens * half,
            )
        leaving.append(out)
        after = [out]

    if stepped:
        x1_rest[1:] = [plane.send(p, far) for p in behind(x1_rest[1:], leaving)]
        x1 = x1_near + x1_rest
    else:
        x1, x1_groups = [exchange(spread(hot1, inputs[0, 1]), experts)], [(0, None)]
    parts, after = [], []
    for h, axis in enumerate(AXES):
        arrived = lax.ppermute(leaving[h], "segment", [(i, i - 1) for i in range(1, segments)])
        arrived = behind(arrived, after)
        if stepped:
            picked = pick(ranks[1], axis, arrived, meta, masks[HALVES + h])
            pieces, layout = sent_rows(plane, axis, picked)
            after = picked
        else:
            pieces, layout = [exchange(spread(hot1, arrived), experts)], None
        parts.append((pieces, [(0, layout)]))
    x1 = behind(x1, after)
    pad, hid1, slope1 = preact(plane, capacity, x1_groups, (X1, HID1), w_in, pad, *x1)
    pulled, gout = early(plane, capacity, parts[0][1], w_out, hid1, pad, *parts[0][0])
    pieces = behind(parts[1][0], [pulled])
    g1, gp1, scores = call(
        functools.partial(second_kernel, plane, capacity, parts[1][1], half),
        [shaped((rows, half), bf16), shaped((rows, wide), bf16), shaped((rows, LANES), bf16)],
        w_out, hid1, slope1, pulled, pad, *pieces, flops=matmul // 2, pad=4,
        scratch=[vmem(2 * LANES), pltpu.SemaphoreType.DMA((1,))],
    )
    scores = exchange(scores, experts)
    grad_in, grad_out = late(features // TILES, gout, pad, g1, gp1)
    (prob_grads,) = call(
        functools.partial(collect_kernel, experts, capacity, topk),
        [shaped((ticks * topk, tokens), bf16)], meta, hot0, hot1, scores,
    )
    prob_grads = jnp.transpose(prob_grads.reshape(ticks, topk, tokens), (0, 2, 1))
    return grad_in[None, None], grad_out[None, None], prob_grads[None]


def solution(mesh):
    return jax.shard_map(
        body,
        mesh=mesh,
        in_specs=(
            P("segment", None, "expert", None),
            P("segment", "expert", None),
            P("segment", "expert", None, None),
            P("segment", "expert", None, None),
            P("segment", None, "expert", None),
            P("segment", None, "expert", None),
        ),
        out_specs=(
            P("segment", "expert", None, None),
            P("segment", "expert", None, None),
            P("segment", None, "expert", None),
        ),
        check_vma=False,
    )
```

```python
import functools

import jax
import jax.numpy as jnp
from jax import lax
from jax.experimental import pallas as pl
from jax.experimental.pallas import tpu as pltpu
from jax.sharding import PartitionSpec as P

half_root = 0.7071067811865476
density_scale = 0.3989422804014327
LANES = 128
AXES = (2, 2)
HALVES = len(AXES)
TILES = 2
LONG = 10**11
OWN_LIMIT = 60 * 1024 * 1024
LATE_LIMIT = 32 * 1024 * 1024
X0, G0, X1, G1, HID0, HID1, GP0, GP1, COLS = range(9)
PAD_BYTES = 66 * 1024 * 1024
VMEM_LIMIT = 20 * 1024 * 1024
f32 = jnp.float32
bf16 = jnp.bfloat16


def dot(a, b, ca, cb):
    return lax.dot_general(a, b, (((ca,), (cb,)), ((), ())), preferred_element_type=f32)


def shaped(shape, dtype):
    return jax.ShapeDtypeStruct(shape, dtype)


def cost(args, outs, flops):
    size = sum(a.size * a.dtype.itemsize for a in list(args) + list(outs))
    return pl.CostEstimate(flops=flops if flops == LONG else 0, bytes_accessed=size * 64, transcendentals=0)


def in_hbm(ref):
    return pl.BlockSpec(memory_space=pltpu.HBM)


def call(kernel, outs, *args, flops=0, scratch=(), pad=None, pad_out=False):
    specs = [pl.BlockSpec() if n != pad else in_hbm(a) for n, a in enumerate(args)]
    return pl.pallas_call(
        kernel,
        out_shape=outs,
        in_specs=specs,
        out_specs=[in_hbm(o) if pad_out and n == 0 else pl.BlockSpec() for n, o in enumerate(outs)],
        input_output_aliases={pad: 0} if pad is not None and pad_out else {},
        scratch_shapes=scratch,
        compiler_params=pltpu.CompilerParams(vmem_limit_bytes=VMEM_LIMIT),
        cost_estimate=cost(args, outs, flops),
    )(*args)


class Plane:
    def __init__(self, experts):
        chips = experts // 2
        across = next(n for n in range(int(chips**0.5), 0, -1) if chips % n == 0)
        self.size = (chips // across, across, 2)
        self.experts = experts

    def other(self, i, offset):
        _, across, cores = self.size
        coords = (i // (across * cores), (i // cores) % across, i % cores)
        a, b, c = ((p + o) % n for p, o, n in zip(coords, offset, self.size))
        return (a * across + b) * cores + c

    def back(self, *offsets):
        return tuple(-sum(o) % n for o, n in zip(zip(*offsets), self.size))

    def along(self, axis):
        return [tuple(n if d == axis else 0 for d in range(3)) for n in range(self.size[axis])]

    def across(self, axis):
        spans = [range(1 if d == axis else n) for d, n in enumerate(self.size)]
        return [(a, b, c) for a in spans[0] for b in spans[1] for c in spans[2]]

    def send(self, value, offset):
        if not any(offset):
            return value
        route = [(i, self.other(i, offset)) for i in range(self.experts)]
        return lax.ppermute(value, "expert", route)


def other_of(plane, offset):
    _, across, cores = plane.size
    i = lax.axis_index("expert")
    coords = (lax.div(i, across * cores), lax.rem(lax.div(i, cores), across), lax.rem(i, cores))
    a, b, c = (lax.rem(p + o, n) for p, o, n in zip(coords, offset, plane.size))
    return (a * across + b) * cores + c


def expander(rows, groups, capacity):
    first = lax.broadcasted_iota(jnp.int32, (rows, groups), 1) * capacity
    row = lax.broadcasted_iota(jnp.int32, (rows, groups), 0)
    return ((row >= first) & (row < first + capacity)).astype(f32).astype(bf16)


def slot_masks(named, capacity):
    count = sum(named)
    groups, tokens = count.shape
    rows = groups * capacity
    earlier = lax.broadcasted_iota(jnp.int32, (tokens, tokens), 0)
    later = lax.broadcasted_iota(jnp.int32, (tokens, tokens), 1)
    before = (earlier < later).astype(f32).astype(bf16)
    rank = dot(count.astype(bf16), before, 1, 0)
    place = jnp.where(count > 0, rank, -1.0).astype(bf16)
    rep = expander(rows, groups, capacity)
    spread = dot(rep, place, 1, 0)
    row = lax.broadcasted_iota(jnp.int32, (rows, tokens), 0)
    owner = ((row.astype(f32) + 0.5) * (1.0 / capacity)).astype(jnp.int32)
    position = (row - owner * capacity).astype(f32)
    return (spread == position).astype(f32), rep


def slots_kernel(experts, capacity, topk, meta_ref, hot0_ref, hot1_ref, prob_ref):
    tokens = meta_ref.shape[2]
    me = lax.axis_index("expert")
    expert = lax.broadcasted_iota(jnp.int32, (experts, tokens), 0).astype(f32)
    own = meta_ref[me]
    lane = lax.broadcasted_iota(jnp.int32, prob_ref.shape, 1)
    columns = jnp.zeros(prob_ref.shape, f32)
    ranks = range(topk)
    for k, hot_ref in enumerate((hot0_ref, hot1_ref)):
        at = [k * topk + j for j in ranks]
        hot, _ = slot_masks([(own[i : i + 1, :] == expert).astype(f32) for i in at], capacity)
        hot_ref[...] = hot.astype(bf16)
        mine = me.astype(f32)
        named = [(meta_ref[:, i, :] == mine).astype(f32) for i in at]
        hot, rep = slot_masks(named, capacity)
        probs = sum(n * meta_ref[:, 2 * topk + i, :] for n, i in zip(named, at))
        column = jnp.sum(hot * dot(rep, probs.astype(bf16), 1, 0), axis=1, keepdims=True)
        columns = jnp.where(lane == k, column, columns)
    prob_ref[...] = columns.astype(bf16)


def block_masks(plane, capacity, ranks, ids, experts):
    tokens = ids.shape[1]
    row = lax.broadcasted_iota(jnp.int32, (len(experts), tokens), 0)
    expert = jnp.zeros(row.shape, f32)
    for i, offset in enumerate(experts):
        expert = jnp.where(row == i, other_of(plane, offset).astype(f32), expert)
    return slot_masks([(ids[i : i + 1, :] == expert).astype(f32) for i in ranks], capacity)[0]


def masks_kernel(plane, capacity, plans, meta_ref, *out_refs):
    for (ranks, blocks, experts), out_ref in zip(plans, out_refs):
        for s, block in enumerate(blocks):
            out_ref[s] = block_masks(
                plane, capacity, ranks, meta_ref[other_of(plane, block)], experts
            ).astype(bf16)


def select_kernel(plane, capacity, plan, meta_ref, *refs):
    ranks, sources, targets = plan
    raw_refs, out_refs = refs[: len(sources)], refs[len(sources) :]
    for s, source in enumerate(sources):
        hot = block_masks(plane, capacity, ranks, meta_ref[other_of(plane, source)], targets)
        picked = dot(hot.astype(bf16), raw_refs[s][...], 1, 0).astype(bf16)
        for i, out_ref in enumerate(out_refs):
            out_ref[s * capacity : (s + 1) * capacity, :] = picked[i * capacity : (i + 1) * capacity]


def own_select_kernel(plane, capacity, plan, tick, *refs):
    ranks, sources, targets = plan
    refs, (raw, sem) = refs[:-2], refs[-2:]
    count = len(sources)
    copies = [pltpu.make_async_copy(refs[count + s].at[tick], raw.at[s], sem.at[s]) for s in range(count)]
    for copy in copies:
        copy.start()
    hots = [block_masks(plane, capacity, ranks, refs[s][...], targets).astype(bf16) for s in range(count)]
    width = refs[-1].shape[1]
    for s in range(count):
        copies[s].wait()
        picked = dot(hots[s], raw[s], 1, 0).astype(bf16)
        at = slice(s * capacity, (s + 1) * capacity)
        for i, out_ref in enumerate(refs[2 * count + 1 : -HALVES]):
            out_ref[at, :] = picked[i * capacity : (i + 1) * capacity]
        for h, out_ref in enumerate(refs[-HALVES:]):
            out_ref[at, :] = picked[-capacity:, h * width : (h + 1) * width]


def own_picked(plane, capacity, plan, tick, metas, raws, pad):
    _, tokens, width = raws[0].shape
    count, rows = len(raws), len(plan[1]) * capacity
    outs = [shaped((rows, width), bf16)] * (len(plan[2]) - 1) + [shaped((rows, width // HALVES), bf16)] * HALVES
    return pl.pallas_call(
        functools.partial(own_select_kernel, plane, capacity, plan, tick),
        out_shape=[pad] + outs,
        in_specs=[pl.BlockSpec()] * count + [in_hbm(r) for r in raws],
        out_specs=[in_hbm(pad)] + [pl.BlockSpec()] * len(outs),
        scratch_shapes=[pltpu.VMEM((count, tokens, width), bf16), pltpu.SemaphoreType.DMA((count,))],
        compiler_params=pltpu.CompilerParams(vmem_limit_bytes=OWN_LIMIT),
        cost_estimate=cost([*metas, *raws], outs, 0),
    )(*metas, *raws)


def pick_own_kernel(hot_ref, raw_ref, out_ref):
    out_ref[...] = dot(hot_ref[0], raw_ref[...], 1, 0).astype(bf16)


def pick_kernel(capacity, hot_ref, own_ref, *refs):
    sources = hot_ref.shape[0]
    raw_refs, out_refs = refs[: sources - 1], refs[sources - 1 :]
    picked = [own_ref[...]]
    picked += [dot(hot_ref[s + 1], raw_ref[...], 1, 0).astype(bf16) for s, raw_ref in enumerate(raw_refs)]
    for s, rows in enumerate(picked):
        for i, out_ref in enumerate(out_refs):
            out_ref[s * capacity : (s + 1) * capacity, :] = rows[i * capacity : (i + 1) * capacity]


def gather_plan(plane, ranks, axis):
    return ranks, [plane.back(u) for u in plane.along(axis)], plane.across(axis)


def return_plan(plane, ranks, axis):
    return ranks, plane.along(axis), [plane.back(t) for t in plane.across(axis)]


def picked_rows(plane, capacity, ranks, axis, value, meta, hot=None):
    tokens, width = value.shape
    plan = gather_plan(plane, ranks, axis)
    raws = [plane.send(value, u) for u in plane.along(axis)]
    outs = [shaped((len(plan[1]) * capacity, width), bf16)] * len(plan[2])
    flops = 2 * tokens * width * capacity * len(plan[1]) * len(plan[2])
    if hot is None:
        return call(functools.partial(select_kernel, plane, capacity, plan), outs, meta, *raws, flops=flops)
    (own,) = call(pick_own_kernel, [shaped((hot.shape[1], width), bf16)], hot, raws[0], flops=LONG)
    return call(functools.partial(pick_kernel, capacity), outs, hot, own, *raws[1:], flops=flops)


def sent_rows(plane, axis, picked):
    return [plane.send(p, t) for p, t in zip(picked, plane.across(axis))], sent_layout(plane, axis)


def sent_layout(plane, axis):
    return [[plane.back(t, u) for u in plane.along(axis)] for t in plane.across(axis)]


def combine_parts_kernel(capacity, blocks, hot_ref, *refs):
    pieces, out_refs = refs[:-blocks], refs[-blocks:]
    for s, out_ref in enumerate(out_refs):
        rows = jnp.concatenate([p[s * capacity : (s + 1) * capacity, :] for p in pieces], axis=0)
        out_ref[...] = dot(hot_ref[s], rows, 0, 0).astype(out_ref.dtype)


def seed_kernel(first, g_ref, own_ref, out_ref):
    width = out_ref.shape[1]
    out_ref[...] = g_ref[:, first : first + width].astype(f32) + own_ref[...]


def add_kernel(own_ref, *refs):
    out_ref = refs[-1]
    total = own_ref[...]
    for ref in refs[:-1]:
        total = total + ref[...].astype(f32)
    out_ref[...] = total.astype(bf16)


def returned_rows(plane, capacity, axis, pieces, hot, g, first, after):
    width, tokens = pieces[0].shape[1], g.shape[0]
    pieces = [plane.send(p, t) for p, t in zip(pieces, plane.across(axis))]
    pieces = behind(pieces, after)
    along = plane.along(axis)
    outs = [shaped((tokens, width), bf16 if any(u) else f32) for u in along]
    own, *parts = call(
        functools.partial(combine_parts_kernel, capacity, len(along)), outs, hot, *pieces,
        flops=2 * hot.size * width,
    )
    sent = [plane.send(p, u) for p, u in zip(parts, along[1:])]
    (own,) = call(functools.partial(seed_kernel, first), [shaped((tokens, width), f32)], g, own, flops=LONG)
    return call(add_kernel, [shaped((tokens, width), bf16)], own, *sent)[0], parts


def behind(values, after):
    return lax.optimization_barrier((values, after))[0] if after else values


def spread_kernel(hot_ref, x_ref, out_ref):
    out_ref[...] = dot(hot_ref[...], x_ref[...], 1, 0).astype(bf16)


def spread(hot, x):
    outs = [shaped((hot.shape[0], x.shape[1]), bf16)]
    return call(spread_kernel, outs, hot, x, flops=2 * hot.size * x.shape[1])[0]


def exchange(rows, experts):
    width = rows.shape[1]
    pieces = rows.reshape(experts, -1, width)
    arrived = lax.all_to_all(pieces, "expert", split_axis=0, concat_axis=0, tiled=True)
    return arrived.reshape(-1, width)


def combine_kernel(first, hot_ref, back_ref, g_ref, out_ref):
    width = out_ref.shape[1]
    summed = dot(hot_ref[...], back_ref[...], 0, 0)
    out_ref[...] = (g_ref[:, first : first + width].astype(f32) + summed).astype(bf16)


def arrange(plane, capacity, groups, refs, out_ref):
    refs = list(refs)
    for first, layout in groups:
        if layout is None:
            piece = refs.pop(0)
            out_ref[:, first : first + piece.shape[1]] = piece[...]
            continue
        for offsets in layout:
            piece = refs.pop(0)
            lanes = slice(first, first + piece.shape[1])
            for s, offset in enumerate(offsets):
                at = pl.multiple_of(other_of(plane, offset) * capacity, 16)
                out_ref[pl.ds(at, capacity), lanes] = piece[s * capacity : (s + 1) * capacity, :]


def gelu_parts(preact):
    cdf = 0.5 * (1.0 + lax.erf(preact * half_root))
    pdf = density_scale * jnp.exp(-0.5 * preact * preact)
    return preact * cdf, cdf + preact * pdf


class Copies:
    def __init__(self, sem):
        self.sem, self.started = sem, []

    def start(self, source, target):
        self.started.append(pltpu.make_async_copy(source, target, self.sem.at[len(self.started)]))
        self.started[-1].start()
        return self.started[-1]

    def wait(self):
        for copy in self.started:
            copy.wait()


def lanes_of(units):
    return -(-units // LANES) * LANES


def plate(pad_ref, n, lanes):
    return pad_ref.at[n, :, pl.ds(0, lanes)]


def preact_kernel(plane, capacity, groups, places, win_ref, _, *refs):
    pad_ref, hid_ref, slope_ref, x, hid, sem = refs[-6:]
    units, copies = win_ref.shape[0], Copies(sem)
    arrange(plane, capacity, groups, refs[:-6], x)
    copies.start(x, pad_ref.at[places[0]])
    activated, slope = gelu_parts(dot(x[...], win_ref[...], 1, 1))
    hidden = activated.astype(bf16)
    hid[:, :units] = hidden
    copies.start(hid, plate(pad_ref, places[1], hid.shape[1]))
    hid_ref[...] = hidden
    slope_ref[...] = slope
    copies.wait()


def preact(plane, capacity, groups, places, w_in, pad, *pieces):
    units = w_in.shape[0]
    rows, features = pad.shape[1:]
    return call(
        functools.partial(preact_kernel, plane, capacity, groups, places),
        [shaped(pad.shape, bf16), shaped((rows, units), bf16), shaped((rows, units), f32)],
        w_in, pad, *pieces, pad=1, pad_out=True,
        scratch=[pltpu.VMEM((rows, n), bf16) for n in (features, lanes_of(units))] + [pltpu.SemaphoreType.DMA((2,))],
    )


def first_preact_kernel(plane, capacity, groups, win_ref, *refs):
    x_ref, hid_ref, slope_ref = refs[-3:]
    arrange(plane, capacity, groups, refs[:-3], x_ref)
    activated, slope = gelu_parts(dot(x_ref[...], win_ref[...], 1, 1))
    hid_ref[:, : slope.shape[1]] = activated.astype(bf16)
    slope_ref[...] = slope


def first_kernel(plane, capacity, groups, plans, win_ref, wout_ref, hid_ref, slope_ref, prob_ref, *refs):
    refs, back = refs[:-1], refs[-1]
    pieces = sum(1 if plan is None else len(plan) for plan in plans)
    refs, back_refs = refs[:-pieces], list(refs[-pieces:])
    g_ref, gp_ref, cols_ref = refs[-3:]
    units = win_ref.shape[0]
    arrange(plane, capacity, groups, refs[:-3], g_ref)
    pulled = dot(g_ref[...], wout_ref[...], 1, 1)
    grad_pre = (prob_ref[:, 0:1].astype(f32) * pulled * slope_ref[...]).astype(bf16)
    gp_ref[:, :units] = grad_pre
    score = jnp.sum(hid_ref[:, :units].astype(f32) * pulled, axis=1, keepdims=True)
    cols_ref[:, :LANES] = prob_ref[...]
    cols_ref[:, LANES:] = jnp.broadcast_to(score, (score.shape[0], LANES)).astype(bf16)
    width = back.shape[1]
    for h, plan in enumerate(plans):
        back[...] = dot(grad_pre, win_ref[:, h * width : (h + 1) * width], 1, 0).astype(bf16)
        if plan is None:
            back_refs.pop(0)[...] = back[...]
            continue
        for blocks in plan:
            out_ref = back_refs.pop(0)
            for s, block in enumerate(blocks):
                at = pl.multiple_of(other_of(plane, block) * capacity, 16)
                out_ref[s * capacity : (s + 1) * capacity, :] = back[pl.ds(at, capacity), :]


def stash_kernel(places, *refs):
    pad_ref, sem = refs[-2:]
    copies = Copies(sem)
    for n, ref in zip(places, refs):
        copies.start(ref, plate(pad_ref, n, ref.shape[1]))
    copies.wait()


def stash(pad, places, *arrays):
    return pl.pallas_call(
        functools.partial(stash_kernel, places),
        out_shape=shaped(pad.shape, bf16),
        in_specs=[pl.BlockSpec()] * len(arrays) + [in_hbm(pad)],
        out_specs=in_hbm(pad),
        compiler_params=pltpu.CompilerParams(vmem_limit_bytes=VMEM_LIMIT),
        scratch_shapes=[pltpu.SemaphoreType.DMA((len(arrays),))],
        input_output_aliases={len(arrays): 0},
        cost_estimate=pl.CostEstimate(flops=0, bytes_accessed=0, transcendentals=0),
    )(*arrays, pad)


def weighted(prob_ref, k, g):
    return (prob_ref[:, k : k + 1].astype(f32) * g.astype(f32)).astype(bf16)


def early_kernel(plane, capacity, groups, wout_ref, hid1_ref, pad_ref, *refs):
    pulled_ref, gout_ref, g, g0, hid0, cols, sem = refs[-7:]
    units, copies = wout_ref.shape[0], Copies(sem)
    copies.start(plate(pad_ref, G0, g0.shape[1]), g0)
    copies.start(plate(pad_ref, HID0, hid0.shape[1]), hid0)
    copies.start(plate(pad_ref, COLS, cols.shape[1]), cols)
    arrange(plane, capacity, groups, refs[:-7], g)
    pulled_ref[...] = dot(g[...], wout_ref[...], 1, 1)
    copies.wait()
    y = jnp.concatenate([weighted(cols, 0, g0[...]), weighted(cols, 1, g[...])], axis=0)
    hid = jnp.concatenate([hid0[:, :units], hid1_ref[...]], axis=0)
    gout_ref[...] = dot(hid, y, 0, 0).astype(bf16)


def early(plane, capacity, groups, w_out, hid1, pad, *pieces):
    rows, units = hid1.shape
    features = w_out.shape[1]
    width = features // HALVES
    args = (w_out, hid1, *pieces)
    outs = [shaped((rows, units), f32), shaped((units, features), bf16)]
    whole = lambda a: pl.BlockSpec(a.shape, lambda i: (0, 0))
    first = lambda a: pl.BlockSpec((a.shape[0], width), lambda i: (0, 0))
    return pl.pallas_call(
        functools.partial(early_kernel, plane, capacity, groups),
        grid=(1,),
        out_shape=outs,
        in_specs=[first(w_out), whole(hid1), in_hbm(pad)] + [whole(p) for p in pieces],
        out_specs=[whole(outs[0]), first(outs[1])],
        scratch_shapes=[pltpu.VMEM((rows, n), bf16) for n in (width, width, lanes_of(units), 2 * LANES)]
        + [pltpu.SemaphoreType.DMA((3,))],
        compiler_params=pltpu.CompilerParams(vmem_limit_bytes=VMEM_LIMIT),
        cost_estimate=cost(args, outs, 3 * units * rows * features),
    )(w_out, hid1, pad, *pieces)


def second_kernel(plane, capacity, groups, first, wout_ref, hid_ref, slope_ref, pulled_ref, pad_ref, *refs):
    g_ref, gp_ref, score_ref, cols, sem = refs[-5:]
    units, copies = wout_ref.shape[0], Copies(sem)
    copies.start(plate(pad_ref, COLS, cols.shape[1]), cols)
    arrange(plane, capacity, groups, refs[:-5], g_ref)
    pulled = pulled_ref[...] + dot(g_ref[...], wout_ref[:, first:], 1, 1)
    copies.wait()
    gp_ref[:, :units] = (cols[:, 1:2].astype(f32) * pulled * slope_ref[...]).astype(bf16)
    score = jnp.sum(hid_ref[...].astype(f32) * pulled, axis=1, keepdims=True)
    lane = lax.broadcasted_iota(jnp.int32, score_ref.shape, 1)
    both = jnp.where(lane == 0, cols[:, LANES:].astype(f32), jnp.where(lane == 1, score, 0.0))
    score_ref[...] = both.astype(bf16)


def late_kernel(width, part, units, _, pad_ref, g1_ref, gp1_ref, *refs):
    gin_ref, gout_ref, cols, x, g, hid, gp, held, sem, out_sem = refs
    rows, features = pad_ref.shape[1:]
    skip = features - part
    copies = Copies(sem)
    top, low = pl.ds(0, rows), pl.ds(rows, rows)
    lanes = lambda at: pl.ds(at, width)
    first = [copies.start(plate(pad_ref, GP0, gp.shape[1]), gp.at[top, :])]
    tiles = []
    for at in range(0, features, width):
        tiles.append(
            [copies.start(pad_ref.at[n, :, lanes(at)], x.at[to, lanes(at)]) for n, to in ((X0, top), (X1, low))]
        )
    then = [copies.start(plate(pad_ref, n, hid.shape[1]), hid.at[at, :]) for n, at in ((HID0, top), (HID1, low))]
    then.append(copies.start(plate(pad_ref, COLS, cols.shape[1]), cols))
    then.append(copies.start(pad_ref.at[G0, :, pl.ds(skip, part)], g))
    sent = []

    def store(n, value, out_ref, at):
        slot = n % held.shape[0]
        if n >= held.shape[0]:
            sent[n - held.shape[0]].wait()
        held[slot] = value.astype(bf16)
        sent.append(pltpu.make_async_copy(held.at[slot], out_ref.at[:, lanes(at)], out_sem.at[slot]))
        sent[-1].start()

    gp[rows:, :] = gp1_ref[...]
    for copy in first:
        copy.wait()
    for n, tile in enumerate(tiles):
        for copy in tile:
            copy.wait()
        at = n * width
        store(n, dot(gp[:, :units], x[:, at : at + width], 0, 0), gin_ref, at)
    for copy in then:
        copy.wait()
    for n in range(part // width):
        at = n * width
        y0 = weighted(cols, 0, g[:, at : at + width])
        y1 = weighted(cols, 1, g1_ref[:, at : at + width])
        store(len(tiles) + n, dot(hid[:, :units], jnp.concatenate([y0, y1], axis=0), 0, 0), gout_ref, skip + at)
    for copy in sent[-held.shape[0] :]:
        copy.wait()


def late(width, done, pad, g1, gp1):
    units, features = done.shape
    rows, part = g1.shape
    outs = [shaped((units, features), bf16)] * 2
    return pl.pallas_call(
        functools.partial(late_kernel, width, part, units),
        out_shape=outs,
        in_specs=[in_hbm(done), in_hbm(pad), pl.BlockSpec(), pl.BlockSpec()],
        out_specs=[in_hbm(o) for o in outs],
        scratch_shapes=[pltpu.VMEM((rows, 2 * LANES), bf16), pltpu.VMEM((2 * rows, features), bf16)]
        + [pltpu.VMEM((rows, part), bf16)]
        + [pltpu.VMEM((2 * rows, lanes_of(units)), bf16)] * 2
        + [pltpu.VMEM((3, units, width), bf16)]
        + [pltpu.SemaphoreType.DMA((7 + 2 * (features // width),)), pltpu.SemaphoreType.DMA((3,))],
        input_output_aliases={0: 1},
        compiler_params=pltpu.CompilerParams(vmem_limit_bytes=LATE_LIMIT),
        cost_estimate=cost((), outs, 6 * units * rows * features),
    )(done, pad, g1, gp1)


def collect_kernel(experts, capacity, topk, meta_ref, hot0_ref, hot1_ref, score_ref, out_ref):
    tokens = meta_ref.shape[2]
    rep = expander(experts * capacity, experts, capacity)
    expert = lax.broadcasted_iota(jnp.int32, (experts, tokens), 0).astype(f32)
    own = meta_ref[lax.axis_index("expert")]
    for k, hot_ref in enumerate((hot0_ref, hot1_ref)):
        placed = hot_ref[...].astype(f32) * score_ref[:, k : k + 1].astype(f32)
        by_expert = dot(rep, placed.astype(bf16), 0, 0)
        for j in range(topk):
            i = k * topk + j
            picked = jnp.where(own[i : i + 1, :] == expert, by_expert, 0.0)
            out_ref[i : i + 1, :] = jnp.sum(picked, axis=0, keepdims=True).astype(bf16)


def body(inputs, entering, weight_in, weight_out, gate_probs, expert_ids):
    experts = lax.axis_size("expert")
    segments = lax.axis_size("segment")
    tokens, features = entering.shape[1:]
    ticks, topk = expert_ids.shape[1], expert_ids.shape[3]
    units = weight_in.shape[2]
    capacity = 3 * tokens * topk // (2 * experts)
    rows = experts * capacity
    plane = Plane(experts)
    matmul = 2 * rows * units * features
    half = features // HALVES
    w_in, w_out = weight_in[0, 0], weight_out[0, 0]
    g0 = entering[0]

    x0 = inputs[0, 0]
    expert_ids, gate_probs = behind((expert_ids, gate_probs), [x0])
    ids = jnp.transpose(expert_ids[0], (0, 2, 1)).reshape(ticks * topk, tokens)
    probs = jnp.transpose(gate_probs[0], (0, 2, 1)).reshape(ticks * topk, tokens)
    meta = jnp.concatenate([ids.astype(f32), probs.astype(f32)], axis=0)
    own_meta = meta
    meta = jnp.broadcast_to(meta[None], (experts,) + meta.shape)
    meta = lax.all_to_all(meta, "expert", split_axis=0, concat_axis=0, tiled=True)
    hot0, hot1, prob = call(
        functools.partial(slots_kernel, experts, capacity, topk),
        [shaped((rows, tokens), bf16)] * 2 + [shaped((rows, LANES), bf16)],
        meta,
    )
    plate_bytes = rows * features * 2
    pad = shaped((max(9, -(-PAD_BYTES // plate_bytes)), rows, features), bf16)

    stepped = capacity % 16 == 0
    ranks = [list(range(k * topk, (k + 1) * topk)) for k in range(ticks)]
    pick = functools.partial(picked_rows, plane, capacity)
    if stepped:
        metas = [own_meta, plane.send(own_meta, (0, 0, 1))]
        x1 = [inputs[0], plane.send(inputs[0], (0, 0, 1))]
        pad, *x1 = own_picked(plane, capacity, gather_plan(plane, ranks[1], 2), 1, metas, x1, pad)
        x1_near, _ = sent_rows(plane, 2, x1[:-HALVES])
        *near_layout, rest_layout = sent_layout(plane, 2)
        x1_groups = [(0, near_layout)] + [(h * half, [rest_layout]) for h in range(HALVES)]
        x1_rest = x1[-HALVES:]
        select_meta = behind(meta, x1)
        x0, x0_layout = sent_rows(plane, 1, pick(ranks[0], 1, x0, select_meta))
        *g0_first, g0_last = pick(ranks[0], 0, g0, select_meta)
        g0_in, g0_layout = sent_rows(plane, 0, [*g0_first, behind(g0_last, [*x1_near, prob])])
        plans = [return_plan(plane, ranks[0], axis) for axis in AXES]
        plans += [gather_plan(plane, ranks[1], axis) for axis in AXES]
        shapes = [shaped((len(b), len(e) * capacity, tokens), bf16) for _, b, e in plans]
        masks = call(functools.partial(masks_kernel, plane, capacity, plans), shapes, meta)
        back_plans = [[[plane.back(plane.back(t, u)) for u in plane.along(axis)] for t in plane.across(axis)] for axis in AXES]
        shapes = [shaped((len(blocks) * capacity, half), bf16) for plan in back_plans for blocks in plan]
    else:
        (pad,) = call(lambda meta_ref, _: None, [pad], meta, pad_out=True)
        x0, x0_layout = [exchange(spread(hot0, x0), experts)], None
        g0_in, g0_layout = [exchange(spread(hot0, g0), experts)], None
        back_plans = [None] * HALVES
        shapes = [shaped((rows, half), bf16)] * HALVES

    if stepped:
        arrived = [*x0, *g0_in]
        x0 = behind(x0, x1_near)
    wide = lanes_of(units)
    vmem = lambda n: pltpu.VMEM((rows, n), bf16)
    x0, hid0, slope0 = call(
        functools.partial(first_preact_kernel, plane, capacity, [(0, x0_layout)]),
        [shaped((rows, features), bf16), shaped((rows, wide), bf16), shaped((rows, units), f32)], w_in, *x0,
    )
    g0_in, gp0, cols, *backs = call(
        functools.partial(first_kernel, plane, capacity, [(0, g0_layout)], back_plans),
        [shaped((rows, n), bf16) for n in (features, wide, 2 * LANES)] + shapes,
        w_in, w_out, hid0, slope0, prob, *g0_in, scratch=[vmem(half)],
    )
    pad = stash(pad, (X0, G0, HID0, GP0, COLS), x0, g0_in, hid0, gp0, cols)
    leaving, after = [], []
    if stepped:
        far = plane.across(2)[-1]
        x1_rest[0] = plane.send(behind(x1_rest[0], [hid0, *arrived]), far)
        after = [pad, x1_rest[0]]
    for h, axis in enumerate(AXES):
        if stepped:
            count = len(plane.across(axis))
            pieces, backs = backs[:count], backs[count:]
            out, parts = returned_rows(plane, capacity, axis, pieces, masks[h], g0, h * half, after)
        else:
            (out,) = call(
                functools.partial(combine_kernel, h * half), [shaped((tokens, half), bf16)],
                hot0, exchange(backs[h], experts), g0, flops=2 * rows * tokens * half,
            )
        leaving.append(out)
        after = [out]

    if stepped:
        x1_rest[1:] = [plane.send(p, far) for p in behind(x1_rest[1:], leaving)]
        x1 = x1_near + x1_rest
    else:
        x1, x1_groups = [exchange(spread(hot1, inputs[0, 1]), experts)], [(0, None)]
    parts, after = [], []
    for h, axis in enumerate(AXES):
        arrived = lax.ppermute(leaving[h], "segment", [(i, i - 1) for i in range(1, segments)])
        arrived = behind(arrived, after)
        if stepped:
            picked = pick(ranks[1], axis, arrived, meta, masks[HALVES + h])
            pieces, layout = sent_rows(plane, axis, picked)
            after = picked
        else:
            pieces, layout = [exchange(spread(hot1, arrived), experts)], None
        parts.append((pieces, [(0, layout)]))
    x1 = behind(x1, after)
    pad, hid1, slope1 = preact(plane, capacity, x1_groups, (X1, HID1), w_in, pad, *x1)
    pulled, gout = early(plane, capacity, parts[0][1], w_out, hid1, pad, *parts[0][0])
    pieces = behind(parts[1][0], [pulled])
    g1, gp1, scores = call(
        functools.partial(second_kernel, plane, capacity, parts[1][1], half),
        [shaped((rows, half), bf16), shaped((rows, wide), bf16), shaped((rows, LANES), bf16)],
        w_out, hid1, slope1, pulled, pad, *pieces, flops=matmul // 2, pad=4,
        scratch=[vmem(2 * LANES), pltpu.SemaphoreType.DMA((1,))],
    )
    scores = exchange(scores, experts)
    grad_in, grad_out = late(features // TILES, gout, pad, g1, gp1)
    (prob_grads,) = call(
        functools.partial(collect_kernel, experts, capacity, topk),
        [shaped((ticks * topk, tokens), bf16)], meta, hot0, hot1, scores,
    )
    prob_grads = jnp.transpose(prob_grads.reshape(ticks, topk, tokens), (0, 2, 1))
    return grad_in[None, None], grad_out[None, None], prob_grads[None]


def solution(mesh):
    return jax.shard_map(
        body,
        mesh=mesh,
        in_specs=(
            P("segment", None, "expert", None),
            P("segment", "expert", None),
            P("segment", "expert", None, None),
            P("segment", "expert", None, None),
            P("segment", None, "expert", None),
            P("segment", None, "expert", None),
        ),
        out_specs=(
            P("segment", "expert", None, None),
            P("segment", "expert", None, None),
            P("segment", None, "expert", None),
        ),
        check_vma=False,
    )
```

```python
import functools

import jax
import jax.numpy as jnp
from jax import lax
from jax.experimental import pallas as pl
from jax.experimental.pallas import tpu as pltpu
from jax.sharding import PartitionSpec as P

half_root = 0.7071067811865476
density_scale = 0.3989422804014327
LANES = 128
AXES = (2, 2)
HALVES = len(AXES)
TILES = 2
LONG = 10**11
OWN_LIMIT = 60 * 1024 * 1024
LATE_LIMIT = 32 * 1024 * 1024
X0, G0, X1, G1, HID0, HID1, GP0, GP1, COLS = range(9)
PAD_BYTES = 66 * 1024 * 1024
VMEM_LIMIT = 20 * 1024 * 1024
f32 = jnp.float32
bf16 = jnp.bfloat16


def dot(a, b, ca, cb):
    return lax.dot_general(a, b, (((ca,), (cb,)), ((), ())), preferred_element_type=f32)


def shaped(shape, dtype):
    return jax.ShapeDtypeStruct(shape, dtype)


def cost(args, outs, flops):
    size = sum(a.size * a.dtype.itemsize for a in list(args) + list(outs))
    return pl.CostEstimate(flops=flops if flops == LONG else 0, bytes_accessed=size * 64, transcendentals=0)


def in_hbm(ref):
    return pl.BlockSpec(memory_space=pltpu.HBM)


def call(kernel, outs, *args, flops=0, scratch=(), pad=None, pad_out=False):
    specs = [pl.BlockSpec() if n != pad else in_hbm(a) for n, a in enumerate(args)]
    return pl.pallas_call(
        kernel,
        out_shape=outs,
        in_specs=specs,
        out_specs=[in_hbm(o) if pad_out and n == 0 else pl.BlockSpec() for n, o in enumerate(outs)],
        input_output_aliases={pad: 0} if pad is not None and pad_out else {},
        scratch_shapes=scratch,
        compiler_params=pltpu.CompilerParams(vmem_limit_bytes=VMEM_LIMIT),
        cost_estimate=cost(args, outs, flops),
    )(*args)


class Plane:
    def __init__(self, experts):
        chips = experts // 2
        across = next(n for n in range(int(chips**0.5), 0, -1) if chips % n == 0)
        self.size = (chips // across, across, 2)
        self.experts = experts

    def other(self, i, offset):
        _, across, cores = self.size
        coords = (i // (across * cores), (i // cores) % across, i % cores)
        a, b, c = ((p + o) % n for p, o, n in zip(coords, offset, self.size))
        return (a * across + b) * cores + c

    def back(self, *offsets):
        return tuple(-sum(o) % n for o, n in zip(zip(*offsets), self.size))

    def along(self, axis):
        return [tuple(n if d == axis else 0 for d in range(3)) for n in range(self.size[axis])]

    def across(self, axis):
        spans = [range(1 if d == axis else n) for d, n in enumerate(self.size)]
        return [(a, b, c) for a in spans[0] for b in spans[1] for c in spans[2]]

    def send(self, value, offset):
        if not any(offset):
            return value
        route = [(i, self.other(i, offset)) for i in range(self.experts)]
        return lax.ppermute(value, "expert", route)


def other_of(plane, offset):
    _, across, cores = plane.size
    i = lax.axis_index("expert")
    coords = (lax.div(i, across * cores), lax.rem(lax.div(i, cores), across), lax.rem(i, cores))
    a, b, c = (lax.rem(p + o, n) for p, o, n in zip(coords, offset, plane.size))
    return (a * across + b) * cores + c


def expander(rows, groups, capacity):
    first = lax.broadcasted_iota(jnp.int32, (rows, groups), 1) * capacity
    row = lax.broadcasted_iota(jnp.int32, (rows, groups), 0)
    return ((row >= first) & (row < first + capacity)).astype(f32).astype(bf16)


def slot_masks(named, capacity):
    count = sum(named)
    groups, tokens = count.shape
    rows = groups * capacity
    earlier = lax.broadcasted_iota(jnp.int32, (tokens, tokens), 0)
    later = lax.broadcasted_iota(jnp.int32, (tokens, tokens), 1)
    before = (earlier < later).astype(f32).astype(bf16)
    rank = dot(count.astype(bf16), before, 1, 0)
    place = jnp.where(count > 0, rank, -1.0).astype(bf16)
    rep = expander(rows, groups, capacity)
    spread = dot(rep, place, 1, 0)
    row = lax.broadcasted_iota(jnp.int32, (rows, tokens), 0)
    owner = ((row.astype(f32) + 0.5) * (1.0 / capacity)).astype(jnp.int32)
    position = (row - owner * capacity).astype(f32)
    return (spread == position).astype(f32), rep


def slots_kernel(experts, capacity, topk, meta_ref, hot0_ref, hot1_ref, prob_ref):
    tokens = meta_ref.shape[2]
    me = lax.axis_index("expert")
    expert = lax.broadcasted_iota(jnp.int32, (experts, tokens), 0).astype(f32)
    own = meta_ref[me]
    lane = lax.broadcasted_iota(jnp.int32, prob_ref.shape, 1)
    columns = jnp.zeros(prob_ref.shape, f32)
    ranks = range(topk)
    for k, hot_ref in enumerate((hot0_ref, hot1_ref)):
        at = [k * topk + j for j in ranks]
        hot, _ = slot_masks([(own[i : i + 1, :] == expert).astype(f32) for i in at], capacity)
        hot_ref[...] = hot.astype(bf16)
        mine = me.astype(f32)
        named = [(meta_ref[:, i, :] == mine).astype(f32) for i in at]
        hot, rep = slot_masks(named, capacity)
        probs = sum(n * meta_ref[:, 2 * topk + i, :] for n, i in zip(named, at))
        column = jnp.sum(hot * dot(rep, probs.astype(bf16), 1, 0), axis=1, keepdims=True)
        columns = jnp.where(lane == k, column, columns)
    prob_ref[...] = columns.astype(bf16)


def block_masks(plane, capacity, ranks, ids, experts):
    tokens = ids.shape[1]
    row = lax.broadcasted_iota(jnp.int32, (len(experts), tokens), 0)
    expert = jnp.zeros(row.shape, f32)
    for i, offset in enumerate(experts):
        expert = jnp.where(row == i, other_of(plane, offset).astype(f32), expert)
    return slot_masks([(ids[i : i + 1, :] == expert).astype(f32) for i in ranks], capacity)[0]


def masks_kernel(plane, capacity, plans, meta_ref, *out_refs):
    for (ranks, blocks, experts), out_ref in zip(plans, out_refs):
        for s, block in enumerate(blocks):
            out_ref[s] = block_masks(
                plane, capacity, ranks, meta_ref[other_of(plane, block)], experts
            ).astype(bf16)


def select_kernel(plane, capacity, plan, meta_ref, *refs):
    ranks, sources, targets = plan
    raw_refs, out_refs = refs[: len(sources)], refs[len(sources) :]
    for s, source in enumerate(sources):
        hot = block_masks(plane, capacity, ranks, meta_ref[other_of(plane, source)], targets)
        picked = dot(hot.astype(bf16), raw_refs[s][...], 1, 0).astype(bf16)
        for i, out_ref in enumerate(out_refs):
            out_ref[s * capacity : (s + 1) * capacity, :] = picked[i * capacity : (i + 1) * capacity]


def own_select_kernel(plane, capacity, plan, tick, *refs):
    ranks, sources, targets = plan
    refs, (raw, sem) = refs[:-2], refs[-2:]
    count = len(sources)
    copies = [pltpu.make_async_copy(refs[count + s].at[tick], raw.at[s], sem.at[s]) for s in range(count)]
    for copy in copies:
        copy.start()
    hots = [block_masks(plane, capacity, ranks, refs[s][...], targets).astype(bf16) for s in range(count)]
    width = refs[-1].shape[1]
    for s in range(count):
        copies[s].wait()
        picked = dot(hots[s], raw[s], 1, 0).astype(bf16)
        at = slice(s * capacity, (s + 1) * capacity)
        for i, out_ref in enumerate(refs[2 * count + 1 : -HALVES]):
            out_ref[at, :] = picked[i * capacity : (i + 1) * capacity]
        for h, out_ref in enumerate(refs[-HALVES:]):
            out_ref[at, :] = picked[-capacity:, h * width : (h + 1) * width]


def own_picked(plane, capacity, plan, tick, metas, raws, pad):
    _, tokens, width = raws[0].shape
    count, rows = len(raws), len(plan[1]) * capacity
    outs = [shaped((rows, width), bf16)] * (len(plan[2]) - 1) + [shaped((rows, width // HALVES), bf16)] * HALVES
    return pl.pallas_call(
        functools.partial(own_select_kernel, plane, capacity, plan, tick),
        out_shape=[pad] + outs,
        in_specs=[pl.BlockSpec()] * count + [in_hbm(r) for r in raws],
        out_specs=[in_hbm(pad)] + [pl.BlockSpec()] * len(outs),
        scratch_shapes=[pltpu.VMEM((count, tokens, width), bf16), pltpu.SemaphoreType.DMA((count,))],
        compiler_params=pltpu.CompilerParams(vmem_limit_bytes=OWN_LIMIT),
        cost_estimate=cost([*metas, *raws], outs, 0),
    )(*metas, *raws)


def pick_own_kernel(hot_ref, raw_ref, out_ref):
    out_ref[...] = dot(hot_ref[0], raw_ref[...], 1, 0).astype(bf16)


def pick_kernel(capacity, hot_ref, own_ref, *refs):
    sources = hot_ref.shape[0]
    raw_refs, out_refs = refs[: sources - 1], refs[sources - 1 :]
    picked = [own_ref[...]]
    picked += [dot(hot_ref[s + 1], raw_ref[...], 1, 0).astype(bf16) for s, raw_ref in enumerate(raw_refs)]
    for s, rows in enumerate(picked):
        for i, out_ref in enumerate(out_refs):
            out_ref[s * capacity : (s + 1) * capacity, :] = rows[i * capacity : (i + 1) * capacity]


def gather_plan(plane, ranks, axis):
    return ranks, [plane.back(u) for u in plane.along(axis)], plane.across(axis)


def return_plan(plane, ranks, axis):
    return ranks, plane.along(axis), [plane.back(t) for t in plane.across(axis)]


def picked_rows(plane, capacity, ranks, axis, value, meta, hot=None):
    tokens, width = value.shape
    plan = gather_plan(plane, ranks, axis)
    raws = [plane.send(value, u) for u in plane.along(axis)]
    outs = [shaped((len(plan[1]) * capacity, width), bf16)] * len(plan[2])
    flops = 2 * tokens * width * capacity * len(plan[1]) * len(plan[2])
    if hot is None:
        return call(functools.partial(select_kernel, plane, capacity, plan), outs, meta, *raws, flops=flops)
    (own,) = call(pick_own_kernel, [shaped((hot.shape[1], width), bf16)], hot, raws[0], flops=LONG)
    return call(functools.partial(pick_kernel, capacity), outs, hot, own, *raws[1:], flops=flops)


def sent_rows(plane, axis, picked):
    return [plane.send(p, t) for p, t in zip(picked, plane.across(axis))], sent_layout(plane, axis)


def sent_layout(plane, axis):
    return [[plane.back(t, u) for u in plane.along(axis)] for t in plane.across(axis)]


def combine_parts_kernel(capacity, blocks, hot_ref, *refs):
    pieces, out_refs = refs[:-blocks], refs[-blocks:]
    for s, out_ref in enumerate(out_refs):
        rows = jnp.concatenate([p[s * capacity : (s + 1) * capacity, :] for p in pieces], axis=0)
        out_ref[...] = dot(hot_ref[s], rows, 0, 0).astype(out_ref.dtype)


def seed_kernel(first, g_ref, own_ref, out_ref):
    width = out_ref.shape[1]
    out_ref[...] = g_ref[:, first : first + width].astype(f32) + own_ref[...]


def add_kernel(own_ref, *refs):
    out_ref = refs[-1]
    total = own_ref[...]
    for ref in refs[:-1]:
        total = total + ref[...].astype(f32)
    out_ref[...] = total.astype(bf16)


def returned_rows(plane, capacity, axis, pieces, hot, g, first, after):
    width, tokens = pieces[0].shape[1], g.shape[0]
    pieces = [plane.send(p, t) for p, t in zip(pieces, plane.across(axis))]
    pieces = behind(pieces, after)
    along = plane.along(axis)
    outs = [shaped((tokens, width), bf16 if any(u) else f32) for u in along]
    own, *parts = call(
        functools.partial(combine_parts_kernel, capacity, len(along)), outs, hot, *pieces,
        flops=2 * hot.size * width,
    )
    sent = [plane.send(p, u) for p, u in zip(parts, along[1:])]
    (own,) = call(functools.partial(seed_kernel, first), [shaped((tokens, width), f32)], g, own, flops=LONG)
    return call(add_kernel, [shaped((tokens, width), bf16)], own, *sent)[0], parts


def behind(values, after):
    return lax.optimization_barrier((values, after))[0] if after else values


def spread_kernel(hot_ref, x_ref, out_ref):
    out_ref[...] = dot(hot_ref[...], x_ref[...], 1, 0).astype(bf16)


def spread(hot, x):
    outs = [shaped((hot.shape[0], x.shape[1]), bf16)]
    return call(spread_kernel, outs, hot, x, flops=2 * hot.size * x.shape[1])[0]


def exchange(rows, experts):
    width = rows.shape[1]
    pieces = rows.reshape(experts, -1, width)
    arrived = lax.all_to_all(pieces, "expert", split_axis=0, concat_axis=0, tiled=True)
    return arrived.reshape(-1, width)


def combine_kernel(first, hot_ref, back_ref, g_ref, out_ref):
    width = out_ref.shape[1]
    summed = dot(hot_ref[...], back_ref[...], 0, 0)
    out_ref[...] = (g_ref[:, first : first + width].astype(f32) + summed).astype(bf16)


def arrange(plane, capacity, groups, refs, out_ref):
    refs = list(refs)
    for first, layout in groups:
        if layout is None:
            piece = refs.pop(0)
            out_ref[:, first : first + piece.shape[1]] = piece[...]
            continue
        for offsets in layout:
            piece = refs.pop(0)
            lanes = slice(first, first + piece.shape[1])
            for s, offset in enumerate(offsets):
                at = pl.multiple_of(other_of(plane, offset) * capacity, 16)
                out_ref[pl.ds(at, capacity), lanes] = piece[s * capacity : (s + 1) * capacity, :]


def gelu_parts(preact):
    cdf = 0.5 * (1.0 + lax.erf(preact * half_root))
    pdf = density_scale * jnp.exp(-0.5 * preact * preact)
    return preact * cdf, cdf + preact * pdf


class Copies:
    def __init__(self, sem):
        self.sem, self.started = sem, []

    def start(self, source, target):
        self.started.append(pltpu.make_async_copy(source, target, self.sem.at[len(self.started)]))
        self.started[-1].start()
        return self.started[-1]

    def wait(self):
        for copy in self.started:
            copy.wait()


def lanes_of(units):
    return -(-units // LANES) * LANES


def plate(pad_ref, n, lanes):
    return pad_ref.at[n, :, pl.ds(0, lanes)]


def preact_kernel(plane, capacity, groups, places, win_ref, _, *refs):
    pad_ref, hid_ref, slope_ref, x, hid, sem = refs[-6:]
    units, copies = win_ref.shape[0], Copies(sem)
    arrange(plane, capacity, groups, refs[:-6], x)
    copies.start(x, pad_ref.at[places[0]])
    activated, slope = gelu_parts(dot(x[...], win_ref[...], 1, 1))
    hidden = activated.astype(bf16)
    hid[:, :units] = hidden
    copies.start(hid, plate(pad_ref, places[1], hid.shape[1]))
    hid_ref[...] = hidden
    slope_ref[...] = slope
    copies.wait()


def preact(plane, capacity, groups, places, w_in, pad, *pieces):
    units = w_in.shape[0]
    rows, features = pad.shape[1:]
    return call(
        functools.partial(preact_kernel, plane, capacity, groups, places),
        [shaped(pad.shape, bf16), shaped((rows, units), bf16), shaped((rows, units), f32)],
        w_in, pad, *pieces, pad=1, pad_out=True,
        scratch=[pltpu.VMEM((rows, n), bf16) for n in (features, lanes_of(units))] + [pltpu.SemaphoreType.DMA((2,))],
    )


def first_preact_kernel(plane, capacity, groups, win_ref, *refs):
    x_ref, hid_ref, slope_ref = refs[-3:]
    arrange(plane, capacity, groups, refs[:-3], x_ref)
    activated, slope = gelu_parts(dot(x_ref[...], win_ref[...], 1, 1))
    hid_ref[:, : slope.shape[1]] = activated.astype(bf16)
    slope_ref[...] = slope


def first_kernel(plane, capacity, groups, plans, win_ref, wout_ref, hid_ref, slope_ref, prob_ref, *refs):
    refs, back = refs[:-1], refs[-1]
    pieces = sum(1 if plan is None else len(plan) for plan in plans)
    refs, back_refs = refs[:-pieces], list(refs[-pieces:])
    g_ref, gp_ref, cols_ref = refs[-3:]
    units = win_ref.shape[0]
    arrange(plane, capacity, groups, refs[:-3], g_ref)
    pulled = dot(g_ref[...], wout_ref[...], 1, 1)
    grad_pre = (prob_ref[:, 0:1].astype(f32) * pulled * slope_ref[...]).astype(bf16)
    gp_ref[:, :units] = grad_pre
    score = jnp.sum(hid_ref[:, :units].astype(f32) * pulled, axis=1, keepdims=True)
    cols_ref[:, :LANES] = prob_ref[...]
    cols_ref[:, LANES:] = jnp.broadcast_to(score, (score.shape[0], LANES)).astype(bf16)
    width = back.shape[1]
    for h, plan in enumerate(plans):
        back[...] = dot(grad_pre, win_ref[:, h * width : (h + 1) * width], 1, 0).astype(bf16)
        if plan is None:
            back_refs.pop(0)[...] = back[...]
            continue
        for blocks in plan:
            out_ref = back_refs.pop(0)
            for s, block in enumerate(blocks):
                at = pl.multiple_of(other_of(plane, block) * capacity, 16)
                out_ref[s * capacity : (s + 1) * capacity, :] = back[pl.ds(at, capacity), :]


def stash_kernel(places, *refs):
    pad_ref, sem = refs[-2:]
    copies = Copies(sem)
    for n, ref in zip(places, refs):
        copies.start(ref, plate(pad_ref, n, ref.shape[1]))
    copies.wait()


def stash(pad, places, *arrays):
    return pl.pallas_call(
        functools.partial(stash_kernel, places),
        out_shape=shaped(pad.shape, bf16),
        in_specs=[pl.BlockSpec()] * len(arrays) + [in_hbm(pad)],
        out_specs=in_hbm(pad),
        compiler_params=pltpu.CompilerParams(vmem_limit_bytes=VMEM_LIMIT),
        scratch_shapes=[pltpu.SemaphoreType.DMA((len(arrays),))],
        input_output_aliases={len(arrays): 0},
        cost_estimate=pl.CostEstimate(flops=0, bytes_accessed=0, transcendentals=0),
    )(*arrays, pad)


def weighted(prob_ref, k, g):
    return (prob_ref[:, k : k + 1].astype(f32) * g.astype(f32)).astype(bf16)


def early_kernel(plane, capacity, groups, wout_ref, hid1_ref, pad_ref, *refs):
    pulled_ref, gout_ref, g, g0, hid0, cols, sem = refs[-7:]
    units, copies = wout_ref.shape[0], Copies(sem)
    copies.start(plate(pad_ref, G0, g0.shape[1]), g0)
    copies.start(plate(pad_ref, HID0, hid0.shape[1]), hid0)
    copies.start(plate(pad_ref, COLS, cols.shape[1]), cols)
    arrange(plane, capacity, groups, refs[:-7], g)
    pulled_ref[...] = dot(g[...], wout_ref[...], 1, 1)
    copies.wait()
    y = jnp.concatenate([weighted(cols, 0, g0[...]), weighted(cols, 1, g[...])], axis=0)
    hid = jnp.concatenate([hid0[:, :units], hid1_ref[...]], axis=0)
    gout_ref[...] = dot(hid, y, 0, 0).astype(bf16)


def early(plane, capacity, groups, w_out, hid1, pad, *pieces):
    rows, units = hid1.shape
    features = w_out.shape[1]
    width = features // HALVES
    args = (w_out, hid1, *pieces)
    outs = [shaped((rows, units), f32), shaped((units, features), bf16)]
    whole = lambda a: pl.BlockSpec(a.shape, lambda i: (0, 0))
    first = lambda a: pl.BlockSpec((a.shape[0], width), lambda i: (0, 0))
    return pl.pallas_call(
        functools.partial(early_kernel, plane, capacity, groups),
        grid=(1,),
        out_shape=outs,
        in_specs=[first(w_out), whole(hid1), in_hbm(pad)] + [whole(p) for p in pieces],
        out_specs=[whole(outs[0]), first(outs[1])],
        scratch_shapes=[pltpu.VMEM((rows, n), bf16) for n in (width, width, lanes_of(units), 2 * LANES)]
        + [pltpu.SemaphoreType.DMA((3,))],
        compiler_params=pltpu.CompilerParams(vmem_limit_bytes=VMEM_LIMIT),
        cost_estimate=cost(args, outs, 3 * units * rows * features),
    )(w_out, hid1, pad, *pieces)


def second_kernel(plane, capacity, groups, first, wout_ref, hid_ref, slope_ref, pulled_ref, pad_ref, *refs):
    g_ref, gp_ref, score_ref, cols, sem = refs[-5:]
    units, copies = wout_ref.shape[0], Copies(sem)
    copies.start(plate(pad_ref, COLS, cols.shape[1]), cols)
    arrange(plane, capacity, groups, refs[:-5], g_ref)
    pulled = pulled_ref[...] + dot(g_ref[...], wout_ref[:, first:], 1, 1)
    copies.wait()
    gp_ref[:, :units] = (cols[:, 1:2].astype(f32) * pulled * slope_ref[...]).astype(bf16)
    score = jnp.sum(hid_ref[...].astype(f32) * pulled, axis=1, keepdims=True)
    lane = lax.broadcasted_iota(jnp.int32, score_ref.shape, 1)
    both = jnp.where(lane == 0, cols[:, LANES:].astype(f32), jnp.where(lane == 1, score, 0.0))
    score_ref[...] = both.astype(bf16)


def late_kernel(width, part, units, _, pad_ref, g1_ref, gp1_ref, *refs):
    gin_ref, gout_ref, cols, x, g, hid, gp, held, sem, out_sem = refs
    rows, features = pad_ref.shape[1:]
    skip = features - part
    copies = Copies(sem)
    top, low = pl.ds(0, rows), pl.ds(rows, rows)
    lanes = lambda at: pl.ds(at, width)
    first = [copies.start(plate(pad_ref, GP0, gp.shape[1]), gp.at[top, :])]
    tiles = []
    for at in range(0, features, width):
        tiles.append(
            [copies.start(pad_ref.at[n, :, lanes(at)], x.at[to, lanes(at)]) for n, to in ((X0, top), (X1, low))]
        )
    then = [copies.start(plate(pad_ref, n, hid.shape[1]), hid.at[at, :]) for n, at in ((HID0, top), (HID1, low))]
    then.append(copies.start(plate(pad_ref, COLS, cols.shape[1]), cols))
    then.append(copies.start(pad_ref.at[G0, :, pl.ds(skip, part)], g))
    sent = []

    def store(n, value, out_ref, at):
        slot = n % held.shape[0]
        if n >= held.shape[0]:
            sent[n - held.shape[0]].wait()
        held[slot] = value.astype(bf16)
        sent.append(pltpu.make_async_copy(held.at[slot], out_ref.at[:, lanes(at)], out_sem.at[slot]))
        sent[-1].start()

    gp[rows:, :] = gp1_ref[...]
    for copy in first:
        copy.wait()
    for n, tile in enumerate(tiles):
        for copy in tile:
            copy.wait()
        at = n * width
        store(n, dot(gp[:, :units], x[:, at : at + width], 0, 0), gin_ref, at)
    for copy in then:
        copy.wait()
    for n in range(part // width):
        at = n * width
        y0 = weighted(cols, 0, g[:, at : at + width])
        y1 = weighted(cols, 1, g1_ref[:, at : at + width])
        store(len(tiles) + n, dot(hid[:, :units], jnp.concatenate([y0, y1], axis=0), 0, 0), gout_ref, skip + at)
    for copy in sent[-held.shape[0] :]:
        copy.wait()


def late(width, done, pad, g1, gp1):
    units, features = done.shape
    rows, part = g1.shape
    outs = [shaped((units, features), bf16)] * 2
    return pl.pallas_call(
        functools.partial(late_kernel, width, part, units),
        out_shape=outs,
        in_specs=[in_hbm(done), in_hbm(pad), pl.BlockSpec(), pl.BlockSpec()],
        out_specs=[in_hbm(o) for o in outs],
        scratch_shapes=[pltpu.VMEM((rows, 2 * LANES), bf16), pltpu.VMEM((2 * rows, features), bf16)]
        + [pltpu.VMEM((rows, part), bf16)]
        + [pltpu.VMEM((2 * rows, lanes_of(units)), bf16)] * 2
        + [pltpu.VMEM((3, units, width), bf16)]
        + [pltpu.SemaphoreType.DMA((7 + 2 * (features // width),)), pltpu.SemaphoreType.DMA((3,))],
        input_output_aliases={0: 1},
        compiler_params=pltpu.CompilerParams(vmem_limit_bytes=LATE_LIMIT),
        cost_estimate=cost((), outs, 6 * units * rows * features),
    )(done, pad, g1, gp1)


def collect_kernel(experts, capacity, topk, meta_ref, hot0_ref, hot1_ref, score_ref, out_ref):
    tokens = meta_ref.shape[2]
    rep = expander(experts * capacity, experts, capacity)
    expert = lax.broadcasted_iota(jnp.int32, (experts, tokens), 0).astype(f32)
    own = meta_ref[lax.axis_index("expert")]
    for k, hot_ref in enumerate((hot0_ref, hot1_ref)):
        placed = hot_ref[...].astype(f32) * score_ref[:, k : k + 1].astype(f32)
        by_expert = dot(rep, placed.astype(bf16), 0, 0)
        for j in range(topk):
            i = k * topk + j
            picked = jnp.where(own[i : i + 1, :] == expert, by_expert, 0.0)
            out_ref[i : i + 1, :] = jnp.sum(picked, axis=0, keepdims=True).astype(bf16)


def body(inputs, entering, weight_in, weight_out, gate_probs, expert_ids):
    experts = lax.axis_size("expert")
    segments = lax.axis_size("segment")
    tokens, features = entering.shape[1:]
    ticks, topk = expert_ids.shape[1], expert_ids.shape[3]
    units = weight_in.shape[2]
    capacity = 3 * tokens * topk // (2 * experts)
    rows = experts * capacity
    plane = Plane(experts)
    matmul = 2 * rows * units * features
    half = features // HALVES
    w_in, w_out = weight_in[0, 0], weight_out[0, 0]
    g0 = entering[0]

    x0 = inputs[0, 0]
    expert_ids, gate_probs = behind((expert_ids, gate_probs), [x0])
    ids = jnp.transpose(expert_ids[0], (0, 2, 1)).reshape(ticks * topk, tokens)
    probs = jnp.transpose(gate_probs[0], (0, 2, 1)).reshape(ticks * topk, tokens)
    meta = jnp.concatenate([ids.astype(f32), probs.astype(f32)], axis=0)
    own_meta = meta
    meta = jnp.broadcast_to(meta[None], (experts,) + meta.shape)
    meta = lax.all_to_all(meta, "expert", split_axis=0, concat_axis=0, tiled=True)
    hot0, hot1, prob = call(
        functools.partial(slots_kernel, experts, capacity, topk),
        [shaped((rows, tokens), bf16)] * 2 + [shaped((rows, LANES), bf16)],
        meta,
    )
    plate_bytes = rows * features * 2
    pad = shaped((max(9, -(-PAD_BYTES // plate_bytes)), rows, features), bf16)

    stepped = capacity % 16 == 0
    ranks = [list(range(k * topk, (k + 1) * topk)) for k in range(ticks)]
    pick = functools.partial(picked_rows, plane, capacity)
    if stepped:
        metas = [own_meta, plane.send(own_meta, (0, 0, 1))]
        x1 = [inputs[0], plane.send(inputs[0], (0, 0, 1))]
        pad, *x1 = own_picked(plane, capacity, gather_plan(plane, ranks[1], 2), 1, metas, x1, pad)
        x1_near, _ = sent_rows(plane, 2, x1[:-HALVES])
        *near_layout, rest_layout = sent_layout(plane, 2)
        x1_groups = [(0, near_layout)] + [(h * half, [rest_layout]) for h in range(HALVES)]
        x1_rest = x1[-HALVES:]
        select_meta = behind(meta, x1)
        x0, x0_layout = sent_rows(plane, 1, pick(ranks[0], 1, x0, select_meta))
        *g0_first, g0_last = pick(ranks[0], 0, g0, select_meta)
        g0_in, g0_layout = sent_rows(plane, 0, [*g0_first, behind(g0_last, [*x1_near, prob])])
        plans = [return_plan(plane, ranks[0], axis) for axis in AXES]
        plans += [gather_plan(plane, ranks[1], axis) for axis in AXES]
        shapes = [shaped((len(b), len(e) * capacity, tokens), bf16) for _, b, e in plans]
        masks = call(functools.partial(masks_kernel, plane, capacity, plans), shapes, meta)
        back_plans = [[[plane.back(plane.back(t, u)) for u in plane.along(axis)] for t in plane.across(axis)] for axis in AXES]
        shapes = [shaped((len(blocks) * capacity, half), bf16) for plan in back_plans for blocks in plan]
    else:
        (pad,) = call(lambda meta_ref, _: None, [pad], meta, pad_out=True)
        x0, x0_layout = [exchange(spread(hot0, x0), experts)], None
        g0_in, g0_layout = [exchange(spread(hot0, g0), experts)], None
        back_plans = [None] * HALVES
        shapes = [shaped((rows, half), bf16)] * HALVES

    if stepped:
        arrived = [*x0, *g0_in]
        x0 = behind(x0, x1_near)
    wide = lanes_of(units)
    vmem = lambda n: pltpu.VMEM((rows, n), bf16)
    x0, hid0, slope0 = call(
        functools.partial(first_preact_kernel, plane, capacity, [(0, x0_layout)]),
        [shaped((rows, features), bf16), shaped((rows, wide), bf16), shaped((rows, units), f32)], w_in, *x0,
    )
    g0_in, gp0, cols, *backs = call(
        functools.partial(first_kernel, plane, capacity, [(0, g0_layout)], back_plans),
        [shaped((rows, n), bf16) for n in (features, wide, 2 * LANES)] + shapes,
        w_in, w_out, hid0, slope0, prob, *g0_in, scratch=[vmem(half)],
    )
    pad = stash(pad, (X0, G0, HID0, GP0, COLS), x0, g0_in, hid0, gp0, cols)
    leaving, after = [], []
    if stepped:
        far = plane.across(2)[-1]
        x1_rest[0] = plane.send(behind(x1_rest[0], [hid0, *arrived]), far)
        after = [pad, x1_rest[0]]
    for h, axis in enumerate(AXES):
        if stepped:
            count = len(plane.across(axis))
            pieces, backs = backs[:count], backs[count:]
            out, parts = returned_rows(plane, capacity, axis, pieces, masks[h], g0, h * half, after)
        else:
            (out,) = call(
                functools.partial(combine_kernel, h * half), [shaped((tokens, half), bf16)],
                hot0, exchange(backs[h], experts), g0, flops=2 * rows * tokens * half,
            )
        leaving.append(out)
        after = [out]

    if stepped:
        x1_rest[1:] = [plane.send(p, far) for p in behind(x1_rest[1:], leaving[:1])]
        x1 = x1_near + x1_rest
    else:
        x1, x1_groups = [exchange(spread(hot1, inputs[0, 1]), experts)], [(0, None)]
    parts, after = [], []
    for h, axis in enumerate(AXES):
        arrived = lax.ppermute(leaving[h], "segment", [(i, i - 1) for i in range(1, segments)])
        arrived = behind(arrived, after)
        if stepped:
            picked = pick(ranks[1], axis, arrived, meta, masks[HALVES + h])
            pieces, layout = sent_rows(plane, axis, picked)
            after = picked
        else:
            pieces, layout = [exchange(spread(hot1, arrived), experts)], None
        parts.append((pieces, [(0, layout)]))
    x1 = behind(x1, after)
    pad, hid1, slope1 = preact(plane, capacity, x1_groups, (X1, HID1), w_in, pad, *x1)
    pulled, gout = early(plane, capacity, parts[0][1], w_out, hid1, pad, *parts[0][0])
    pieces = behind(parts[1][0], [pulled])
    g1, gp1, scores = call(
        functools.partial(second_kernel, plane, capacity, parts[1][1], half),
        [shaped((rows, half), bf16), shaped((rows, wide), bf16), shaped((rows, LANES), bf16)],
        w_out, hid1, slope1, pulled, pad, *pieces, flops=matmul // 2, pad=4,
        scratch=[vmem(2 * LANES), pltpu.SemaphoreType.DMA((1,))],
    )
    scores = exchange(scores, experts)
    grad_in, grad_out = late(features // TILES, gout, pad, g1, gp1)
    (prob_grads,) = call(
        functools.partial(collect_kernel, experts, capacity, topk),
        [shaped((ticks * topk, tokens), bf16)], meta, hot0, hot1, scores,
    )
    prob_grads = jnp.transpose(prob_grads.reshape(ticks, topk, tokens), (0, 2, 1))
    return grad_in[None, None], grad_out[None, None], prob_grads[None]


def solution(mesh):
    return jax.shard_map(
        body,
        mesh=mesh,
        in_specs=(
            P("segment", None, "expert", None),
            P("segment", "expert", None),
            P("segment", "expert", None, None),
            P("segment", "expert", None, None),
            P("segment", None, "expert", None),
            P("segment", None, "expert", None),
        ),
        out_specs=(
            P("segment", "expert", None, None),
            P("segment", "expert", None, None),
            P("segment", None, "expert", None),
        ),
        check_vma=False,
    )
```

```python
import functools

import jax
import jax.numpy as jnp
from jax import lax
from jax.experimental import pallas as pl
from jax.experimental.pallas import tpu as pltpu
from jax.sharding import PartitionSpec as P

half_root = 0.7071067811865476
density_scale = 0.3989422804014327
LANES = 128
AXES = (2, 2)
HALVES = len(AXES)
TILES = 2
LONG = 10**11
OWN_LIMIT = 60 * 1024 * 1024
LATE_LIMIT = 32 * 1024 * 1024
X0, G0, X1, G1, HID0, HID1, GP0, GP1, COLS = range(9)
PAD_BYTES = 66 * 1024 * 1024
VMEM_LIMIT = 20 * 1024 * 1024
f32 = jnp.float32
bf16 = jnp.bfloat16


def dot(a, b, ca, cb):
    return lax.dot_general(a, b, (((ca,), (cb,)), ((), ())), preferred_element_type=f32)


def shaped(shape, dtype):
    return jax.ShapeDtypeStruct(shape, dtype)


def cost(args, outs, flops):
    size = sum(a.size * a.dtype.itemsize for a in list(args) + list(outs))
    return pl.CostEstimate(flops=flops if flops == LONG else 0, bytes_accessed=size * 64, transcendentals=0)


def in_hbm(ref):
    return pl.BlockSpec(memory_space=pltpu.HBM)


def call(kernel, outs, *args, flops=0, scratch=(), pad=None, pad_out=False):
    specs = [pl.BlockSpec() if n != pad else in_hbm(a) for n, a in enumerate(args)]
    return pl.pallas_call(
        kernel,
        out_shape=outs,
        in_specs=specs,
        out_specs=[in_hbm(o) if pad_out and n == 0 else pl.BlockSpec() for n, o in enumerate(outs)],
        input_output_aliases={pad: 0} if pad is not None and pad_out else {},
        scratch_shapes=scratch,
        compiler_params=pltpu.CompilerParams(vmem_limit_bytes=VMEM_LIMIT),
        cost_estimate=cost(args, outs, flops),
    )(*args)


class Plane:
    def __init__(self, experts):
        chips = experts // 2
        across = next(n for n in range(int(chips**0.5), 0, -1) if chips % n == 0)
        self.size = (chips // across, across, 2)
        self.experts = experts

    def other(self, i, offset):
        _, across, cores = self.size
        coords = (i // (across * cores), (i // cores) % across, i % cores)
        a, b, c = ((p + o) % n for p, o, n in zip(coords, offset, self.size))
        return (a * across + b) * cores + c

    def back(self, *offsets):
        return tuple(-sum(o) % n for o, n in zip(zip(*offsets), self.size))

    def along(self, axis):
        return [tuple(n if d == axis else 0 for d in range(3)) for n in range(self.size[axis])]

    def across(self, axis):
        spans = [range(1 if d == axis else n) for d, n in enumerate(self.size)]
        return [(a, b, c) for a in spans[0] for b in spans[1] for c in spans[2]]

    def send(self, value, offset):
        if not any(offset):
            return value
        route = [(i, self.other(i, offset)) for i in range(self.experts)]
        return lax.ppermute(value, "expert", route)


def other_of(plane, offset):
    _, across, cores = plane.size
    i = lax.axis_index("expert")
    coords = (lax.div(i, across * cores), lax.rem(lax.div(i, cores), across), lax.rem(i, cores))
    a, b, c = (lax.rem(p + o, n) for p, o, n in zip(coords, offset, plane.size))
    return (a * across + b) * cores + c


def expander(rows, groups, capacity):
    first = lax.broadcasted_iota(jnp.int32, (rows, groups), 1) * capacity
    row = lax.broadcasted_iota(jnp.int32, (rows, groups), 0)
    return ((row >= first) & (row < first + capacity)).astype(f32).astype(bf16)


def slot_masks(named, capacity):
    count = sum(named)
    groups, tokens = count.shape
    rows = groups * capacity
    earlier = lax.broadcasted_iota(jnp.int32, (tokens, tokens), 0)
    later = lax.broadcasted_iota(jnp.int32, (tokens, tokens), 1)
    before = (earlier < later).astype(f32).astype(bf16)
    rank = dot(count.astype(bf16), before, 1, 0)
    place = jnp.where(count > 0, rank, -1.0).astype(bf16)
    rep = expander(rows, groups, capacity)
    spread = dot(rep, place, 1, 0)
    row = lax.broadcasted_iota(jnp.int32, (rows, tokens), 0)
    owner = ((row.astype(f32) + 0.5) * (1.0 / capacity)).astype(jnp.int32)
    position = (row - owner * capacity).astype(f32)
    return (spread == position).astype(f32), rep


def slots_kernel(experts, capacity, topk, meta_ref, hot0_ref, hot1_ref, prob_ref):
    tokens = meta_ref.shape[2]
    me = lax.axis_index("expert")
    expert = lax.broadcasted_iota(jnp.int32, (experts, tokens), 0).astype(f32)
    own = meta_ref[me]
    lane = lax.broadcasted_iota(jnp.int32, prob_ref.shape, 1)
    columns = jnp.zeros(prob_ref.shape, f32)
    ranks = range(topk)
    for k, hot_ref in enumerate((hot0_ref, hot1_ref)):
        at = [k * topk + j for j in ranks]
        hot, _ = slot_masks([(own[i : i + 1, :] == expert).astype(f32) for i in at], capacity)
        hot_ref[...] = hot.astype(bf16)
        mine = me.astype(f32)
        named = [(meta_ref[:, i, :] == mine).astype(f32) for i in at]
        hot, rep = slot_masks(named, capacity)
        probs = sum(n * meta_ref[:, 2 * topk + i, :] for n, i in zip(named, at))
        column = jnp.sum(hot * dot(rep, probs.astype(bf16), 1, 0), axis=1, keepdims=True)
        columns = jnp.where(lane == k, column, columns)
    prob_ref[...] = columns.astype(bf16)


def block_masks(plane, capacity, ranks, ids, experts):
    tokens = ids.shape[1]
    row = lax.broadcasted_iota(jnp.int32, (len(experts), tokens), 0)
    expert = jnp.zeros(row.shape, f32)
    for i, offset in enumerate(experts):
        expert = jnp.where(row == i, other_of(plane, offset).astype(f32), expert)
    return slot_masks([(ids[i : i + 1, :] == expert).astype(f32) for i in ranks], capacity)[0]


def masks_kernel(plane, capacity, plans, meta_ref, *out_refs):
    for (ranks, blocks, experts), out_ref in zip(plans, out_refs):
        for s, block in enumerate(blocks):
            out_ref[s] = block_masks(
                plane, capacity, ranks, meta_ref[other_of(plane, block)], experts
            ).astype(bf16)


def select_kernel(plane, capacity, plan, meta_ref, *refs):
    ranks, sources, targets = plan
    raw_refs, out_refs = refs[: len(sources)], refs[len(sources) :]
    for s, source in enumerate(sources):
        hot = block_masks(plane, capacity, ranks, meta_ref[other_of(plane, source)], targets)
        picked = dot(hot.astype(bf16), raw_refs[s][...], 1, 0).astype(bf16)
        for i, out_ref in enumerate(out_refs):
            out_ref[s * capacity : (s + 1) * capacity, :] = picked[i * capacity : (i + 1) * capacity]


def own_select_kernel(plane, capacity, plan, tick, *refs):
    ranks, sources, targets = plan
    refs, (raw, sem) = refs[:-2], refs[-2:]
    count = len(sources)
    copies = [pltpu.make_async_copy(refs[count + s].at[tick], raw.at[s], sem.at[s]) for s in range(count)]
    for copy in copies:
        copy.start()
    hots = [block_masks(plane, capacity, ranks, refs[s][...], targets).astype(bf16) for s in range(count)]
    width = refs[-1].shape[1]
    for s in range(count):
        copies[s].wait()
        picked = dot(hots[s], raw[s], 1, 0).astype(bf16)
        at = slice(s * capacity, (s + 1) * capacity)
        for i, out_ref in enumerate(refs[2 * count + 1 : -HALVES]):
            out_ref[at, :] = picked[i * capacity : (i + 1) * capacity]
        for h, out_ref in enumerate(refs[-HALVES:]):
            out_ref[at, :] = picked[-capacity:, h * width : (h + 1) * width]


def own_picked(plane, capacity, plan, tick, metas, raws, pad):
    _, tokens, width = raws[0].shape
    count, rows = len(raws), len(plan[1]) * capacity
    outs = [shaped((rows, width), bf16)] * (len(plan[2]) - 1) + [shaped((rows, width // HALVES), bf16)] * HALVES
    return pl.pallas_call(
        functools.partial(own_select_kernel, plane, capacity, plan, tick),
        out_shape=[pad] + outs,
        in_specs=[pl.BlockSpec()] * count + [in_hbm(r) for r in raws],
        out_specs=[in_hbm(pad)] + [pl.BlockSpec()] * len(outs),
        scratch_shapes=[pltpu.VMEM((count, tokens, width), bf16), pltpu.SemaphoreType.DMA((count,))],
        compiler_params=pltpu.CompilerParams(vmem_limit_bytes=OWN_LIMIT),
        cost_estimate=cost([*metas, *raws], outs, 0),
    )(*metas, *raws)


def pick_own_kernel(hot_ref, raw_ref, out_ref):
    out_ref[...] = dot(hot_ref[0], raw_ref[...], 1, 0).astype(bf16)


def pick_kernel(capacity, hot_ref, own_ref, *refs):
    sources = hot_ref.shape[0]
    raw_refs, out_refs = refs[: sources - 1], refs[sources - 1 :]
    picked = [own_ref[...]]
    picked += [dot(hot_ref[s + 1], raw_ref[...], 1, 0).astype(bf16) for s, raw_ref in enumerate(raw_refs)]
    for s, rows in enumerate(picked):
        for i, out_ref in enumerate(out_refs):
            out_ref[s * capacity : (s + 1) * capacity, :] = rows[i * capacity : (i + 1) * capacity]


def gather_plan(plane, ranks, axis):
    return ranks, [plane.back(u) for u in plane.along(axis)], plane.across(axis)


def return_plan(plane, ranks, axis):
    return ranks, plane.along(axis), [plane.back(t) for t in plane.across(axis)]


def picked_rows(plane, capacity, ranks, axis, value, meta, hot=None):
    tokens, width = value.shape
    plan = gather_plan(plane, ranks, axis)
    raws = [plane.send(value, u) for u in plane.along(axis)]
    outs = [shaped((len(plan[1]) * capacity, width), bf16)] * len(plan[2])
    flops = 2 * tokens * width * capacity * len(plan[1]) * len(plan[2])
    if hot is None:
        return call(functools.partial(select_kernel, plane, capacity, plan), outs, meta, *raws, flops=flops)
    (own,) = call(pick_own_kernel, [shaped((hot.shape[1], width), bf16)], hot, raws[0], flops=LONG)
    return call(functools.partial(pick_kernel, capacity), outs, hot, own, *raws[1:], flops=flops)


def sent_rows(plane, axis, picked):
    return [plane.send(p, t) for p, t in zip(picked, plane.across(axis))], sent_layout(plane, axis)


def sent_layout(plane, axis):
    return [[plane.back(t, u) for u in plane.along(axis)] for t in plane.across(axis)]


def combine_parts_kernel(capacity, blocks, hot_ref, *refs):
    pieces, out_refs = refs[:-blocks], refs[-blocks:]
    for s, out_ref in enumerate(out_refs):
        rows = jnp.concatenate([p[s * capacity : (s + 1) * capacity, :] for p in pieces], axis=0)
        out_ref[...] = dot(hot_ref[s], rows, 0, 0).astype(out_ref.dtype)


def seed_kernel(first, g_ref, own_ref, out_ref):
    width = out_ref.shape[1]
    out_ref[...] = g_ref[:, first : first + width].astype(f32) + own_ref[...]


def add_kernel(own_ref, *refs):
    out_ref = refs[-1]
    total = own_ref[...]
    for ref in refs[:-1]:
        total = total + ref[...].astype(f32)
    out_ref[...] = total.astype(bf16)


def returned_rows(plane, capacity, axis, pieces, hot, g, first, after):
    width, tokens = pieces[0].shape[1], g.shape[0]
    pieces = [plane.send(p, t) for p, t in zip(pieces, plane.across(axis))]
    pieces = behind(pieces, after)
    along = plane.along(axis)
    outs = [shaped((tokens, width), bf16 if any(u) else f32) for u in along]
    own, *parts = call(
        functools.partial(combine_parts_kernel, capacity, len(along)), outs, hot, *pieces,
        flops=2 * hot.size * width,
    )
    sent = [plane.send(p, u) for p, u in zip(parts, along[1:])]
    (own,) = call(functools.partial(seed_kernel, first), [shaped((tokens, width), f32)], g, own, flops=LONG)
    return call(add_kernel, [shaped((tokens, width), bf16)], own, *sent)[0], parts


def behind(values, after):
    return lax.optimization_barrier((values, after))[0] if after else values


def spread_kernel(hot_ref, x_ref, out_ref):
    out_ref[...] = dot(hot_ref[...], x_ref[...], 1, 0).astype(bf16)


def spread(hot, x):
    outs = [shaped((hot.shape[0], x.shape[1]), bf16)]
    return call(spread_kernel, outs, hot, x, flops=2 * hot.size * x.shape[1])[0]


def exchange(rows, experts):
    width = rows.shape[1]
    pieces = rows.reshape(experts, -1, width)
    arrived = lax.all_to_all(pieces, "expert", split_axis=0, concat_axis=0, tiled=True)
    return arrived.reshape(-1, width)


def combine_kernel(first, hot_ref, back_ref, g_ref, out_ref):
    width = out_ref.shape[1]
    summed = dot(hot_ref[...], back_ref[...], 0, 0)
    out_ref[...] = (g_ref[:, first : first + width].astype(f32) + summed).astype(bf16)


def arrange(plane, capacity, groups, refs, out_ref):
    refs = list(refs)
    for first, layout in groups:
        if layout is None:
            piece = refs.pop(0)
            out_ref[:, first : first + piece.shape[1]] = piece[...]
            continue
        for offsets in layout:
            piece = refs.pop(0)
            lanes = slice(first, first + piece.shape[1])
            for s, offset in enumerate(offsets):
                at = pl.multiple_of(other_of(plane, offset) * capacity, 16)
                out_ref[pl.ds(at, capacity), lanes] = piece[s * capacity : (s + 1) * capacity, :]


def gelu_parts(preact):
    cdf = 0.5 * (1.0 + lax.erf(preact * half_root))
    pdf = density_scale * jnp.exp(-0.5 * preact * preact)
    return preact * cdf, cdf + preact * pdf


class Copies:
    def __init__(self, sem):
        self.sem, self.started = sem, []

    def start(self, source, target):
        self.started.append(pltpu.make_async_copy(source, target, self.sem.at[len(self.started)]))
        self.started[-1].start()
        return self.started[-1]

    def wait(self):
        for copy in self.started:
            copy.wait()


def lanes_of(units):
    return -(-units // LANES) * LANES


def plate(pad_ref, n, lanes):
    return pad_ref.at[n, :, pl.ds(0, lanes)]


def preact_kernel(plane, capacity, groups, places, win_ref, _, *refs):
    pad_ref, hid_ref, slope_ref, x, hid, sem = refs[-6:]
    units, copies = win_ref.shape[0], Copies(sem)
    arrange(plane, capacity, groups, refs[:-6], x)
    copies.start(x, pad_ref.at[places[0]])
    activated, slope = gelu_parts(dot(x[...], win_ref[...], 1, 1))
    hidden = activated.astype(bf16)
    hid[:, :units] = hidden
    copies.start(hid, plate(pad_ref, places[1], hid.shape[1]))
    hid_ref[...] = hidden
    slope_ref[...] = slope
    copies.wait()


def preact(plane, capacity, groups, places, w_in, pad, *pieces):
    units = w_in.shape[0]
    rows, features = pad.shape[1:]
    return call(
        functools.partial(preact_kernel, plane, capacity, groups, places),
        [shaped(pad.shape, bf16), shaped((rows, units), bf16), shaped((rows, units), f32)],
        w_in, pad, *pieces, pad=1, pad_out=True,
        scratch=[pltpu.VMEM((rows, n), bf16) for n in (features, lanes_of(units))] + [pltpu.SemaphoreType.DMA((2,))],
    )


def first_preact_kernel(plane, capacity, groups, win_ref, *refs):
    x_ref, hid_ref, slope_ref = refs[-3:]
    arrange(plane, capacity, groups, refs[:-3], x_ref)
    activated, slope = gelu_parts(dot(x_ref[...], win_ref[...], 1, 1))
    hid_ref[:, : slope.shape[1]] = activated.astype(bf16)
    slope_ref[...] = slope


def first_kernel(plane, capacity, groups, plans, win_ref, wout_ref, hid_ref, slope_ref, prob_ref, *refs):
    refs, back = refs[:-1], refs[-1]
    pieces = sum(1 if plan is None else len(plan) for plan in plans)
    refs, back_refs = refs[:-pieces], list(refs[-pieces:])
    g_ref, gp_ref, cols_ref = refs[-3:]
    units = win_ref.shape[0]
    arrange(plane, capacity, groups, refs[:-3], g_ref)
    pulled = dot(g_ref[...], wout_ref[...], 1, 1)
    grad_pre = (prob_ref[:, 0:1].astype(f32) * pulled * slope_ref[...]).astype(bf16)
    gp_ref[:, :units] = grad_pre
    score = jnp.sum(hid_ref[:, :units].astype(f32) * pulled, axis=1, keepdims=True)
    cols_ref[:, :LANES] = prob_ref[...]
    cols_ref[:, LANES:] = jnp.broadcast_to(score, (score.shape[0], LANES)).astype(bf16)
    width = back.shape[1]
    for h, plan in enumerate(plans):
        back[...] = dot(grad_pre, win_ref[:, h * width : (h + 1) * width], 1, 0).astype(bf16)
        if plan is None:
            back_refs.pop(0)[...] = back[...]
            continue
        for blocks in plan:
            out_ref = back_refs.pop(0)
            for s, block in enumerate(blocks):
                at = pl.multiple_of(other_of(plane, block) * capacity, 16)
                out_ref[s * capacity : (s + 1) * capacity, :] = back[pl.ds(at, capacity), :]


def stash_kernel(places, *refs):
    pad_ref, sem = refs[-2:]
    copies = Copies(sem)
    for n, ref in zip(places, refs):
        copies.start(ref, plate(pad_ref, n, ref.shape[1]))
    copies.wait()


def stash(pad, places, *arrays):
    return pl.pallas_call(
        functools.partial(stash_kernel, places),
        out_shape=shaped(pad.shape, bf16),
        in_specs=[pl.BlockSpec()] * len(arrays) + [in_hbm(pad)],
        out_specs=in_hbm(pad),
        compiler_params=pltpu.CompilerParams(vmem_limit_bytes=VMEM_LIMIT),
        scratch_shapes=[pltpu.SemaphoreType.DMA((len(arrays),))],
        input_output_aliases={len(arrays): 0},
        cost_estimate=pl.CostEstimate(flops=0, bytes_accessed=0, transcendentals=0),
    )(*arrays, pad)


def weighted(prob_ref, k, g):
    return (prob_ref[:, k : k + 1].astype(f32) * g.astype(f32)).astype(bf16)


def early_kernel(plane, capacity, groups, wout_ref, hid1_ref, pad_ref, *refs):
    pulled_ref, gout_ref, cols_ref, g, g0, hid0, cols, sem = refs[-8:]
    units, copies = wout_ref.shape[0], Copies(sem)
    copies.start(plate(pad_ref, G0, g0.shape[1]), g0)
    copies.start(plate(pad_ref, HID0, hid0.shape[1]), hid0)
    copies.start(plate(pad_ref, COLS, cols.shape[1]), cols)
    arrange(plane, capacity, groups, refs[:-8], g)
    pulled_ref[...] = dot(g[...], wout_ref[...], 1, 1)
    copies.wait()
    cols_ref[...] = cols[...]
    y = jnp.concatenate([weighted(cols, 0, g0[...]), weighted(cols, 1, g[...])], axis=0)
    hid = jnp.concatenate([hid0[:, :units], hid1_ref[...]], axis=0)
    gout_ref[...] = dot(hid, y, 0, 0).astype(bf16)


def early(plane, capacity, groups, w_out, hid1, pad, *pieces):
    rows, units = hid1.shape
    features = w_out.shape[1]
    width = features // HALVES
    args = (w_out, hid1, *pieces)
    outs = [shaped((rows, units), f32), shaped((units, features), bf16), shaped((rows, 2 * LANES), bf16)]
    whole = lambda a: pl.BlockSpec(a.shape, lambda i: (0, 0))
    first = lambda a: pl.BlockSpec((a.shape[0], width), lambda i: (0, 0))
    return pl.pallas_call(
        functools.partial(early_kernel, plane, capacity, groups),
        grid=(1,),
        out_shape=outs,
        in_specs=[first(w_out), whole(hid1), in_hbm(pad)] + [whole(p) for p in pieces],
        out_specs=[whole(outs[0]), first(outs[1]), whole(outs[2])],
        scratch_shapes=[pltpu.VMEM((rows, n), bf16) for n in (width, width, lanes_of(units), 2 * LANES)]
        + [pltpu.SemaphoreType.DMA((3,))],
        compiler_params=pltpu.CompilerParams(vmem_limit_bytes=VMEM_LIMIT),
        cost_estimate=cost(args, outs, 3 * units * rows * features),
    )(w_out, hid1, pad, *pieces)


def second_kernel(plane, capacity, groups, first, wout_ref, hid_ref, slope_ref, pulled_ref, cols, *refs):
    g_ref, gp_ref, score_ref = refs[-3:]
    units = wout_ref.shape[0]
    arrange(plane, capacity, groups, refs[:-3], g_ref)
    pulled = pulled_ref[...] + dot(g_ref[...], wout_ref[:, first:], 1, 1)
    gp_ref[:, :units] = (cols[:, 1:2].astype(f32) * pulled * slope_ref[...]).astype(bf16)
    score = jnp.sum(hid_ref[...].astype(f32) * pulled, axis=1, keepdims=True)
    lane = lax.broadcasted_iota(jnp.int32, score_ref.shape, 1)
    both = jnp.where(lane == 0, cols[:, LANES:].astype(f32), jnp.where(lane == 1, score, 0.0))
    score_ref[...] = both.astype(bf16)


def late_kernel(width, part, units, _, pad_ref, g1_ref, gp1_ref, *refs):
    gin_ref, gout_ref, cols, x, g, hid, gp, held, sem, out_sem = refs
    rows, features = pad_ref.shape[1:]
    skip = features - part
    copies = Copies(sem)
    top, low = pl.ds(0, rows), pl.ds(rows, rows)
    lanes = lambda at: pl.ds(at, width)
    first = [copies.start(plate(pad_ref, GP0, gp.shape[1]), gp.at[top, :])]
    tiles = []
    for at in range(0, features, width):
        tiles.append(
            [copies.start(pad_ref.at[n, :, lanes(at)], x.at[to, lanes(at)]) for n, to in ((X0, top), (X1, low))]
        )
    then = [copies.start(plate(pad_ref, n, hid.shape[1]), hid.at[at, :]) for n, at in ((HID0, top), (HID1, low))]
    then.append(copies.start(plate(pad_ref, COLS, cols.shape[1]), cols))
    then.append(copies.start(pad_ref.at[G0, :, pl.ds(skip, part)], g))
    sent = []

    def store(n, value, out_ref, at):
        slot = n % held.shape[0]
        if n >= held.shape[0]:
            sent[n - held.shape[0]].wait()
        held[slot] = value.astype(bf16)
        sent.append(pltpu.make_async_copy(held.at[slot], out_ref.at[:, lanes(at)], out_sem.at[slot]))
        sent[-1].start()

    gp[rows:, :] = gp1_ref[...]
    for copy in first:
        copy.wait()
    for n, tile in enumerate(tiles):
        for copy in tile:
            copy.wait()
        at = n * width
        store(n, dot(gp[:, :units], x[:, at : at + width], 0, 0), gin_ref, at)
    for copy in then:
        copy.wait()
    for n in range(part // width):
        at = n * width
        y0 = weighted(cols, 0, g[:, at : at + width])
        y1 = weighted(cols, 1, g1_ref[:, at : at + width])
        store(len(tiles) + n, dot(hid[:, :units], jnp.concatenate([y0, y1], axis=0), 0, 0), gout_ref, skip + at)
    for copy in sent[-held.shape[0] :]:
        copy.wait()


def late(width, done, pad, g1, gp1):
    units, features = done.shape
    rows, part = g1.shape
    outs = [shaped((units, features), bf16)] * 2
    return pl.pallas_call(
        functools.partial(late_kernel, width, part, units),
        out_shape=outs,
        in_specs=[in_hbm(done), in_hbm(pad), pl.BlockSpec(), pl.BlockSpec()],
        out_specs=[in_hbm(o) for o in outs],
        scratch_shapes=[pltpu.VMEM((rows, 2 * LANES), bf16), pltpu.VMEM((2 * rows, features), bf16)]
        + [pltpu.VMEM((rows, part), bf16)]
        + [pltpu.VMEM((2 * rows, lanes_of(units)), bf16)] * 2
        + [pltpu.VMEM((3, units, width), bf16)]
        + [pltpu.SemaphoreType.DMA((7 + 2 * (features // width),)), pltpu.SemaphoreType.DMA((3,))],
        input_output_aliases={0: 1},
        compiler_params=pltpu.CompilerParams(vmem_limit_bytes=LATE_LIMIT),
        cost_estimate=cost((), outs, 6 * units * rows * features),
    )(done, pad, g1, gp1)


def collect_kernel(experts, capacity, topk, meta_ref, hot0_ref, hot1_ref, score_ref, out_ref):
    tokens = meta_ref.shape[2]
    rep = expander(experts * capacity, experts, capacity)
    expert = lax.broadcasted_iota(jnp.int32, (experts, tokens), 0).astype(f32)
    own = meta_ref[lax.axis_index("expert")]
    for k, hot_ref in enumerate((hot0_ref, hot1_ref)):
        placed = hot_ref[...].astype(f32) * score_ref[:, k : k + 1].astype(f32)
        by_expert = dot(rep, placed.astype(bf16), 0, 0)
        for j in range(topk):
            i = k * topk + j
            picked = jnp.where(own[i : i + 1, :] == expert, by_expert, 0.0)
            out_ref[i : i + 1, :] = jnp.sum(picked, axis=0, keepdims=True).astype(bf16)


def body(inputs, entering, weight_in, weight_out, gate_probs, expert_ids):
    experts = lax.axis_size("expert")
    segments = lax.axis_size("segment")
    tokens, features = entering.shape[1:]
    ticks, topk = expert_ids.shape[1], expert_ids.shape[3]
    units = weight_in.shape[2]
    capacity = 3 * tokens * topk // (2 * experts)
    rows = experts * capacity
    plane = Plane(experts)
    matmul = 2 * rows * units * features
    half = features // HALVES
    w_in, w_out = weight_in[0, 0], weight_out[0, 0]
    g0 = entering[0]

    x0 = inputs[0, 0]
    expert_ids, gate_probs = behind((expert_ids, gate_probs), [x0])
    ids = jnp.transpose(expert_ids[0], (0, 2, 1)).reshape(ticks * topk, tokens)
    probs = jnp.transpose(gate_probs[0], (0, 2, 1)).reshape(ticks * topk, tokens)
    meta = jnp.concatenate([ids.astype(f32), probs.astype(f32)], axis=0)
    own_meta = meta
    meta = jnp.broadcast_to(meta[None], (experts,) + meta.shape)
    meta = lax.all_to_all(meta, "expert", split_axis=0, concat_axis=0, tiled=True)
    hot0, hot1, prob = call(
        functools.partial(slots_kernel, experts, capacity, topk),
        [shaped((rows, tokens), bf16)] * 2 + [shaped((rows, LANES), bf16)],
        meta,
    )
    plate_bytes = rows * features * 2
    pad = shaped((max(9, -(-PAD_BYTES // plate_bytes)), rows, features), bf16)

    stepped = capacity % 16 == 0
    ranks = [list(range(k * topk, (k + 1) * topk)) for k in range(ticks)]
    pick = functools.partial(picked_rows, plane, capacity)
    if stepped:
        metas = [own_meta, plane.send(own_meta, (0, 0, 1))]
        x1 = [inputs[0], plane.send(inputs[0], (0, 0, 1))]
        pad, *x1 = own_picked(plane, capacity, gather_plan(plane, ranks[1], 2), 1, metas, x1, pad)
        x1_near, _ = sent_rows(plane, 2, x1[:-HALVES])
        *near_layout, rest_layout = sent_layout(plane, 2)
        x1_groups = [(0, near_layout)] + [(h * half, [rest_layout]) for h in range(HALVES)]
        x1_rest = x1[-HALVES:]
        select_meta = behind(meta, x1)
        x0, x0_layout = sent_rows(plane, 1, pick(ranks[0], 1, x0, select_meta))
        *g0_first, g0_last = pick(ranks[0], 0, g0, select_meta)
        g0_in, g0_layout = sent_rows(plane, 0, [*g0_first, behind(g0_last, [*x1_near, prob])])
        plans = [return_plan(plane, ranks[0], axis) for axis in AXES]
        plans += [gather_plan(plane, ranks[1], axis) for axis in AXES]
        shapes = [shaped((len(b), len(e) * capacity, tokens), bf16) for _, b, e in plans]
        masks = call(functools.partial(masks_kernel, plane, capacity, plans), shapes, meta)
        back_plans = [[[plane.back(plane.back(t, u)) for u in plane.along(axis)] for t in plane.across(axis)] for axis in AXES]
        shapes = [shaped((len(blocks) * capacity, half), bf16) for plan in back_plans for blocks in plan]
    else:
        (pad,) = call(lambda meta_ref, _: None, [pad], meta, pad_out=True)
        x0, x0_layout = [exchange(spread(hot0, x0), experts)], None
        g0_in, g0_layout = [exchange(spread(hot0, g0), experts)], None
        back_plans = [None] * HALVES
        shapes = [shaped((rows, half), bf16)] * HALVES

    if stepped:
        arrived = [*x0, *g0_in]
        x0 = behind(x0, x1_near)
    wide = lanes_of(units)
    vmem = lambda n: pltpu.VMEM((rows, n), bf16)
    x0, hid0, slope0 = call(
        functools.partial(first_preact_kernel, plane, capacity, [(0, x0_layout)]),
        [shaped((rows, features), bf16), shaped((rows, wide), bf16), shaped((rows, units), f32)], w_in, *x0,
    )
    g0_in, gp0, cols, *backs = call(
        functools.partial(first_kernel, plane, capacity, [(0, g0_layout)], back_plans),
        [shaped((rows, n), bf16) for n in (features, wide, 2 * LANES)] + shapes,
        w_in, w_out, hid0, slope0, prob, *g0_in, scratch=[vmem(half)],
    )
    pad = stash(pad, (X0, G0, HID0, GP0, COLS), x0, g0_in, hid0, gp0, cols)
    leaving, after = [], []
    if stepped:
        far = plane.across(2)[-1]
        x1_rest[0] = plane.send(behind(x1_rest[0], [hid0, *arrived]), far)
        after = [pad, x1_rest[0]]
    for h, axis in enumerate(AXES):
        if stepped:
            count = len(plane.across(axis))
            pieces, backs = backs[:count], backs[count:]
            out, parts = returned_rows(plane, capacity, axis, pieces, masks[h], g0, h * half, after)
        else:
            (out,) = call(
                functools.partial(combine_kernel, h * half), [shaped((tokens, half), bf16)],
                hot0, exchange(backs[h], experts), g0, flops=2 * rows * tokens * half,
            )
        leaving.append(out)
        after = [out]

    if stepped:
        x1_rest[1:] = [plane.send(p, far) for p in behind(x1_rest[1:], leaving[:1])]
        x1 = x1_near + x1_rest
    else:
        x1, x1_groups = [exchange(spread(hot1, inputs[0, 1]), experts)], [(0, None)]
    parts, after = [], []
    for h, axis in enumerate(AXES):
        arrived = lax.ppermute(leaving[h], "segment", [(i, i - 1) for i in range(1, segments)])
        arrived = behind(arrived, after)
        if stepped:
            picked = pick(ranks[1], axis, arrived, meta, masks[HALVES + h])
            pieces, layout = sent_rows(plane, axis, picked)
            after = picked
        else:
            pieces, layout = [exchange(spread(hot1, arrived), experts)], None
        parts.append((pieces, [(0, layout)]))
    x1 = behind(x1, after)
    pad, hid1, slope1 = preact(plane, capacity, x1_groups, (X1, HID1), w_in, pad, *x1)
    pulled, gout, cols = early(plane, capacity, parts[0][1], w_out, hid1, pad, *parts[0][0])
    pieces = behind(parts[1][0], [pulled])
    g1, gp1, scores = call(
        functools.partial(second_kernel, plane, capacity, parts[1][1], half),
        [shaped((rows, half), bf16), shaped((rows, wide), bf16), shaped((rows, LANES), bf16)],
        w_out, hid1, slope1, pulled, cols, *pieces, flops=matmul // 2,
    )
    scores = exchange(scores, experts)
    grad_in, grad_out = late(features // TILES, gout, pad, g1, gp1)
    (prob_grads,) = call(
        functools.partial(collect_kernel, experts, capacity, topk),
        [shaped((ticks * topk, tokens), bf16)], meta, hot0, hot1, scores,
    )
    prob_grads = jnp.transpose(prob_grads.reshape(ticks, topk, tokens), (0, 2, 1))
    return grad_in[None, None], grad_out[None, None], prob_grads[None]


def solution(mesh):
    return jax.shard_map(
        body,
        mesh=mesh,
        in_specs=(
            P("segment", None, "expert", None),
            P("segment", "expert", None),
            P("segment", "expert", None, None),
            P("segment", "expert", None, None),
            P("segment", None, "expert", None),
            P("segment", None, "expert", None),
        ),
        out_specs=(
            P("segment", "expert", None, None),
            P("segment", "expert", None, None),
            P("segment", None, "expert", None),
        ),
        check_vma=False,
    )
```
